32 devices in a mesh: inst: 16 (over z, y, x), tp: 2 (over core).
Axes of the slice: x: 2, y: 2, z: 4, core: 2. Of those that a mesh axis runs over, the one named last changes fastest.
Arguments:
- query_one: bfloat16 [256, 16, 128], P('inst', 'tp'), may hold values from -32 to 32
- key_one: bfloat16 [256, 2, 128], P('inst', 'tp'), may hold values from -6 to 6
- value_one: bfloat16 [256, 2, 128], P('inst', 'tp'), may hold values from -6 to 6
- key_pages: bfloat16 [1024, 2, 64, 128], P('inst', 'tp'), may hold values from -32 to 32
- value_pages: bfloat16 [1024, 2, 64, 128], P('inst', 'tp'), may hold values from -6 to 6
- page_table: int32 [256, 4], P('inst'), may hold values from 0 to 63, as said below
- lengths: int32 [256], P('inst'), may hold values from 8 to 254, as said below
- dest_instance: int32 [256], P('inst'), may hold values from 0 to 15, as said below
- dest_slot: int32 [256], P('inst'), may hold values from 0 to 15, as said below
- query_two: bfloat16 [256, 16, 128], P('inst', 'tp'), may hold values from -32 to 32
- key_two: bfloat16 [256, 2, 128], P('inst', 'tp'), may hold values from -6 to 6
- value_two: bfloat16 [256, 2, 128], P('inst', 'tp'), may hold values from -6 to 6
- out_weight: bfloat16 [2048, 4096], P('tp'), may hold values from -0.1875 to 0.1875
Outputs:
- out_one: bfloat16 [256, 4096], P('inst')
- out_two: bfloat16 [256, 4096], P('inst')
- key_cache: bfloat16 [1024, 2, 64, 128], P('inst', 'tp')
- value_cache: bfloat16 [1024, 2, 64, 128], P('inst', 'tp')
The draws below stay inside these ranges and needn't reach their ends.
Inputs may be any that keep to these rules, and one draw needn't show every extreme that they name: `page_table`: the rows of one instance name each of its 64 pages exactly once. `lengths`: some request has exactly 254. `dest_instance`: the 16 requests of one instance go to 16 different instances, and every instance receives exactly 16 requests. `dest_slot`: the requests that reach one instance take its slots once each.
All inputs are finite; a program needn't handle non-finite values.
Results may differ from the reference program's by a relative error of at most 0.022.
Values may be sent and summed in bfloat16 or wider, within the bound.
No kernel may reach another device: no remote copies, remote signals or barrier semaphores. Data moves between devices by JAX's collectives and lax.ppermute only.
A program may use at most 64 MiB of HBM per device.

```python
import jax
import jax.numpy as jnp

HD = 128
QPK = 8
DW = 4096
PAGE = 64
SLOTS = 16
PR = 4
KVH = 2
QH = 16
INSTANCES = 16
REQUESTS = 256
POOL = 64
LMAX = 254


def plan_tables(key):
    key = jax.random.fold_in(key, 7)
    rho = jax.random.permutation(jax.random.fold_in(key, 1), INSTANCES)
    tau = jax.random.permutation(jax.random.fold_in(key, 2), INSTANCES)
    offsets = jax.random.permutation(jax.random.fold_in(key, 3), INSTANCES)[:SLOTS]
    dest = rho[(tau[:, None] + offsets[None, :]) % INSTANCES]
    keys = jax.random.split(jax.random.fold_in(key, 4), INSTANCES)
    orders = jax.vmap(lambda one: jax.random.permutation(one, SLOTS))(keys)
    columns = jnp.arange(SLOTS, dtype=jnp.int32)[None, :]
    slot = orders[dest, columns]
    return (dest.reshape(-1).astype(jnp.int32), slot.reshape(-1).astype(jnp.int32))


def draw_queries(key, salt):
    key = jax.random.fold_in(key, salt)
    shape = (REQUESTS, QH, HD)
    base = jnp.clip(jax.random.normal(key, shape, jnp.float32), -6.0, 6.0)
    return base.astype(jnp.bfloat16)


def draw_query_one(key, part):
    return draw_queries(key, 21)


def draw_query_two(key, part):
    return draw_queries(key, 22)


def draw_key_pages(key, part):
    key = jax.random.fold_in(key, 11)
    shape = (INSTANCES * POOL, KVH, PAGE, HD)
    base = jnp.clip(jax.random.normal(key, shape, jnp.float32), -6.0, 6.0)
    return base.astype(jnp.bfloat16)


def draw_page_table(key, part):
    key = jax.random.fold_in(key, 5)
    keys = jax.random.split(key, INSTANCES)
    table = jax.vmap(lambda one: jax.random.permutation(one, POOL))(keys)
    return table.reshape(REQUESTS, PR).astype(jnp.int32)


def draw_lengths(key, part):
    key = jax.random.fold_in(key, 3)
    heat = jax.random.randint(jax.random.fold_in(key, 1), (INSTANCES, 1), LMAX // 8, LMAX - 7)
    spread = jax.random.randint(jax.random.fold_in(key, 2), (INSTANCES, SLOTS), 0, 1 << 20)
    values = (8 + spread % heat).reshape(-1)
    where_most = jax.random.randint(jax.random.fold_in(key, 4), (), 0, REQUESTS)
    return values.at[where_most].set(LMAX).astype(jnp.int32)


def draw_dest_instance(key, part):
    return plan_tables(key)[0]


def draw_dest_slot(key, part):
    return plan_tables(key)[1]


def level_of(own_key, shape, shards, least, high):
    factor_of = 1.0
    for axis_at, parts in shards:
        steps = jax.random.uniform(jax.random.fold_in(jax.random.fold_in(own_key, 6), axis_at), (parts,), jnp.float32, least / len(shards), high / len(shards))
        factor_of = factor_of * jnp.repeat(jnp.exp(steps), shape[axis_at] // parts).reshape((-1,) + (1,) * (len(shape) - 1 - axis_at))
    return factor_of


def noise(rng, dims, width, reach, pieces=(), kind=jnp.bfloat16):
    drawn = width * jax.random.normal(rng, dims, jnp.float32)
    if pieces:
        drawn = drawn * level_of(rng, dims, pieces, -0.22, 0.18)
    return jnp.clip(drawn, -reach, reach).astype(kind)


def setup_inputs(seed: int = 0) -> dict:
    key_of = jax.random.split(jax.random.key(seed), 14)
    query_one = draw_query_one(jax.random.fold_in(key_of[13], 71), 0)
    key_one = noise(key_of[1], (REQUESTS, KVH, HD), 1.0, 6.0, ((0, 16), (1, 2)))
    value_one = noise(key_of[2], (REQUESTS, KVH, HD), 1.0, 6.0, ((0, 16), (1, 2)))
    key_pages = draw_key_pages(jax.random.fold_in(key_of[13], 71), 0)
    value_pages = noise(key_of[4], (INSTANCES * POOL, KVH, PAGE, HD), 1.0, 6.0, ((0, 16), (1, 2)))
    page_table = draw_page_table(jax.random.fold_in(key_of[13], 71), 0)
    lengths = draw_lengths(jax.random.fold_in(key_of[13], 71), 0)
    dest_instance = draw_dest_instance(jax.random.fold_in(key_of[13], 71), 0)
    dest_slot = draw_dest_slot(jax.random.fold_in(key_of[13], 71), 0)
    query_two = draw_query_two(jax.random.fold_in(key_of[13], 71), 0)
    key_two = noise(key_of[10], (REQUESTS, KVH, HD), 1.0, 6.0, ((0, 16), (1, 2)))
    value_two = noise(key_of[11], (REQUESTS, KVH, HD), 1.0, 6.0, ((0, 16), (1, 2)))
    out_weight = noise(key_of[12], (QH * HD, DW), (QPK * HD) ** -0.5, 0.1875, ((0, 2),))
    return {"query_one": query_one, "key_one": key_one, "value_one": value_one, "key_pages": key_pages, "value_pages": value_pages, "page_table": page_table, "lengths": lengths, "dest_instance": dest_instance, "dest_slot": dest_slot, "query_two": query_two, "key_two": key_two, "value_two": value_two, "out_weight": out_weight}


NEG = -1e30


def put_token(pages, token, position):
    rows = jnp.arange(pages.shape[0], dtype=jnp.int32)
    size = pages.shape[3]
    return pages.at[rows, position // size, :, position % size, :].set(token)


def attend(query, pages_k, pages_v, count):
    rows = query.shape[0]
    grouped = query.astype(jnp.float32).reshape(rows, KVH, QPK, HD)
    scores = jnp.einsum("rkgd,rpktd->rkgpt", grouped, pages_k.astype(jnp.float32))
    scores = scores.reshape(rows, KVH, QPK, PR * PAGE) * (HD ** -0.5)
    live = jnp.arange(PR * PAGE, dtype=jnp.int32)[None, :] < count[:, None]
    live = live[:, None, None, :]
    scores = jnp.where(live, scores, NEG)
    top = jnp.max(scores, axis=-1, keepdims=True)
    expo = jnp.where(live, jnp.exp(scores - top), 0.0)
    weights = (expo / jnp.sum(expo, axis=-1, keepdims=True)).astype(jnp.bfloat16)
    weights = weights.astype(jnp.float32).reshape(rows, KVH, QPK, PR, PAGE)
    mixed = jnp.einsum("rkgpt,rpktd->rkgd", weights, pages_v.astype(jnp.float32))
    return mixed.astype(jnp.bfloat16).reshape(rows, QH * HD)


def reference(query_one, key_one, value_one, key_pages, value_pages, page_table, lengths, dest_instance, dest_slot, query_two, key_two, value_two, out_weight):
    rows = jnp.arange(REQUESTS, dtype=jnp.int32)
    home = rows // SLOTS
    global_pages = (home[:, None] * POOL + page_table).astype(jnp.int32)
    written_k = put_token(key_pages[global_pages], key_one, lengths)
    written_v = put_token(value_pages[global_pages], value_one, lengths)
    first = attend(query_one, written_k, written_v, lengths + 1)
    out_one = jnp.dot(first, out_weight, preferred_element_type=jnp.float32).astype(jnp.bfloat16)
    target = (dest_instance * SLOTS + dest_slot).astype(jnp.int32)
    moved_k = jnp.zeros_like(written_k).at[target].set(written_k)
    moved_v = jnp.zeros_like(written_v).at[target].set(written_v)
    moved_lengths = jnp.zeros_like(lengths).at[target].set(lengths)
    moved_k = put_token(moved_k, key_two, moved_lengths + 1)
    moved_v = put_token(moved_v, value_two, moved_lengths + 1)
    second = attend(query_two, moved_k, moved_v, moved_lengths + 2)
    out_two = jnp.dot(second, out_weight, preferred_element_type=jnp.float32).astype(jnp.bfloat16)
    key_cache = moved_k.reshape(REQUESTS * PR, KVH, PAGE, HD)
    value_cache = moved_v.reshape(REQUESTS * PR, KVH, PAGE, HD)
    return (out_one, out_two, key_cache, value_cache)
```

```python
import functools

import jax
import jax.numpy as jnp
from jax import lax
from jax.experimental import pallas as pl
from jax.experimental.pallas import tpu as pltpu
from jax.sharding import PartitionSpec as P

NEG = -1e30
TAIL = 16
CHUNK = 512
VMEM_BYTES = 32 * 1024 * 1024


def row_of(block, at):
    rows = lax.broadcasted_iota(jnp.int32, block.shape, 0)
    return jnp.sum(jnp.where(rows == at, block, 0.0), axis=0, keepdims=True)


def pack_kernel(n, pages, *refs):
    table, lengths, dest, slot, key_one, value_one, key_pages, value_pages = refs[:8]
    outs = refs[8 : 8 + n]
    source, tails, sems = refs[8 + n :]
    me = lax.axis_index("inst")
    size = key_pages.shape[1]
    span = pages * size

    def note(r, carry):
        source[dest[r]] = r
        return carry

    lax.fori_loop(0, n, note, 0)
    for s in range(n):
        r = source[me ^ s]
        for p in range(pages):
            page = table[r, p]
            pltpu.make_async_copy(
                key_pages.at[page], outs[s].at[pl.ds(p * size, size)], sems.at[s]
            ).start()
            pltpu.make_async_copy(
                value_pages.at[page], outs[s].at[pl.ds(span + p * size, size)], sems.at[s]
            ).start()
    keys = key_one[...].astype(jnp.float32)
    values = value_one[...].astype(jnp.float32)
    at = lax.broadcasted_iota(jnp.int32, (TAIL, keys.shape[1]), 0)
    for s in range(n):
        r = source[me ^ s]
        tail = jnp.where(at == 0, row_of(keys, r), row_of(values, r))
        tail = jnp.where(at == 2, slot[r].astype(jnp.float32), tail)
        tail = jnp.where(at == 3, lengths[r].astype(jnp.float32), tail)
        tails[s] = tail.astype(jnp.bfloat16)
        pltpu.make_async_copy(
            tails.at[s], outs[s].at[pl.ds(2 * span, TAIL)], sems.at[s]
        ).start()
    for s in range(n):
        pltpu.make_async_copy(outs[s], outs[s], sems.at[s]).wait()


def put_row(cache, index, row, position):
    size = cache.shape[2]
    page = position // size
    base = pl.multiple_of((position % size) // TAIL * TAIL, TAIL)
    block = cache[index, page, pl.ds(base, TAIL), :]
    at = lax.broadcasted_iota(jnp.int32, block.shape, 0)
    mixed = jnp.where(at == position % TAIL, row, block.astype(jnp.float32))
    cache[index, page, pl.ds(base, TAIL), :] = mixed.astype(jnp.bfloat16)


def attend(queries, keys, values, counts):
    width = queries[0].shape[1]
    scores = []
    for q, k, count in zip(queries, keys, counts):
        s = lax.dot_general(q, k, (((1,), (1,)), ((), ())), preferred_element_type=jnp.float32)
        live = lax.broadcasted_iota(jnp.int32, s.shape, 1) < count
        scores.append(jnp.where(live, s * width ** (-0.5), NEG))
    group = scores[0].shape[0]
    score = jnp.concatenate(scores, axis=0)
    top = jnp.max(score, axis=-1, keepdims=True)
    expo = jnp.where(score > 0.5 * NEG, jnp.exp(score - top), 0.0)
    weights = (expo / jnp.sum(expo, axis=-1, keepdims=True)).astype(jnp.bfloat16)
    return [
        jnp.dot(weights[i * group : (i + 1) * group], v, preferred_element_type=jnp.float32)
        for i, v in enumerate(values)
    ]


def weight_copies(weight, held, sems):
    width = weight.shape[1] // sems.shape[0]
    return [
        pltpu.make_async_copy(
            weight.at[:, pl.ds(c * width, width)], held.at[:, pl.ds(c * width, width)], sems.at[c]
        )
        for c in range(sems.shape[0])
    ]


def project(mixed, held, out, copies):
    heads = mixed.shape[1]
    rows = jnp.concatenate([mixed[:, h, :] for h in range(heads)], axis=1).astype(jnp.bfloat16)
    width = held.shape[1] // len(copies)
    for c, copy in enumerate(copies):
        copy.wait()
        part = jnp.dot(
            rows, held[:, c * width : (c + 1) * width], preferred_element_type=jnp.float32
        )
        out[:, c * width : (c + 1) * width] = part.astype(jnp.bfloat16)


def first_kernel(slots, pages, *refs):
    table, lengths, query, key_one, value_one, key_pages, value_pages, weight, out = refs[:9]
    keys, values, new_k, new_v, mixed, held, sems, wsems = refs[9:]
    copies = weight_copies(weight, held, wsems)
    for r in range(slots):
        for p in range(pages):
            page = table[r, p]
            pltpu.make_async_copy(key_pages.at[page], keys.at[r, p], sems.at[0, r]).start()
            pltpu.make_async_copy(value_pages.at[page], values.at[r, p], sems.at[1, r]).start()
    for copy in copies:
        copy.start()
    new_k[...] = key_one[...].astype(jnp.float32)
    new_v[...] = value_one[...].astype(jnp.float32)
    for r in range(slots):
        pltpu.make_async_copy(keys.at[r], keys.at[r], sems.at[0, r]).wait()
        pltpu.make_async_copy(values.at[r], values.at[r], sems.at[1, r]).wait()
        put_row(keys, r, new_k[r : r + 1, :], lengths[r])
        put_row(values, r, new_v[r : r + 1, :], lengths[r])
    span = pages * keys.shape[2]
    width = keys.shape[3]
    results = attend(
        [query[r] for r in range(slots)],
        [keys[r].reshape(span, width) for r in range(slots)],
        [values[r].reshape(span, width) for r in range(slots)],
        [lengths[r] + 1 for r in range(slots)],
    )
    for r in range(slots):
        mixed[r] = results[r]
    project(mixed, held, out, copies)


def second_kernel(n, pages, *refs):
    arrived = refs[:n]
    query, key_two, value_two, weight, out, key_cache, value_cache = refs[n : n + 7]
    keys, values, tails, new_k, new_v, mixed, held, sems, osems, wsems = refs[n + 7 :]
    size = keys.shape[2]
    span = pages * size
    width = keys.shape[3]
    copies = weight_copies(weight, held, wsems)
    for s in range(n):
        pltpu.make_async_copy(arrived[s].at[pl.ds(2 * span, TAIL)], tails.at[s], sems.at[2, s]).start()
        for p in range(pages):
            pltpu.make_async_copy(
                arrived[s].at[pl.ds(p * size, size)], keys.at[s, p], sems.at[0, s]
            ).start()
            pltpu.make_async_copy(
                arrived[s].at[pl.ds(span + p * size, size)], values.at[s, p], sems.at[1, s]
            ).start()
    for copy in copies:
        copy.start()
    new_k[...] = key_two[...].astype(jnp.float32)
    new_v[...] = value_two[...].astype(jnp.float32)
    slots = []
    lengths = []
    outgoing = []
    for s in range(n):
        pltpu.make_async_copy(tails.at[s], tails.at[s], sems.at[2, s]).wait()
        tail = tails[s].astype(jnp.float32)
        slots.append(jnp.max(tail[2:3, :]).astype(jnp.int32))
        lengths.append(jnp.max(tail[3:4, :]).astype(jnp.int32))
    for s in range(n):
        tail = tails[s].astype(jnp.float32)
        pltpu.make_async_copy(keys.at[s], keys.at[s], sems.at[0, s]).wait()
        pltpu.make_async_copy(values.at[s], values.at[s], sems.at[1, s]).wait()
        put_row(keys, s, tail[0:1, :], lengths[s])
        put_row(values, s, tail[1:2, :], lengths[s])
        put_row(keys, s, new_k[pl.ds(slots[s], 1), :], lengths[s] + 1)
        put_row(values, s, new_v[pl.ds(slots[s], 1), :], lengths[s] + 1)
        for ref, cache, at in ((keys, key_cache, 0), (values, value_cache, 1)):
            copy = pltpu.make_async_copy(
                ref.at[s], cache.at[pl.ds(slots[s] * pages, pages)], osems.at[at, s]
            )
            copy.start()
            outgoing.append(copy)
    results = attend(
        [query[slots[s]] for s in range(n)],
        [keys[s].reshape(span, width) for s in range(n)],
        [values[s].reshape(span, width) for s in range(n)],
        [lengths[s] + 2 for s in range(n)],
    )
    for s in range(n):
        mixed[slots[s]] = results[s]
    project(mixed, held, out, copies)
    for copy in outgoing:
        copy.wait()


def total(partial, size):
    if size == 2:
        other = lax.ppermute(partial, "tp", [(0, 1), (1, 0)])
        return (partial.astype(jnp.float32) + other.astype(jnp.float32)).astype(jnp.bfloat16)
    return lax.psum(partial, "tp")


def shards(
    n,
    tp,
    query_one,
    key_one,
    value_one,
    key_pages,
    value_pages,
    page_table,
    lengths,
    dest_instance,
    dest_slot,
    query_two,
    key_two,
    value_two,
    out_weight,
):
    slots, pages = page_table.shape
    pool, kv_heads, size, width = key_pages.shape
    heads = query_one.shape[1]
    depth, columns = out_weight.shape
    span = pages * size
    assert kv_heads == 1 and slots == n and n & (n - 1) == 0 and span <= 256
    key_pages = key_pages.reshape(pool, size, width)
    value_pages = value_pages.reshape(pool, size, width)
    key_one = key_one.reshape(slots, width)
    value_one = value_one.reshape(slots, width)
    key_two = key_two.reshape(slots, width)
    value_two = value_two.reshape(slots, width)

    smem = pl.BlockSpec(memory_space=pltpu.SMEM)
    vmem = pl.BlockSpec(memory_space=pltpu.VMEM)
    far = pl.BlockSpec(memory_space=pl.ANY)
    params = pltpu.CompilerParams(vmem_limit_bytes=VMEM_BYTES)
    bf16 = jnp.bfloat16
    parcel = jax.ShapeDtypeStruct((2 * span + TAIL, width), bf16)
    parcel_bytes = (2 * span + TAIL) * width * 2

    packed = pl.pallas_call(
        functools.partial(pack_kernel, n, pages),
        out_shape=[parcel] * n,
        in_specs=[smem] * 4 + [vmem] * 2 + [far] * 2,
        out_specs=[far] * n,
        scratch_shapes=[
            pltpu.SMEM((n,), jnp.int32),
            pltpu.VMEM((n, TAIL, width), bf16),
            pltpu.SemaphoreType.DMA((n,)),
        ],
        compiler_params=params,
        cost_estimate=pl.CostEstimate(flops=0, bytes_accessed=2 * n * parcel_bytes, transcendentals=0),
        name="pack",
    )(page_table, lengths, dest_instance, dest_slot, key_one, value_one, key_pages, value_pages)

    arrived = [packed[0]] + [None] * (n - 1)
    for s in reversed(range(1, n)):
        arrived[s] = lax.ppermute(packed[s], "inst", [(i, i ^ s) for i in range(n)])

    chunks = max(1, columns // CHUNK)
    attend_scratch = [
        pltpu.VMEM((slots, pages, size, width), bf16),
        pltpu.VMEM((slots, pages, size, width), bf16),
    ]
    flops = 4 * slots * heads * span * width + 2 * slots * depth * columns
    moved = 2 * depth * columns + 4 * slots * span * width
    partial_one = pl.pallas_call(
        functools.partial(first_kernel, slots, pages),
        out_shape=jax.ShapeDtypeStruct((slots, columns), bf16),
        in_specs=[smem] * 2 + [vmem] * 3 + [far] * 3,
        out_specs=vmem,
        scratch_shapes=attend_scratch
        + [
            pltpu.VMEM((slots, width), jnp.float32),
            pltpu.VMEM((slots, width), jnp.float32),
            pltpu.VMEM((slots, heads, width), jnp.float32),
            pltpu.VMEM((depth, columns), bf16),
            pltpu.SemaphoreType.DMA((2, slots)),
            pltpu.SemaphoreType.DMA((chunks,)),
        ],
        compiler_params=params,
        cost_estimate=pl.CostEstimate(flops=flops, bytes_accessed=moved, transcendentals=slots * heads * span),
        name="first",
    )(page_table, lengths, query_one, key_one, value_one, key_pages, value_pages, out_weight)
    out_one = total(partial_one, tp)

    cache = jax.ShapeDtypeStruct((slots * pages, size, width), bf16)
    partial_two, key_cache, value_cache = pl.pallas_call(
        functools.partial(second_kernel, n, pages),
        out_shape=[jax.ShapeDtypeStruct((slots, columns), bf16), cache, cache],
        in_specs=[far] * n + [vmem] * 3 + [far],
        out_specs=[vmem, far, far],
        scratch_shapes=attend_scratch
        + [
            pltpu.VMEM((n, TAIL, width), bf16),
            pltpu.VMEM((slots, width), jnp.float32),
            pltpu.VMEM((slots, width), jnp.float32),
            pltpu.VMEM((slots, heads, width), jnp.float32),
            pltpu.VMEM((depth, columns), bf16),
            pltpu.SemaphoreType.DMA((3, n)),
            pltpu.SemaphoreType.DMA((2, n)),
            pltpu.SemaphoreType.DMA((chunks,)),
        ],
        compiler_params=params,
        cost_estimate=pl.CostEstimate(
            flops=flops, bytes_accessed=moved + 4 * slots * span * width, transcendentals=slots * heads * span
        ),
        name="second",
    )(*arrived, query_two, key_two, value_two, out_weight)
    out_two = total(partial_two, tp)
    shape = (slots * pages, kv_heads, size, width)
    return (out_one, out_two, key_cache.reshape(shape), value_cache.reshape(shape))


def solution(mesh):
    sizes = dict(mesh.shape)
    return jax.shard_map(
        functools.partial(shards, sizes["inst"], sizes["tp"]),
        mesh=mesh,
        in_specs=(
            P("inst", "tp", None),
            P("inst", "tp", None),
            P("inst", "tp", None),
            P("inst", "tp", None, None),
            P("inst", "tp", None, None),
            P("inst", None),
            P("inst"),
            P("inst"),
            P("inst"),
            P("inst", "tp", None),
            P("inst", "tp", None),
            P("inst", "tp", None),
            P("tp", None),
        ),
        out_specs=(
            P("inst", None),
            P("inst", None),
            P("inst", "tp", None, None),
            P("inst", "tp", None, None),
        ),
        check_vma=False,
    )
```

```python
import functools

import jax
import jax.numpy as jnp
from jax import lax
from jax.experimental import pallas as pl
from jax.experimental.pallas import tpu as pltpu
from jax.sharding import PartitionSpec as P

NEG = -1e30
TAIL = 16
GROUPS = 4
CHUNKS = 8
VMEM_BYTES = 24 * 1024 * 1024


def row_of(block, at):
    rows = lax.broadcasted_iota(jnp.int32, block.shape, 0)
    return jnp.sum(jnp.where(rows == at, block, 0.0), axis=0, keepdims=True)


def put_row(parcels, index, offset, row, position):
    base = pl.multiple_of(offset + position // TAIL * TAIL, TAIL)
    block = parcels[index, pl.ds(base, TAIL), :]
    at = lax.broadcasted_iota(jnp.int32, block.shape, 0)
    mixed = jnp.where(at == position % TAIL, row, block.astype(jnp.float32))
    parcels[index, pl.ds(base, TAIL), :] = mixed.astype(jnp.bfloat16)


def invert(dest, source, n):
    def note(r, carry):
        source[dest[r]] = r
        return carry

    lax.fori_loop(0, n, note, 0)


def begin(pairs, sem):
    copies = [pltpu.make_async_copy(a, b, sem.at[i]) for i, (a, b) in enumerate(pairs)]
    for copy in copies:
        copy.start()
    return copies


def finish(copies):
    for copy in copies:
        copy.wait()


def pack_kernel(n, pages, *refs):
    far, out = refs[:8], refs[8]
    table, lengths, dest, slot, key_one, value_one, key_pool, value_pool = refs[9:17]
    source, parcels, sems, osems = refs[17:]
    copies = begin(list(zip(far, (table, lengths, dest, slot, key_one, value_one, key_pool, value_pool))), sems)
    size = key_pool.shape[1]
    span = pages * size
    finish(copies[:6])
    invert(dest, source, n)
    keys = key_one[...].astype(jnp.float32)
    values = value_one[...].astype(jnp.float32)
    at = lax.broadcasted_iota(jnp.int32, (TAIL, keys.shape[1]), 0)
    copies[6].wait()
    for d in range(n):
        r = source[d]
        for p in range(pages):
            parcels[d, p * size : (p + 1) * size, :] = key_pool[table[p, r]]
    for d in range(n):
        r = source[d]
        put_row(parcels, d, 0, row_of(keys, r), lengths[r])
        tail = jnp.where(at == 0, slot[r].astype(jnp.float32), lengths[r].astype(jnp.float32))
        parcels[d, 2 * span : 2 * span + TAIL, :] = tail.astype(jnp.bfloat16)
    copies[7].wait()
    outgoing = []
    for d in range(n):
        r = source[d]
        for p in range(pages):
            parcels[d, span + p * size : span + (p + 1) * size, :] = value_pool[table[p, r]]
        put_row(parcels, d, span, row_of(values, r), lengths[r])
        copy = pltpu.make_async_copy(parcels.at[d], out.at[d], osems.at[d])
        copy.start()
        outgoing.append(copy)
    finish(outgoing)


def attend(queries, keys, values, counts):
    width = queries[0].shape[1]
    scores = []
    for q, k, count in zip(queries, keys, counts):
        s = lax.dot_general(q, k, (((1,), (1,)), ((), ())), preferred_element_type=jnp.float32)
        live = lax.broadcasted_iota(jnp.int32, s.shape, 1) < count
        scores.append(jnp.where(live, s * width ** (-0.5), NEG))
    group = scores[0].shape[0]
    score = jnp.concatenate(scores, axis=0)
    top = jnp.max(score, axis=-1, keepdims=True)
    expo = jnp.exp(score - top)
    weights = (expo / jnp.sum(expo, axis=-1, keepdims=True)).astype(jnp.bfloat16)
    return [
        jnp.dot(weights[i * group : (i + 1) * group], v, preferred_element_type=jnp.float32)
        for i, v in enumerate(values)
    ]


def project(mixed, weight, out):
    heads = mixed.shape[1]
    rows = jnp.concatenate([mixed[:, h, :] for h in range(heads)], axis=1).astype(jnp.bfloat16)
    width = weight.shape[1] // CHUNKS
    for c in range(CHUNKS):
        part = jnp.dot(
            rows, weight[:, c * width : (c + 1) * width], preferred_element_type=jnp.float32
        )
        out[:, c * width : (c + 1) * width] = part.astype(jnp.bfloat16)


def load_groups(source, parcels, sems):
    step = source.shape[0] // GROUPS
    return begin(
        [(source.at[pl.ds(g * step, step)], parcels.at[pl.ds(g * step, step)]) for g in range(GROUPS)],
        sems,
    )


def first_kernel(n, span, *refs):
    far, weight, out = refs[:4], refs[4], refs[5]
    lengths, dest, query, parcels, source, mixed, sems, psems = refs[6:]
    copies = begin(list(zip(far[:3], (lengths, dest, query))), sems)
    loads = load_groups(far[3], parcels, psems)
    finish(copies)
    invert(dest, source, n)
    finish(loads)
    at = [source[d] for d in range(n)]
    results = attend(
        [query[r] for r in at],
        [parcels[d, :span, :] for d in range(n)],
        [parcels[d, span : 2 * span, :] for d in range(n)],
        [lengths[r] + 1 for r in at],
    )
    for r, result in zip(at, results):
        mixed[r] = result
    project(mixed, weight, out)


def second_kernel(n, pages, *refs):
    far, weight, out, key_cache, value_cache = refs[:4], refs[4], refs[5], refs[6], refs[7]
    query, key_two, value_two, parcels, new_k, new_v, mixed, sems, psems, osems = refs[8:]
    span = (parcels.shape[1] - TAIL) // 2
    loads = load_groups(far[0], parcels, psems)
    copies = begin(list(zip(far[1:], (query, key_two, value_two))), sems)
    finish(copies)
    new_k[...] = key_two[...].astype(jnp.float32)
    new_v[...] = value_two[...].astype(jnp.float32)
    finish(loads)
    slots = []
    lengths = []
    for s in range(n):
        tail = parcels[s, 2 * span : 2 * span + TAIL, :].astype(jnp.float32)
        slots.append(jnp.max(tail[0:1, :]).astype(jnp.int32))
        lengths.append(jnp.max(tail[1:2, :]).astype(jnp.int32))
    outgoing = []
    for s in range(n):
        put_row(parcels, s, 0, new_k[pl.ds(slots[s], 1), :], lengths[s] + 1)
        put_row(parcels, s, span, new_v[pl.ds(slots[s], 1), :], lengths[s] + 1)
        for cache, at in ((key_cache, 0), (value_cache, 1)):
            copy = pltpu.make_async_copy(
                parcels.at[s, pl.ds(at * span, span)], cache.at[slots[s]], osems.at[at, s]
            )
            copy.start()
            outgoing.append(copy)
    results = attend(
        [query[slots[s]] for s in range(n)],
        [parcels[s, :span, :] for s in range(n)],
        [parcels[s, span : 2 * span, :] for s in range(n)],
        [lengths[s] + 2 for s in range(n)],
    )
    for s in range(n):
        mixed[slots[s]] = results[s]
    project(mixed, weight, out)
    finish(outgoing)


def total(partial, size):
    if size == 2:
        other = lax.ppermute(partial, "tp", [(0, 1), (1, 0)])
        return (partial.astype(jnp.float32) + other.astype(jnp.float32)).astype(jnp.bfloat16)
    return lax.psum(partial, "tp")


def hbm(x):
    return pltpu.with_memory_space_constraint(x, pltpu.HBM)


def shards(
    n,
    tp,
    query_one,
    key_one,
    value_one,
    key_pages,
    value_pages,
    page_table,
    lengths,
    dest_instance,
    dest_slot,
    query_two,
    key_two,
    value_two,
    out_weight,
):
    slots, pages = page_table.shape
    pool, kv_heads, size, width = key_pages.shape
    heads = query_one.shape[1]
    depth, columns = out_weight.shape
    span = pages * size
    assert kv_heads == 1 and slots == n and span <= 256
    key_pages = key_pages.reshape(pool, size, width)
    value_pages = value_pages.reshape(pool, size, width)
    key_one = key_one.reshape(slots, width)
    value_one = value_one.reshape(slots, width)
    key_two = key_two.reshape(slots, width)
    value_two = value_two.reshape(slots, width)

    vmem = pl.BlockSpec(memory_space=pltpu.VMEM)
    far = pl.BlockSpec(memory_space=pltpu.HBM)
    params = pltpu.CompilerParams(vmem_limit_bytes=VMEM_BYTES)
    bf16, f32, i32 = jnp.bfloat16, jnp.float32, jnp.int32
    rows = 2 * span + TAIL
    parcels = pltpu.VMEM((n, rows, width), bf16)

    packed = pl.pallas_call(
        functools.partial(pack_kernel, n, pages),
        out_shape=jax.ShapeDtypeStruct((n, rows, width), bf16),
        in_specs=[far] * 8,
        out_specs=far,
        scratch_shapes=[
            pltpu.SMEM((pages, slots), i32),
            pltpu.SMEM((slots,), i32),
            pltpu.SMEM((slots,), i32),
            pltpu.SMEM((slots,), i32),
            pltpu.VMEM((slots, width), bf16),
            pltpu.VMEM((slots, width), bf16),
            pltpu.VMEM((pool, size, width), bf16),
            pltpu.VMEM((pool, size, width), bf16),
            pltpu.SMEM((n,), i32),
            parcels,
            pltpu.SemaphoreType.DMA((8,)),
            pltpu.SemaphoreType.DMA((n,)),
        ],
        compiler_params=params,
        cost_estimate=pl.CostEstimate(flops=0, bytes_accessed=4 * n * rows * width, transcendentals=0),
        name="pack",
    )(
        hbm(page_table.T),
        hbm(lengths),
        hbm(dest_instance),
        hbm(dest_slot),
        hbm(key_one),
        hbm(value_one),
        hbm(key_pages),
        hbm(value_pages),
    )

    arrived = lax.all_to_all(packed, "inst", split_axis=0, concat_axis=0, tiled=True)

    weight = pltpu.with_memory_space_constraint(out_weight, pltpu.VMEM)
    flops = 4 * slots * heads * span * width + 2 * slots * depth * columns
    moved = 2 * depth * columns + 4 * slots * span * width
    partial_one = pl.pallas_call(
        functools.partial(first_kernel, n, span),
        out_shape=jax.ShapeDtypeStruct((slots, columns), bf16),
        in_specs=[far] * 4 + [vmem],
        out_specs=vmem,
        scratch_shapes=[
            pltpu.SMEM((slots,), i32),
            pltpu.SMEM((slots,), i32),
            pltpu.VMEM((slots, heads, width), bf16),
            parcels,
            pltpu.SMEM((n,), i32),
            pltpu.VMEM((slots, heads, width), f32),
            pltpu.SemaphoreType.DMA((3,)),
            pltpu.SemaphoreType.DMA((GROUPS,)),
        ],
        compiler_params=params,
        cost_estimate=pl.CostEstimate(flops=flops, bytes_accessed=moved, transcendentals=slots * heads * span),
        name="first",
    )(hbm(lengths), hbm(dest_instance), hbm(query_one), hbm(packed), weight)
    out_one = total(partial_one, tp)

    cache = jax.ShapeDtypeStruct((slots, span, width), bf16)
    partial_two, key_cache, value_cache = pl.pallas_call(
        functools.partial(second_kernel, n, pages),
        out_shape=[jax.ShapeDtypeStruct((slots, columns), bf16), cache, cache],
        in_specs=[far] * 4 + [vmem],
        out_specs=[vmem, far, far],
        scratch_shapes=[
            pltpu.VMEM((slots, heads, width), bf16),
            pltpu.VMEM((slots, width), bf16),
            pltpu.VMEM((slots, width), bf16),
            parcels,
            pltpu.VMEM((slots, width), f32),
            pltpu.VMEM((slots, width), f32),
            pltpu.VMEM((slots, heads, width), f32),
            pltpu.SemaphoreType.DMA((3,)),
            pltpu.SemaphoreType.DMA((GROUPS,)),
            pltpu.SemaphoreType.DMA((2, n)),
        ],
        compiler_params=params,
        cost_estimate=pl.CostEstimate(
            flops=flops, bytes_accessed=moved + 4 * slots * span * width, transcendentals=slots * heads * span
        ),
        name="second",
    )(hbm(arrived), hbm(query_two), hbm(key_two), hbm(value_two), weight)
    out_two = total(partial_two, tp)
    shape = (slots * pages, kv_heads, size, width)
    return (out_one, out_two, key_cache.reshape(shape), value_cache.reshape(shape))


def solution(mesh):
    sizes = dict(mesh.shape)
    return jax.shard_map(
        functools.partial(shards, sizes["inst"], sizes["tp"]),
        mesh=mesh,
        in_specs=(
            P("inst", "tp", None),
            P("inst", "tp", None),
            P("inst", "tp", None),
            P("inst", "tp", None, None),
            P("inst", "tp", None, None),
            P("inst", None),
            P("inst"),
            P("inst"),
            P("inst"),
            P("inst", "tp", None),
            P("inst", "tp", None),
            P("inst", "tp", None),
            P("tp", None),
        ),
        out_specs=(
            P("inst", None),
            P("inst", None),
            P("inst", "tp", None, None),
            P("inst", "tp", None, None),
        ),
        check_vma=False,
    )
```

```python
import functools

import jax
import jax.numpy as jnp
from jax import lax
from jax.experimental import pallas as pl
from jax.experimental.pallas import tpu as pltpu
from jax.sharding import PartitionSpec as P

NEG = -1e30
TAIL = 16
CHUNKS = 8
AHEAD = 6
LATE = 4
VMEM_BYTES = 24 * 1024 * 1024


def row_of(block, at):
    rows = lax.broadcasted_iota(jnp.int32, block.shape, 0)
    return jnp.sum(jnp.where(rows == at, block, 0.0), axis=0, keepdims=True)


def put_row(parcel, offset, row, position):
    base = pl.multiple_of(offset + position // TAIL * TAIL, TAIL)
    block = parcel[pl.ds(base, TAIL), :]
    at = lax.broadcasted_iota(jnp.int32, block.shape, 0)
    mixed = jnp.where(at == position % TAIL, row, block.astype(jnp.float32))
    parcel[pl.ds(base, TAIL), :] = mixed.astype(jnp.bfloat16)


def invert(dest, source, n):
    def note(r, carry):
        source[dest[r]] = r
        return carry

    lax.fori_loop(0, n, note, 0)


def begin(pairs, sem):
    copies = [pltpu.make_async_copy(a, b, sem.at[i]) for i, (a, b) in enumerate(pairs)]
    for copy in copies:
        copy.start()
    return copies


def finish(copies):
    for copy in copies:
        copy.wait()


def pack_kernel(n, pages, *refs):
    far, outs = refs[:8], refs[8 : 8 + n]
    table, lengths, dest, slot, key_one, value_one, key_pool, value_pool, source, sems = refs[8 + n :]
    copies = begin(list(zip(far, (table, lengths, dest, slot, key_one, value_one, key_pool, value_pool))), sems)
    me = lax.axis_index("inst")
    size = key_pool.shape[1]
    span = pages * size
    finish(copies[:6])
    invert(dest, source, n)
    keys = key_one[...].astype(jnp.float32)
    values = value_one[...].astype(jnp.float32)
    at = lax.broadcasted_iota(jnp.int32, (TAIL, keys.shape[1]), 0)
    for pool, token, offset, copy in ((key_pool, keys, 0, copies[6]), (value_pool, values, span, copies[7])):
        copy.wait()
        for s in range(n):
            r = source[me ^ s]
            for p in range(pages):
                outs[s][offset + p * size : offset + (p + 1) * size, :] = pool[table[p, r]]
            put_row(outs[s], offset, row_of(token, r), lengths[r])
    for s in range(n):
        r = source[me ^ s]
        tail = jnp.where(at == 0, slot[r].astype(jnp.float32), lengths[r].astype(jnp.float32))
        outs[s][2 * span : 2 * span + TAIL, :] = tail.astype(jnp.bfloat16)


def attend(queries, keys, values, counts):
    width = queries[0].shape[1]
    scores = []
    for q, k, count in zip(queries, keys, counts):
        s = lax.dot_general(q, k, (((1,), (1,)), ((), ())), preferred_element_type=jnp.float32)
        live = lax.broadcasted_iota(jnp.int32, s.shape, 1) < count
        scores.append(jnp.where(live, s * width ** (-0.5), NEG))
    group = scores[0].shape[0]
    score = jnp.concatenate(scores, axis=0)
    top = jnp.max(score, axis=-1, keepdims=True)
    expo = jnp.exp(score - top)
    weights = (expo / jnp.sum(expo, axis=-1, keepdims=True)).astype(jnp.bfloat16)
    return [
        jnp.dot(weights[i * group : (i + 1) * group], v, preferred_element_type=jnp.float32)
        for i, v in enumerate(values)
    ]


def project(mixed, weight, out):
    heads = mixed.shape[1]
    rows = jnp.concatenate([mixed[:, h, :] for h in range(heads)], axis=1).astype(jnp.bfloat16)
    width = weight.shape[1] // CHUNKS
    for c in range(CHUNKS):
        part = jnp.dot(
            rows, weight[:, c * width : (c + 1) * width], preferred_element_type=jnp.float32
        )
        out[:, c * width : (c + 1) * width] = part.astype(jnp.bfloat16)


def first_kernel(n, *refs):
    far, parcels, out, weight = refs[:4], refs[4 : 4 + n], refs[4 + n], refs[5 + n]
    lengths, dest, query, source, mixed, sems = refs[6 + n :]
    copies = begin(list(zip(far, (lengths, dest, query, weight))), sems)
    me = lax.axis_index("inst")
    span = (parcels[0].shape[0] - TAIL) // 2
    finish(copies[:3])
    invert(dest, source, n)
    at = [source[me ^ s] for s in range(n)]
    results = attend(
        [query[r] for r in at],
        [parcel[:span, :] for parcel in parcels],
        [parcel[span : 2 * span, :] for parcel in parcels],
        [lengths[r] + 1 for r in at],
    )
    for r, result in zip(at, results):
        mixed[r] = result
    copies[3].wait()
    project(mixed, weight, out)


def place(arrived, query, key_two, value_two, key_cache, value_cache, parcels, mixed, osems):
    span = (arrived[0].shape[0] - TAIL) // 2
    count = len(arrived)
    slots = []
    lengths = []
    for parcel in arrived:
        tail = parcel[2 * span : 2 * span + TAIL, :].astype(jnp.float32)
        slots.append(jnp.max(tail[0:1, :]).astype(jnp.int32))
        lengths.append(jnp.max(tail[1:2, :]).astype(jnp.int32))
    for i, parcel in enumerate(arrived):
        parcels[i] = parcel[: 2 * span, :]
    outgoing = []
    for i in range(count):
        held = parcels.at[i]
        put_row(held, 0, key_two[pl.ds(slots[i], 1), :], lengths[i] + 1)
        put_row(held, span, value_two[pl.ds(slots[i], 1), :], lengths[i] + 1)
        for cache, at in ((key_cache, 0), (value_cache, 1)):
            copy = pltpu.make_async_copy(
                held.at[pl.ds(at * span, span)], cache.at[slots[i]], osems.at[at, i]
            )
            copy.start()
            outgoing.append(copy)
    results = attend(
        [query[j] for j in slots],
        [parcels[i, :span, :] for i in range(count)],
        [parcels[i, span : 2 * span, :] for i in range(count)],
        [length + 2 for length in lengths],
    )
    for j, result in zip(slots, results):
        mixed[j] = result
    return outgoing


def early_kernel(count, pair, *refs):
    arrived, far, halves = refs[:count], refs[count : count + 3], refs[count + 3 : count + 3 + pair]
    key_cache, value_cache, mixed = refs[count + 3 + pair : count + 6 + pair]
    query, key_two, value_two, new_k, new_v, parcels, sems, osems = refs[-8:]
    copies = begin(list(zip(far, (query, key_two, value_two))), sems)
    if pair:
        out = refs[count + 6 + pair]
        both = halves[0][...].astype(jnp.float32) + halves[1][...].astype(jnp.float32)
        out[...] = both.astype(jnp.bfloat16)
    finish(copies)
    new_k[...] = key_two[...].astype(jnp.float32)
    new_v[...] = value_two[...].astype(jnp.float32)
    finish(place(arrived, query, new_k, new_v, key_cache, value_cache, parcels, mixed, osems))


def late_kernel(count, *refs):
    arrived, far, weight, before = refs[:count], refs[count : count + 3], refs[count + 3], refs[count + 4]
    out, key_cache, value_cache = refs[count + 7 : count + 10]
    query, key_two, value_two, new_k, new_v, parcels, mixed, sems, osems = refs[-9:]
    copies = begin(list(zip(far, (query, key_two, value_two))), sems)
    mixed[...] = before[...]
    finish(copies)
    new_k[...] = key_two[...].astype(jnp.float32)
    new_v[...] = value_two[...].astype(jnp.float32)
    outgoing = place(arrived, query, new_k, new_v, key_cache, value_cache, parcels, mixed, osems)
    project(mixed, weight, out)
    finish(outgoing)


def swap(partial):
    return lax.ppermute(partial, "tp", [(0, 1), (1, 0)])


def near(x):
    return pltpu.with_memory_space_constraint(x, pltpu.VMEM)


def hbm(x):
    return pltpu.with_memory_space_constraint(x, pltpu.HBM)


def step_order(n):
    far = list(range(n // 2, n))
    close = list(range(1, n // 2))
    return [s for pair in zip(far, close) for s in pair] + far[len(close) :]


def shards(
    n,
    tp,
    query_one,
    key_one,
    value_one,
    key_pages,
    value_pages,
    page_table,
    lengths,
    dest_instance,
    dest_slot,
    query_two,
    key_two,
    value_two,
    out_weight,
):
    slots, pages = page_table.shape
    pool, kv_heads, size, width = key_pages.shape
    heads = query_one.shape[1]
    depth, columns = out_weight.shape
    span = pages * size
    assert kv_heads == 1 and slots == n and span <= 256
    key_pages = key_pages.reshape(pool, size, width)
    value_pages = value_pages.reshape(pool, size, width)
    key_one = key_one.reshape(slots, width)
    value_one = value_one.reshape(slots, width)
    key_two = key_two.reshape(slots, width)
    value_two = value_two.reshape(slots, width)

    vmem = pl.BlockSpec(memory_space=pltpu.VMEM)
    far = pl.BlockSpec(memory_space=pltpu.HBM)
    params = pltpu.CompilerParams(vmem_limit_bytes=VMEM_BYTES)
    bf16, f32, i32 = jnp.bfloat16, jnp.float32, jnp.int32
    rows = 2 * span + TAIL
    parcel = jax.ShapeDtypeStruct((rows, width), bf16)

    packed = pl.pallas_call(
        functools.partial(pack_kernel, n, pages),
        out_shape=[parcel] * n,
        in_specs=[far] * 8,
        out_specs=[vmem] * n,
        scratch_shapes=[
            pltpu.SMEM((pages, slots), i32),
            pltpu.SMEM((slots,), i32),
            pltpu.SMEM((slots,), i32),
            pltpu.SMEM((slots,), i32),
            pltpu.VMEM((slots, width), bf16),
            pltpu.VMEM((slots, width), bf16),
            pltpu.VMEM((pool, size, width), bf16),
            pltpu.VMEM((pool, size, width), bf16),
            pltpu.SMEM((n,), i32),
            pltpu.SemaphoreType.DMA((8,)),
        ],
        compiler_params=params,
        cost_estimate=pl.CostEstimate(flops=0, bytes_accessed=4 * n * rows * width, transcendentals=0),
        name="pack",
    )(
        hbm(page_table.T),
        hbm(lengths),
        hbm(dest_instance),
        hbm(dest_slot),
        hbm(key_one),
        hbm(value_one),
        hbm(key_pages),
        hbm(value_pages),
    )

    flops = 4 * slots * heads * span * width + 2 * slots * depth * columns
    moved = 2 * depth * columns + 4 * slots * span * width
    order = step_order(n)
    late = order[-LATE:]
    arrived = {0: packed[0]}

    def send(s, block):
        arrived[s] = lax.ppermute(block, "inst", [(i, i ^ s) for i in range(n)])

    for s in order[:AHEAD]:
        send(s, packed[s])
    query_late = lax.optimization_barrier((query_one, arrived[order[0]]))[0]
    partial_one, weight = pl.pallas_call(
        functools.partial(first_kernel, n),
        out_shape=[
            jax.ShapeDtypeStruct((slots, columns), bf16),
            jax.ShapeDtypeStruct((depth, columns), bf16),
        ],
        in_specs=[far] * 4 + [vmem] * n,
        out_specs=[vmem, vmem],
        scratch_shapes=[
            pltpu.SMEM((slots,), i32),
            pltpu.SMEM((slots,), i32),
            pltpu.VMEM((slots, heads, width), bf16),
            pltpu.SMEM((n,), i32),
            pltpu.VMEM((slots, heads, width), f32),
            pltpu.SemaphoreType.DMA((4,)),
        ],
        compiler_params=params,
        cost_estimate=pl.CostEstimate(flops=flops, bytes_accessed=moved, transcendentals=slots * heads * span),
        name="first",
    )(hbm(lengths), hbm(dest_instance), hbm(query_late), hbm(out_weight), *packed)

    for s in order[AHEAD:]:
        send(s, lax.optimization_barrier((packed[s], partial_one))[0])
    early = [0] + order[:-LATE]

    halves = [partial_one, swap(partial_one)] if tp == 2 else []
    cache = jax.ShapeDtypeStruct((slots, span, width), bf16)
    common = [
        pltpu.VMEM((slots, heads, width), bf16),
        pltpu.VMEM((slots, width), bf16),
        pltpu.VMEM((slots, width), bf16),
        pltpu.VMEM((slots, width), f32),
        pltpu.VMEM((slots, width), f32),
    ]
    mixed = jax.ShapeDtypeStruct((slots, heads, width), f32)
    some = len(early)
    results = pl.pallas_call(
        functools.partial(early_kernel, some, len(halves)),
        out_shape=[cache, cache, mixed] + [jax.ShapeDtypeStruct((slots, columns), bf16)] * (len(halves) // 2),
        in_specs=[vmem] * some + [far] * 3 + [vmem] * len(halves),
        out_specs=[far, far, vmem] + [vmem] * (len(halves) // 2),
        scratch_shapes=common
        + [
            pltpu.VMEM((some, 2 * span, width), bf16),
            pltpu.SemaphoreType.DMA((3,)),
            pltpu.SemaphoreType.DMA((2, some)),
        ],
        compiler_params=params,
        cost_estimate=pl.CostEstimate(
            flops=4 * some * heads * span * width,
            bytes_accessed=8 * some * span * width,
            transcendentals=some * heads * span,
        ),
        name="early",
    )(*[arrived[s] for s in early], hbm(query_two), hbm(key_two), hbm(value_two), *halves)
    key_cache, value_cache, mixed = results[:3]
    out_one = results[3] if halves else lax.psum(partial_one, "tp")

    partial_two, key_cache, value_cache = pl.pallas_call(
        functools.partial(late_kernel, LATE),
        out_shape=[jax.ShapeDtypeStruct((slots, columns), bf16), cache, cache],
        in_specs=[vmem] * LATE + [far] * 3 + [vmem] * 2 + [far] * 2,
        out_specs=[vmem, far, far],
        input_output_aliases={LATE + 5: 1, LATE + 6: 2},
        scratch_shapes=common
        + [
            pltpu.VMEM((LATE, 2 * span, width), bf16),
            pltpu.VMEM((slots, heads, width), f32),
            pltpu.SemaphoreType.DMA((3,)),
            pltpu.SemaphoreType.DMA((2, LATE)),
        ],
        compiler_params=params,
        cost_estimate=pl.CostEstimate(flops=flops, bytes_accessed=moved, transcendentals=LATE * heads * span),
        name="late",
    )(
        *[arrived[s] for s in late],
        hbm(query_two),
        hbm(key_two),
        hbm(value_two),
        near(weight),
        mixed,
        hbm(key_cache),
        hbm(value_cache),
    )
    if tp == 2:
        both = partial_two.astype(f32) + swap(partial_two).astype(f32)
        out_two = both.astype(bf16)
    else:
        out_two = lax.psum(partial_two, "tp")
    shape = (slots * pages, kv_heads, size, width)
    return (out_one, out_two, key_cache.reshape(shape), value_cache.reshape(shape))


def solution(mesh):
    sizes = dict(mesh.shape)
    return jax.shard_map(
        functools.partial(shards, sizes["inst"], sizes["tp"]),
        mesh=mesh,
        in_specs=(
            P("inst", "tp", None),
            P("inst", "tp", None),
            P("inst", "tp", None),
            P("inst", "tp", None, None),
            P("inst", "tp", None, None),
            P("inst", None),
            P("inst"),
            P("inst"),
            P("inst"),
            P("inst", "tp", None),
            P("inst", "tp", None),
            P("inst", "tp", None),
            P("tp", None),
        ),
        out_specs=(
            P("inst", None),
            P("inst", None),
            P("inst", "tp", None, None),
            P("inst", "tp", None, None),
        ),
        check_vma=False,
    )
```

```python
import functools

import jax
import jax.numpy as jnp
from jax import lax
from jax.experimental import pallas as pl
from jax.experimental.pallas import tpu as pltpu
from jax.sharding import PartitionSpec as P

NEG = -1e30
TAIL = 16
CHUNKS = 8
AHEAD = 5
LATE = 3
VMEM_BYTES = 24 * 1024 * 1024


def row_of(block, at):
    rows = lax.broadcasted_iota(jnp.int32, block.shape, 0)
    return jnp.sum(jnp.where(rows == at, block, 0.0), axis=0, keepdims=True)


def put_row(block, row, position):
    base = pl.multiple_of(position // TAIL * TAIL, TAIL)
    part = block[pl.ds(base, TAIL), :]
    at = lax.broadcasted_iota(jnp.int32, part.shape, 0)
    mixed = jnp.where(at == position % TAIL, row, part.astype(jnp.float32))
    block[pl.ds(base, TAIL), :] = mixed.astype(jnp.bfloat16)


def invert(dest, source, n):
    def note(r, carry):
        source[dest[r]] = r
        return carry

    lax.fori_loop(0, n, note, 0)


def begin(pairs, sem):
    copies = [pltpu.make_async_copy(a, b, sem.at[i]) for i, (a, b) in enumerate(pairs)]
    for copy in copies:
        copy.start()
    return copies


def finish(copies):
    for copy in copies:
        copy.wait()


def views(ref, span):
    return ref.at[pl.ds(0, span)], ref.at[pl.ds(span, span)], ref.at[pl.ds(2 * span, TAIL)]


def parcels_of(refs, half, span):
    home, keys, rest, others = refs[0], refs[1], refs[2], refs[3:]
    near = [views(home.at[d], span) for d in range(half)]
    split = (keys, rest.at[pl.ds(0, span)], rest.at[pl.ds(span, TAIL)])
    return near + [split] + [views(ref, span) for ref in others]


def sources(source, half):
    me = lax.axis_index("inst")
    base = me // half * half
    return [source[base + d] for d in range(half)] + [source[me ^ s] for s in range(half, 2 * half)]


def pack_kernel(half, pages, *refs):
    far, outs = refs[:8], refs[8 : 10 + half]
    table, lengths, dest, slot, key_one, value_one, key_pool, value_pool, source, sems = refs[10 + half :]
    copies = begin(list(zip(far, (table, lengths, dest, slot, key_one, value_one, key_pool, value_pool))), sems)
    size = key_pool.shape[1]
    parcels = parcels_of(outs, half, pages * size)
    finish(copies[:6])
    invert(dest, source, 2 * half)
    at = sources(source, half)
    tokens = (key_one[...].astype(jnp.float32), value_one[...].astype(jnp.float32))
    for which, pool in ((0, key_pool), (1, value_pool)):
        copies[6 + which].wait()
        for r, parcel in zip(at, parcels):
            for p in range(pages):
                parcel[which][p * size : (p + 1) * size, :] = pool[table[p, r]]
            put_row(parcel[which], row_of(tokens[which], r), lengths[r])
    rows = lax.broadcasted_iota(jnp.int32, (TAIL, key_one.shape[1]), 0)
    for r, parcel in zip(at, parcels):
        tail = jnp.where(rows == 0, slot[r].astype(jnp.float32), lengths[r].astype(jnp.float32))
        parcel[2][...] = tail.astype(jnp.bfloat16)


def attend(queries, keys, values, counts):
    width = queries[0].shape[1]
    scores = []
    for q, k, count in zip(queries, keys, counts):
        s = lax.dot_general(q, k, (((1,), (1,)), ((), ())), preferred_element_type=jnp.float32)
        live = lax.broadcasted_iota(jnp.int32, s.shape, 1) < count
        scores.append(jnp.where(live, s * width ** (-0.5), NEG))
    group = scores[0].shape[0]
    score = jnp.concatenate(scores, axis=0)
    top = jnp.max(score, axis=-1, keepdims=True)
    expo = jnp.exp(score - top)
    weights = (expo / jnp.sum(expo, axis=-1, keepdims=True)).astype(jnp.bfloat16)
    return [
        jnp.dot(weights[i * group : (i + 1) * group], v, preferred_element_type=jnp.float32)
        for i, v in enumerate(values)
    ]


def project(mixed, weight, out):
    heads = mixed.shape[1]
    rows = jnp.concatenate([mixed[:, h, :] for h in range(heads)], axis=1).astype(jnp.bfloat16)
    width = weight.shape[1] // CHUNKS
    for c in range(CHUNKS):
        part = jnp.dot(
            rows, weight[:, c * width : (c + 1) * width], preferred_element_type=jnp.float32
        )
        out[:, c * width : (c + 1) * width] = part.astype(jnp.bfloat16)


def first_kernel(half, span, *refs):
    far, parcels, out, weight = refs[:4], refs[4 : 6 + half], refs[6 + half], refs[7 + half]
    lengths, dest, query, source, mixed, sems = refs[8 + half :]
    copies = begin(list(zip(far, (lengths, dest, query, weight))), sems)
    parcels = parcels_of(parcels, half, span)
    finish(copies[:3])
    invert(dest, source, 2 * half)
    at = sources(source, half)
    results = attend(
        [query[r] for r in at],
        [parcel[0][...] for parcel in parcels],
        [parcel[1][...] for parcel in parcels],
        [lengths[r] + 1 for r in at],
    )
    for r, result in zip(at, results):
        mixed[r] = result
    copies[3].wait()
    project(mixed, weight, out)


def place(arrived, query, key_two, value_two, key_cache, value_cache, held, mixed, osems):
    count = len(arrived)
    slots = []
    lengths = []
    for parcel in arrived:
        tail = parcel[2][...].astype(jnp.float32)
        slots.append(jnp.max(tail[0:1, :]).astype(jnp.int32))
        lengths.append(jnp.max(tail[1:2, :]).astype(jnp.int32))
    for i, parcel in enumerate(arrived):
        held[0, i] = parcel[0][...]
        held[1, i] = parcel[1][...]
    outgoing = []
    for i in range(count):
        for which, (token, cache) in enumerate(((key_two, key_cache), (value_two, value_cache))):
            put_row(held.at[which, i], token[pl.ds(slots[i], 1), :], lengths[i] + 1)
            copy = pltpu.make_async_copy(held.at[which, i], cache.at[slots[i]], osems.at[which, i])
            copy.start()
            outgoing.append(copy)
    results = attend(
        [query[j] for j in slots],
        [held[0, i] for i in range(count)],
        [held[1, i] for i in range(count)],
        [length + 2 for length in lengths],
    )
    for j, result in zip(slots, results):
        mixed[j] = result
    return outgoing


def early_kernel(half, count, span, pair, *refs):
    arrived, far, halves = refs[: count + 1], refs[count + 1 : count + 4], refs[count + 4 : count + 4 + pair]
    key_cache, value_cache, mixed = refs[count + 4 + pair : count + 7 + pair]
    query, key_two, value_two, new_k, new_v, held, sems, osems = refs[-8:]
    copies = begin(list(zip(far, (query, key_two, value_two))), sems)
    if pair:
        out = refs[count + 7 + pair]
        both = halves[0][...].astype(jnp.float32) + halves[1][...].astype(jnp.float32)
        out[...] = both.astype(jnp.bfloat16)
    finish(copies)
    new_k[...] = key_two[...].astype(jnp.float32)
    new_v[...] = value_two[...].astype(jnp.float32)
    parcels = [views(arrived[0].at[d], span) for d in range(half)] + [views(ref, span) for ref in arrived[1:]]
    finish(place(parcels, query, new_k, new_v, key_cache, value_cache, held, mixed, osems))


def late_kernel(count, span, *refs):
    arrived, far, weight, before = refs[: count + 1], refs[count + 1 : count + 4], refs[count + 4], refs[count + 5]
    out, key_cache, value_cache = refs[count + 8 : count + 11]
    query, key_two, value_two, new_k, new_v, held, mixed, sems, osems = refs[-9:]
    copies = begin(list(zip(far, (query, key_two, value_two))), sems)
    mixed[...] = before[...]
    finish(copies)
    new_k[...] = key_two[...].astype(jnp.float32)
    new_v[...] = value_two[...].astype(jnp.float32)
    keys, rest = arrived[0], arrived[1]
    parcels = [(keys, rest.at[pl.ds(0, span)], rest.at[pl.ds(span, TAIL)])] + [views(ref, span) for ref in arrived[2:]]
    outgoing = place(parcels, query, new_k, new_v, key_cache, value_cache, held, mixed, osems)
    project(mixed, weight, out)
    finish(outgoing)


def swap(partial):
    return lax.ppermute(partial, "tp", [(0, 1), (1, 0)])


def near(x):
    return pltpu.with_memory_space_constraint(x, pltpu.VMEM)


def hbm(x):
    return pltpu.with_memory_space_constraint(x, pltpu.HBM)


def shards(
    n,
    tp,
    query_one,
    key_one,
    value_one,
    key_pages,
    value_pages,
    page_table,
    lengths,
    dest_instance,
    dest_slot,
    query_two,
    key_two,
    value_two,
    out_weight,
):
    slots, pages = page_table.shape
    pool, kv_heads, size, width = key_pages.shape
    heads = query_one.shape[1]
    depth, columns = out_weight.shape
    span = pages * size
    assert kv_heads == 1 and slots == n and n % 2 == 0 and span <= 256
    key_pages = key_pages.reshape(pool, size, width)
    value_pages = value_pages.reshape(pool, size, width)
    key_one = key_one.reshape(slots, width)
    value_one = value_one.reshape(slots, width)
    key_two = key_two.reshape(slots, width)
    value_two = value_two.reshape(slots, width)

    vmem = pl.BlockSpec(memory_space=pltpu.VMEM)
    far = pl.BlockSpec(memory_space=pltpu.HBM)
    params = pltpu.CompilerParams(vmem_limit_bytes=VMEM_BYTES)
    bf16, f32, i32 = jnp.bfloat16, jnp.float32, jnp.int32
    rows = 2 * span + TAIL
    half = n // 2

    def block(*lead):
        return jax.ShapeDtypeStruct((*lead, width), bf16)

    shapes = [block(half, rows), block(span), block(span + TAIL)] + [block(rows)] * (half - 1)

    packed = pl.pallas_call(
        functools.partial(pack_kernel, half, pages),
        out_shape=shapes,
        in_specs=[far] * 8,
        out_specs=[vmem] * len(shapes),
        scratch_shapes=[
            pltpu.SMEM((pages, slots), i32),
            pltpu.SMEM((slots,), i32),
            pltpu.SMEM((slots,), i32),
            pltpu.SMEM((slots,), i32),
            pltpu.VMEM((slots, width), bf16),
            pltpu.VMEM((slots, width), bf16),
            pltpu.VMEM((pool, size, width), bf16),
            pltpu.VMEM((pool, size, width), bf16),
            pltpu.SMEM((n,), i32),
            pltpu.SemaphoreType.DMA((8,)),
        ],
        compiler_params=params,
        cost_estimate=pl.CostEstimate(flops=0, bytes_accessed=4 * n * rows * width, transcendentals=0),
        name="pack",
    )(
        hbm(page_table.T),
        hbm(lengths),
        hbm(dest_instance),
        hbm(dest_slot),
        hbm(key_one),
        hbm(value_one),
        hbm(key_pages),
        hbm(value_pages),
    )

    flops = 4 * slots * heads * span * width + 2 * slots * depth * columns
    moved = 2 * depth * columns + 4 * slots * span * width
    def send(s, block):
        return lax.ppermute(block, "inst", [(i, i ^ s) for i in range(n)])

    def after(x, y):
        return lax.optimization_barrier((x, y))[0]

    home, split_keys, split_rest, others = packed[0], packed[1], packed[2], packed[3:]
    arrived_keys = send(half, split_keys)
    arrived = [send(half + 1 + i, others[i]) for i in range(AHEAD)]
    groups = [list(range(half)), list(range(half, n))]
    arrived_home = lax.all_to_all(home, "inst", 0, 0, axis_index_groups=groups, tiled=True)
    partial_one, weight = pl.pallas_call(
        functools.partial(first_kernel, half, span),
        out_shape=[
            jax.ShapeDtypeStruct((slots, columns), bf16),
            jax.ShapeDtypeStruct((depth, columns), bf16),
        ],
        in_specs=[far] * 4 + [vmem] * len(shapes),
        out_specs=[vmem, vmem],
        scratch_shapes=[
            pltpu.SMEM((slots,), i32),
            pltpu.SMEM((slots,), i32),
            pltpu.VMEM((slots, heads, width), bf16),
            pltpu.SMEM((n,), i32),
            pltpu.VMEM((slots, heads, width), f32),
            pltpu.SemaphoreType.DMA((4,)),
        ],
        compiler_params=params,
        cost_estimate=pl.CostEstimate(flops=flops, bytes_accessed=moved, transcendentals=slots * heads * span),
        name="first",
    )(hbm(lengths), hbm(dest_instance), hbm(after(query_one, arrived_home)), hbm(out_weight), *packed)

    arrived += [send(half + 1 + i, after(others[i], partial_one)) for i in range(AHEAD, half - 1)]
    arrived_rest = send(half, after(split_rest, partial_one))
    early, late = arrived[: half - LATE], [arrived_keys, arrived_rest] + arrived[half - LATE :]

    halves = [partial_one, swap(partial_one)] if tp == 2 else []
    cache = jax.ShapeDtypeStruct((slots, span, width), bf16)
    common = [
        pltpu.VMEM((slots, heads, width), bf16),
        pltpu.VMEM((slots, width), bf16),
        pltpu.VMEM((slots, width), bf16),
        pltpu.VMEM((slots, width), f32),
        pltpu.VMEM((slots, width), f32),
    ]
    mixed = jax.ShapeDtypeStruct((slots, heads, width), f32)
    some = half + len(early)
    results = pl.pallas_call(
        functools.partial(early_kernel, half, len(early), span, len(halves)),
        out_shape=[cache, cache, mixed] + [jax.ShapeDtypeStruct((slots, columns), bf16)] * (len(halves) // 2),
        in_specs=[vmem] * (1 + len(early)) + [far] * 3 + [vmem] * len(halves),
        out_specs=[far, far, vmem] + [vmem] * (len(halves) // 2),
        scratch_shapes=common
        + [
            pltpu.VMEM((2, some, span, width), bf16),
            pltpu.SemaphoreType.DMA((3,)),
            pltpu.SemaphoreType.DMA((2, some)),
        ],
        compiler_params=params,
        cost_estimate=pl.CostEstimate(
            flops=4 * some * heads * span * width,
            bytes_accessed=8 * some * span * width,
            transcendentals=some * heads * span,
        ),
        name="early",
    )(near(arrived_home), *early, hbm(query_two), hbm(key_two), hbm(value_two), *halves)
    key_cache, value_cache, mixed = results[:3]
    out_one = results[3] if halves else lax.psum(partial_one, "tp")

    partial_two, key_cache, value_cache = pl.pallas_call(
        functools.partial(late_kernel, LATE, span),
        out_shape=[jax.ShapeDtypeStruct((slots, columns), bf16), cache, cache],
        in_specs=[vmem] * len(late) + [far] * 3 + [vmem] * 2 + [far] * 2,
        out_specs=[vmem, far, far],
        input_output_aliases={len(late) + 5: 1, len(late) + 6: 2},
        scratch_shapes=common
        + [
            pltpu.VMEM((2, LATE, span, width), bf16),
            pltpu.VMEM((slots, heads, width), f32),
            pltpu.SemaphoreType.DMA((3,)),
            pltpu.SemaphoreType.DMA((2, LATE)),
        ],
        compiler_params=params,
        cost_estimate=pl.CostEstimate(flops=flops, bytes_accessed=moved, transcendentals=LATE * heads * span),
        name="late",
    )(
        *late,
        hbm(query_two),
        hbm(key_two),
        hbm(value_two),
        near(weight),
        mixed,
        hbm(key_cache),
        hbm(value_cache),
    )
    if tp == 2:
        both = partial_two.astype(f32) + swap(partial_two).astype(f32)
        out_two = both.astype(bf16)
    else:
        out_two = lax.psum(partial_two, "tp")
    shape = (slots * pages, kv_heads, size, width)
    return (out_one, out_two, key_cache.reshape(shape), value_cache.reshape(shape))


def solution(mesh):
    sizes = dict(mesh.shape)
    return jax.shard_map(
        functools.partial(shards, sizes["inst"], sizes["tp"]),
        mesh=mesh,
        in_specs=(
            P("inst", "tp", None),
            P("inst", "tp", None),
            P("inst", "tp", None),
            P("inst", "tp", None, None),
            P("inst", "tp", None, None),
            P("inst", None),
            P("inst"),
            P("inst"),
            P("inst"),
            P("inst", "tp", None),
            P("inst", "tp", None),
            P("inst", "tp", None),
            P("tp", None),
        ),
        out_specs=(
            P("inst", None),
            P("inst", None),
            P("inst", "tp", None, None),
            P("inst", "tp", None, None),
        ),
        check_vma=False,
    )
```

```python
import functools

import jax
import jax.numpy as jnp
from jax import lax
from jax.experimental import pallas as pl
from jax.experimental.pallas import tpu as pltpu
from jax.sharding import PartitionSpec as P

NEG = -1e30
TAIL = 16
CHUNKS = 8
AHEAD = 6
LATE = 3
VMEM_BYTES = 24 * 1024 * 1024


def row_of(block, at):
    rows = lax.broadcasted_iota(jnp.int32, block.shape, 0)
    return jnp.sum(jnp.where(rows == at, block, 0.0), axis=0, keepdims=True)


def put_row(block, row, position):
    base = pl.multiple_of(position // TAIL * TAIL, TAIL)
    part = block[pl.ds(base, TAIL), :]
    at = lax.broadcasted_iota(jnp.int32, part.shape, 0)
    mixed = jnp.where(at == position % TAIL, row, part.astype(jnp.float32))
    block[pl.ds(base, TAIL), :] = mixed.astype(jnp.bfloat16)


def invert(dest, source, n):
    def note(r, carry):
        source[dest[r]] = r
        return carry

    lax.fori_loop(0, n, note, 0)


def begin(pairs, sem):
    copies = [pltpu.make_async_copy(a, b, sem.at[i]) for i, (a, b) in enumerate(pairs)]
    for copy in copies:
        copy.start()
    return copies


def finish(copies):
    for copy in copies:
        copy.wait()


def parcels_of(refs, span):
    return [
        (ref.at[pl.ds(0, span)], ref.at[pl.ds(span, span)], ref.at[pl.ds(2 * span, TAIL)]) for ref in refs
    ]


def sources(source, steps):
    me = lax.axis_index("inst")
    return [source[me ^ s] for s in steps]


def pack_kernel(steps, pages, *refs):
    n = len(steps)
    far, outs = refs[:8], refs[8 : 8 + n]
    table, lengths, dest, slot, key_one, value_one, key_pool, value_pool, source, sems = refs[8 + n :]
    copies = begin(list(zip(far, (table, lengths, dest, slot, key_one, value_one, key_pool, value_pool))), sems)
    size = key_pool.shape[1]
    parcels = parcels_of(outs, pages * size)
    finish(copies[:6])
    invert(dest, source, n)
    at = sources(source, steps)
    tokens = (key_one[...].astype(jnp.float32), value_one[...].astype(jnp.float32))
    for which, pool in ((0, key_pool), (1, value_pool)):
        copies[6 + which].wait()
        for r, parcel in zip(at, parcels):
            for p in range(pages):
                parcel[which][p * size : (p + 1) * size, :] = pool[table[p, r]]
            put_row(parcel[which], row_of(tokens[which], r), lengths[r])
    rows = lax.broadcasted_iota(jnp.int32, (TAIL, key_one.shape[1]), 0)
    for r, parcel in zip(at, parcels):
        tail = jnp.where(rows == 0, slot[r].astype(jnp.float32), lengths[r].astype(jnp.float32))
        parcel[2][...] = tail.astype(jnp.bfloat16)


def attend(queries, keys, values, counts):
    width = queries[0].shape[1]
    scores = []
    for q, k, count in zip(queries, keys, counts):
        s = lax.dot_general(q, k, (((1,), (1,)), ((), ())), preferred_element_type=jnp.float32)
        live = lax.broadcasted_iota(jnp.int32, s.shape, 1) < count
        scores.append(jnp.where(live, s * width ** (-0.5), NEG))
    group = scores[0].shape[0]
    score = jnp.concatenate(scores, axis=0)
    top = jnp.max(score, axis=-1, keepdims=True)
    expo = jnp.exp(score - top)
    weights = (expo / jnp.sum(expo, axis=-1, keepdims=True)).astype(jnp.bfloat16)
    return [
        jnp.dot(weights[i * group : (i + 1) * group], v, preferred_element_type=jnp.float32)
        for i, v in enumerate(values)
    ]


def project(mixed, weight, out):
    heads = mixed.shape[1]
    rows = jnp.concatenate([mixed[:, h, :] for h in range(heads)], axis=1).astype(jnp.bfloat16)
    width = weight.shape[1] // CHUNKS
    for c in range(CHUNKS):
        part = jnp.dot(
            rows, weight[:, c * width : (c + 1) * width], preferred_element_type=jnp.float32
        )
        out[:, c * width : (c + 1) * width] = part.astype(jnp.bfloat16)


def first_kernel(steps, span, *refs):
    n = len(steps)
    far, parcels, out, weight = refs[:4], refs[4 : 4 + n], refs[4 + n], refs[5 + n]
    lengths, dest, query, source, mixed, sems = refs[6 + n :]
    copies = begin(list(zip(far, (lengths, dest, query, weight))), sems)
    parcels = parcels_of(parcels, span)
    finish(copies[:3])
    invert(dest, source, n)
    at = sources(source, steps)
    results = attend(
        [query[r] for r in at],
        [parcel[0][...] for parcel in parcels],
        [parcel[1][...] for parcel in parcels],
        [lengths[r] + 1 for r in at],
    )
    for r, result in zip(at, results):
        mixed[r] = result
    copies[3].wait()
    project(mixed, weight, out)


def place(arrived, query, key_two, value_two, key_cache, value_cache, held, mixed, osems):
    count = len(arrived)
    slots = []
    lengths = []
    for parcel in arrived:
        tail = parcel[2][...].astype(jnp.float32)
        slots.append(jnp.max(tail[0:1, :]).astype(jnp.int32))
        lengths.append(jnp.max(tail[1:2, :]).astype(jnp.int32))
    for i, parcel in enumerate(arrived):
        held[0, i] = parcel[0][...]
        held[1, i] = parcel[1][...]
    outgoing = []
    for i in range(count):
        for which, (token, cache) in enumerate(((key_two, key_cache), (value_two, value_cache))):
            put_row(held.at[which, i], token[pl.ds(slots[i], 1), :], lengths[i] + 1)
            copy = pltpu.make_async_copy(held.at[which, i], cache.at[slots[i]], osems.at[which, i])
            copy.start()
            outgoing.append(copy)
    results = attend(
        [query[j] for j in slots],
        [held[0, i] for i in range(count)],
        [held[1, i] for i in range(count)],
        [length + 2 for length in lengths],
    )
    for j, result in zip(slots, results):
        mixed[j] = result
    return outgoing


def early_kernel(count, span, pair, *refs):
    arrived, far, halves = refs[:count], refs[count : count + 3], refs[count + 3 : count + 3 + pair]
    key_cache, value_cache, mixed, query, new_k, new_v = refs[count + 3 + pair : count + 9 + pair]
    key_two, value_two, held, sems, osems = refs[-5:]
    copies = begin(list(zip(far, (query, key_two, value_two))), sems)
    if pair:
        out = refs[count + 9 + pair]
        both = halves[0][...].astype(jnp.float32) + halves[1][...].astype(jnp.float32)
        out[...] = both.astype(jnp.bfloat16)
    finish(copies)
    new_k[...] = key_two[...].astype(jnp.float32)
    new_v[...] = value_two[...].astype(jnp.float32)
    parcels = parcels_of(arrived, span)
    finish(place(parcels, query, new_k, new_v, key_cache, value_cache, held, mixed, osems))


def late_kernel(count, span, *refs):
    arrived, (query, new_k, new_v, weight, before) = refs[:count], refs[count : count + 5]
    out, key_cache, value_cache, held, mixed, osems = refs[count + 7 :]
    mixed[...] = before[...]
    parcels = parcels_of(arrived, span)
    outgoing = place(parcels, query, new_k, new_v, key_cache, value_cache, held, mixed, osems)
    project(mixed, weight, out)
    finish(outgoing)


def swap(partial):
    return lax.ppermute(partial, "tp", [(0, 1), (1, 0)])


def near(x):
    return pltpu.with_memory_space_constraint(x, pltpu.VMEM)


def hbm(x):
    return pltpu.with_memory_space_constraint(x, pltpu.HBM)


def step_order(n):
    half = n // 2
    crossing = [s for pair in zip(range(half, half + half // 2), range(half + half // 2, n)) for s in pair]
    staying = list(range(1, half))
    order = []
    for kind in "cnnccncnccncncn":
        queue = crossing if kind == "c" else staying
        if queue:
            order.append(queue.pop(0))
    while crossing or staying:
        order += crossing[:1] + staying[:1]
        del crossing[:1], staying[:1]
    return order


def shards(
    n,
    tp,
    query_one,
    key_one,
    value_one,
    key_pages,
    value_pages,
    page_table,
    lengths,
    dest_instance,
    dest_slot,
    query_two,
    key_two,
    value_two,
    out_weight,
):
    slots, pages = page_table.shape
    pool, kv_heads, size, width = key_pages.shape
    heads = query_one.shape[1]
    depth, columns = out_weight.shape
    span = pages * size
    assert kv_heads == 1 and slots == n and n >= 16 and span <= 256
    key_pages = key_pages.reshape(pool, size, width)
    value_pages = value_pages.reshape(pool, size, width)
    key_one = key_one.reshape(slots, width)
    value_one = value_one.reshape(slots, width)
    key_two = key_two.reshape(slots, width)
    value_two = value_two.reshape(slots, width)

    vmem = pl.BlockSpec(memory_space=pltpu.VMEM)
    far = pl.BlockSpec(memory_space=pltpu.HBM)
    params = pltpu.CompilerParams(vmem_limit_bytes=VMEM_BYTES)
    bf16, f32, i32 = jnp.bfloat16, jnp.float32, jnp.int32
    rows = 2 * span + TAIL
    order = step_order(n)
    steps = [0] + order

    def block(height):
        return jax.ShapeDtypeStruct((height, width), bf16)

    shapes = [block(rows)] * n

    packed = pl.pallas_call(
        functools.partial(pack_kernel, steps, pages),
        out_shape=shapes,
        in_specs=[far] * 8,
        out_specs=[vmem] * len(shapes),
        scratch_shapes=[
            pltpu.SMEM((pages, slots), i32),
            pltpu.SMEM((slots,), i32),
            pltpu.SMEM((slots,), i32),
            pltpu.SMEM((slots,), i32),
            pltpu.VMEM((slots, width), bf16),
            pltpu.VMEM((slots, width), bf16),
            pltpu.VMEM((pool, size, width), bf16),
            pltpu.VMEM((pool, size, width), bf16),
            pltpu.SMEM((n,), i32),
            pltpu.SemaphoreType.DMA((8,)),
        ],
        compiler_params=params,
        cost_estimate=pl.CostEstimate(flops=0, bytes_accessed=4 * n * rows * width, transcendentals=0),
        name="pack",
    )(
        hbm(page_table.T),
        hbm(lengths),
        hbm(dest_instance),
        hbm(dest_slot),
        hbm(key_one),
        hbm(value_one),
        hbm(key_pages),
        hbm(value_pages),
    )

    flops = 4 * slots * heads * span * width + 2 * slots * depth * columns
    moved = 2 * depth * columns + 4 * slots * span * width
    arrived = [packed[0]]

    def send(i, *after):
        block = lax.optimization_barrier((packed[i], *after))[0] if after else packed[i]
        arrived.append(lax.ppermute(block, "inst", [(d, d ^ steps[i]) for d in range(n)]))

    for i in range(1, 1 + AHEAD):
        send(i)
    query_late = lax.optimization_barrier((query_one, arrived[1]))[0]
    partial_one, weight = pl.pallas_call(
        functools.partial(first_kernel, steps, span),
        out_shape=[
            jax.ShapeDtypeStruct((slots, columns), bf16),
            jax.ShapeDtypeStruct((depth, columns), bf16),
        ],
        in_specs=[far] * 4 + [vmem] * len(shapes),
        out_specs=[vmem, vmem],
        scratch_shapes=[
            pltpu.SMEM((slots,), i32),
            pltpu.SMEM((slots,), i32),
            pltpu.VMEM((slots, heads, width), bf16),
            pltpu.SMEM((n,), i32),
            pltpu.VMEM((slots, heads, width), f32),
            pltpu.SemaphoreType.DMA((4,)),
        ],
        compiler_params=params,
        cost_estimate=pl.CostEstimate(flops=flops, bytes_accessed=moved, transcendentals=slots * heads * span),
        name="first",
    )(hbm(lengths), hbm(dest_instance), hbm(query_late), hbm(out_weight), *packed)

    for i in range(1 + AHEAD, n):
        send(i, partial_one)
    early, late = arrived[:-LATE], arrived[-LATE:]
    halves = [partial_one, swap(partial_one)] if tp == 2 else []

    cache = jax.ShapeDtypeStruct((slots, span, width), bf16)
    mixed = jax.ShapeDtypeStruct((slots, heads, width), f32)
    some = len(early)
    results = pl.pallas_call(
        functools.partial(early_kernel, some, span, len(halves)),
        out_shape=[cache, cache, mixed]
        + [jax.ShapeDtypeStruct((slots, heads, width), bf16)]
        + [jax.ShapeDtypeStruct((slots, width), f32)] * 2
        + [jax.ShapeDtypeStruct((slots, columns), bf16)] * (len(halves) // 2),
        in_specs=[vmem] * some + [far] * 3 + [vmem] * len(halves),
        out_specs=[far, far] + [vmem] * (4 + len(halves) // 2),
        scratch_shapes=[
            pltpu.VMEM((slots, width), bf16),
            pltpu.VMEM((slots, width), bf16),
            pltpu.VMEM((2, some, span, width), bf16),
            pltpu.SemaphoreType.DMA((3,)),
            pltpu.SemaphoreType.DMA((2, some)),
        ],
        compiler_params=params,
        cost_estimate=pl.CostEstimate(
            flops=4 * some * heads * span * width,
            bytes_accessed=8 * some * span * width,
            transcendentals=some * heads * span,
        ),
        name="early",
    )(*early, hbm(query_two), hbm(key_two), hbm(value_two), *halves)
    key_cache, value_cache, *carried = results[:6]
    out_one = results[6] if halves else lax.psum(partial_one, "tp")

    partial_two, key_cache, value_cache = pl.pallas_call(
        functools.partial(late_kernel, LATE, span),
        out_shape=[jax.ShapeDtypeStruct((slots, columns), bf16), cache, cache],
        in_specs=[vmem] * (len(late) + 5) + [far] * 2,
        out_specs=[vmem, far, far],
        input_output_aliases={len(late) + 5: 1, len(late) + 6: 2},
        scratch_shapes=[
            pltpu.VMEM((2, LATE, span, width), bf16),
            pltpu.VMEM((slots, heads, width), f32),
            pltpu.SemaphoreType.DMA((2, LATE)),
        ],
        compiler_params=params,
        cost_estimate=pl.CostEstimate(flops=flops, bytes_accessed=moved, transcendentals=LATE * heads * span),
        name="late",
    )(
        *late,
        *[near(x) for x in carried[1:]],
        near(weight),
        near(carried[0]),
        hbm(key_cache),
        hbm(value_cache),
    )
    if tp == 2:
        both = partial_two.astype(f32) + swap(partial_two).astype(f32)
        out_two = both.astype(bf16)
    else:
        out_two = lax.psum(partial_two, "tp")
    shape = (slots * pages, kv_heads, size, width)
    return (out_one, out_two, key_cache.reshape(shape), value_cache.reshape(shape))


def solution(mesh):
    sizes = dict(mesh.shape)
    return jax.shard_map(
        functools.partial(shards, sizes["inst"], sizes["tp"]),
        mesh=mesh,
        in_specs=(
            P("inst", "tp", None),
            P("inst", "tp", None),
            P("inst", "tp", None),
            P("inst", "tp", None, None),
            P("inst", "tp", None, None),
            P("inst", None),
            P("inst"),
            P("inst"),
            P("inst"),
            P("inst", "tp", None),
            P("inst", "tp", None),
            P("inst", "tp", None),
            P("tp", None),
        ),
        out_specs=(
            P("inst", None),
            P("inst", None),
            P("inst", "tp", None, None),
            P("inst", "tp", None, None),
        ),
        check_vma=False,
    )
```

```python
import functools

import jax
import jax.numpy as jnp
from jax import lax
from jax.experimental import pallas as pl
from jax.experimental.pallas import tpu as pltpu
from jax.sharding import PartitionSpec as P

NEG = -1e30
TAIL = 16
CHUNKS = 8
AHEAD = 5
LATE = 5
VMEM_BYTES = 24 * 1024 * 1024


def row_of(block, at):
    rows = lax.broadcasted_iota(jnp.int32, block.shape, 0)
    return jnp.sum(jnp.where(rows == at, block, 0.0), axis=0, keepdims=True)


def put_row(block, row, position):
    base = pl.multiple_of(position // TAIL * TAIL, TAIL)
    part = block[pl.ds(base, TAIL), :]
    at = lax.broadcasted_iota(jnp.int32, part.shape, 0)
    mixed = jnp.where(at == position % TAIL, row, part.astype(jnp.float32))
    block[pl.ds(base, TAIL), :] = mixed.astype(jnp.bfloat16)


def invert(dest, source, n):
    def note(r, carry):
        source[dest[r]] = r
        return carry

    lax.fori_loop(0, n, note, 0)


def begin(pairs, sem):
    copies = [pltpu.make_async_copy(a, b, sem.at[i]) for i, (a, b) in enumerate(pairs)]
    for copy in copies:
        copy.start()
    return copies


def finish(copies):
    for copy in copies:
        copy.wait()


def parcels_of(refs, span):
    return [
        (ref.at[pl.ds(0, span)], ref.at[pl.ds(span, span)], ref.at[pl.ds(2 * span, TAIL)]) for ref in refs
    ]


def sources(source, steps):
    me = lax.axis_index("inst")
    return [source[me ^ s] for s in steps]


def pack_kernel(steps, pages, *refs):
    n = len(steps)
    far, outs = refs[:8], refs[8 : 8 + n]
    table, lengths, dest, slot, key_one, value_one, key_pool, value_pool, source, sems = refs[8 + n :]
    copies = begin(list(zip(far, (table, lengths, dest, slot, key_one, value_one, key_pool, value_pool))), sems)
    size = key_pool.shape[1]
    parcels = parcels_of(outs, pages * size)
    finish(copies[:6])
    invert(dest, source, n)
    at = sources(source, steps)
    tokens = (key_one[...].astype(jnp.float32), value_one[...].astype(jnp.float32))
    for which, pool in ((0, key_pool), (1, value_pool)):
        copies[6 + which].wait()
        for r, parcel in zip(at, parcels):
            for p in range(pages):
                parcel[which][p * size : (p + 1) * size, :] = pool[table[p, r]]
            put_row(parcel[which], row_of(tokens[which], r), lengths[r])
    rows = lax.broadcasted_iota(jnp.int32, (TAIL, key_one.shape[1]), 0)
    for r, parcel in zip(at, parcels):
        tail = jnp.where(rows == 0, slot[r].astype(jnp.float32), lengths[r].astype(jnp.float32))
        parcel[2][...] = tail.astype(jnp.bfloat16)


def attend(queries, keys, values, counts):
    width = queries[0].shape[1]
    scores = []
    for q, k, count in zip(queries, keys, counts):
        s = lax.dot_general(q, k, (((1,), (1,)), ((), ())), preferred_element_type=jnp.float32)
        live = lax.broadcasted_iota(jnp.int32, s.shape, 1) < count
        scores.append(jnp.where(live, s * width ** (-0.5), NEG))
    group = scores[0].shape[0]
    score = jnp.concatenate(scores, axis=0)
    top = jnp.max(score, axis=-1, keepdims=True)
    expo = jnp.exp(score - top)
    weights = (expo / jnp.sum(expo, axis=-1, keepdims=True)).astype(jnp.bfloat16)
    return [
        jnp.dot(weights[i * group : (i + 1) * group], v, preferred_element_type=jnp.float32)
        for i, v in enumerate(values)
    ]


def project(mixed, weight, out):
    heads = mixed.shape[1]
    rows = jnp.concatenate([mixed[:, h, :] for h in range(heads)], axis=1).astype(jnp.bfloat16)
    width = weight.shape[1] // CHUNKS
    for c in range(CHUNKS):
        part = jnp.dot(
            rows, weight[:, c * width : (c + 1) * width], preferred_element_type=jnp.float32
        )
        out[:, c * width : (c + 1) * width] = part.astype(jnp.bfloat16)


def first_kernel(steps, span, *refs):
    n = len(steps)
    far, parcels, out, weight = refs[:4], refs[4 : 4 + n], refs[4 + n], refs[5 + n]
    lengths, dest, query, source, mixed, sems = refs[6 + n :]
    copies = begin(list(zip(far, (lengths, dest, query, weight))), sems)
    parcels = parcels_of(parcels, span)
    finish(copies[:3])
    invert(dest, source, n)
    at = sources(source, steps)
    results = attend(
        [query[r] for r in at],
        [parcel[0][...] for parcel in parcels],
        [parcel[1][...] for parcel in parcels],
        [lengths[r] + 1 for r in at],
    )
    for r, result in zip(at, results):
        mixed[r] = result
    copies[3].wait()
    project(mixed, weight, out)


def place(arrived, query, key_two, value_two, key_cache, value_cache, held, mixed, osems):
    count = len(arrived)
    slots = []
    lengths = []
    for parcel in arrived:
        tail = parcel[2][...].astype(jnp.float32)
        slots.append(jnp.max(tail[0:1, :]).astype(jnp.int32))
        lengths.append(jnp.max(tail[1:2, :]).astype(jnp.int32))
    for i, parcel in enumerate(arrived):
        held[0, i] = parcel[0][...]
        held[1, i] = parcel[1][...]
    outgoing = []
    for i in range(count):
        for which, (token, cache) in enumerate(((key_two, key_cache), (value_two, value_cache))):
            put_row(held.at[which, i], token[pl.ds(slots[i], 1), :], lengths[i] + 1)
            copy = pltpu.make_async_copy(held.at[which, i], cache.at[slots[i]], osems.at[which, i])
            copy.start()
            outgoing.append(copy)
    results = attend(
        [query[j] for j in slots],
        [held[0, i] for i in range(count)],
        [held[1, i] for i in range(count)],
        [length + 2 for length in lengths],
    )
    for j, result in zip(slots, results):
        mixed[j] = result
    return outgoing


def early_kernel(count, span, pair, *refs):
    arrived, far, halves = refs[:count], refs[count : count + 3], refs[count + 3 : count + 3 + pair]
    key_cache, value_cache, mixed, query, new_k, new_v = refs[count + 3 + pair : count + 9 + pair]
    key_two, value_two, held, sems, osems = refs[-5:]
    copies = begin(list(zip(far, (query, key_two, value_two))), sems)
    if pair:
        out = refs[count + 9 + pair]
        both = halves[0][...].astype(jnp.float32) + halves[1][...].astype(jnp.float32)
        out[...] = both.astype(jnp.bfloat16)
    finish(copies)
    new_k[...] = key_two[...].astype(jnp.float32)
    new_v[...] = value_two[...].astype(jnp.float32)
    parcels = parcels_of(arrived, span)
    finish(place(parcels, query, new_k, new_v, key_cache, value_cache, held, mixed, osems))


def late_kernel(count, span, *refs):
    arrived, (query, new_k, new_v, weight, before) = refs[:count], refs[count : count + 5]
    out, key_cache, value_cache, held, mixed, osems = refs[count + 7 :]
    mixed[...] = before[...]
    parcels = parcels_of(arrived, span)
    outgoing = place(parcels, query, new_k, new_v, key_cache, value_cache, held, mixed, osems)
    project(mixed, weight, out)
    finish(outgoing)


def swap(partial):
    return lax.ppermute(partial, "tp", [(0, 1), (1, 0)])


def near(x):
    return pltpu.with_memory_space_constraint(x, pltpu.VMEM)


def hbm(x):
    return pltpu.with_memory_space_constraint(x, pltpu.HBM)


def step_order(n):
    half = n // 2
    crossing = list(range(half, n))
    staying = list(range(1, half))
    order = []
    for kind in "cncncncncncncnc":
        queue = crossing if kind == "c" else staying
        if queue:
            order.append(queue.pop(0))
    while crossing or staying:
        order += crossing[:1] + staying[:1]
        del crossing[:1], staying[:1]
    return order


def shards(
    n,
    tp,
    query_one,
    key_one,
    value_one,
    key_pages,
    value_pages,
    page_table,
    lengths,
    dest_instance,
    dest_slot,
    query_two,
    key_two,
    value_two,
    out_weight,
):
    slots, pages = page_table.shape
    pool, kv_heads, size, width = key_pages.shape
    heads = query_one.shape[1]
    depth, columns = out_weight.shape
    span = pages * size
    assert kv_heads == 1 and slots == n and n >= 16 and span <= 256
    key_pages = key_pages.reshape(pool, size, width)
    value_pages = value_pages.reshape(pool, size, width)
    key_one = key_one.reshape(slots, width)
    value_one = value_one.reshape(slots, width)
    key_two = key_two.reshape(slots, width)
    value_two = value_two.reshape(slots, width)

    vmem = pl.BlockSpec(memory_space=pltpu.VMEM)
    far = pl.BlockSpec(memory_space=pltpu.HBM)
    params = pltpu.CompilerParams(vmem_limit_bytes=VMEM_BYTES)
    bf16, f32, i32 = jnp.bfloat16, jnp.float32, jnp.int32
    rows = 2 * span + TAIL
    order = step_order(n)
    steps = [0] + order

    def block(height):
        return jax.ShapeDtypeStruct((height, width), bf16)

    shapes = [block(rows)] * n

    packed = pl.pallas_call(
        functools.partial(pack_kernel, steps, pages),
        out_shape=shapes,
        in_specs=[far] * 8,
        out_specs=[vmem] * len(shapes),
        scratch_shapes=[
            pltpu.SMEM((pages, slots), i32),
            pltpu.SMEM((slots,), i32),
            pltpu.SMEM((slots,), i32),
            pltpu.SMEM((slots,), i32),
            pltpu.VMEM((slots, width), bf16),
            pltpu.VMEM((slots, width), bf16),
            pltpu.VMEM((pool, size, width), bf16),
            pltpu.VMEM((pool, size, width), bf16),
            pltpu.SMEM((n,), i32),
            pltpu.SemaphoreType.DMA((8,)),
        ],
        compiler_params=params,
        cost_estimate=pl.CostEstimate(flops=0, bytes_accessed=4 * n * rows * width, transcendentals=0),
        name="pack",
    )(
        hbm(page_table.T),
        hbm(lengths),
        hbm(dest_instance),
        hbm(dest_slot),
        hbm(key_one),
        hbm(value_one),
        hbm(key_pages),
        hbm(value_pages),
    )

    flops = 4 * slots * heads * span * width + 2 * slots * depth * columns
    moved = 2 * depth * columns + 4 * slots * span * width
    arrived = [packed[0]]

    def send(i, *after):
        block = lax.optimization_barrier((packed[i], *after))[0] if after else packed[i]
        arrived.append(lax.ppermute(block, "inst", [(d, d ^ steps[i]) for d in range(n)]))

    for i in range(1, 1 + AHEAD):
        send(i)
    partial_one, weight = pl.pallas_call(
        functools.partial(first_kernel, steps, span),
        out_shape=[
            jax.ShapeDtypeStruct((slots, columns), bf16),
            jax.ShapeDtypeStruct((depth, columns), bf16),
        ],
        in_specs=[far] * 4 + [vmem] * len(shapes),
        out_specs=[vmem, vmem],
        scratch_shapes=[
            pltpu.SMEM((slots,), i32),
            pltpu.SMEM((slots,), i32),
            pltpu.VMEM((slots, heads, width), bf16),
            pltpu.SMEM((n,), i32),
            pltpu.VMEM((slots, heads, width), f32),
            pltpu.SemaphoreType.DMA((4,)),
        ],
        compiler_params=params,
        cost_estimate=pl.CostEstimate(flops=flops, bytes_accessed=moved, transcendentals=slots * heads * span),
        name="first",
    )(hbm(lengths), hbm(dest_instance), hbm(query_one), hbm(out_weight), *packed)

    for i in range(1 + AHEAD, n):
        send(i, partial_one)
    early, late = arrived[:-LATE], arrived[-LATE:]
    halves = []
    if tp == 2:
        halves = [partial_one, swap(lax.optimization_barrier((partial_one, arrived[n // 2]))[0])]

    cache = jax.ShapeDtypeStruct((slots, span, width), bf16)
    mixed = jax.ShapeDtypeStruct((slots, heads, width), f32)
    some = len(early)
    results = pl.pallas_call(
        functools.partial(early_kernel, some, span, len(halves)),
        out_shape=[cache, cache, mixed]
        + [jax.ShapeDtypeStruct((slots, heads, width), bf16)]
        + [jax.ShapeDtypeStruct((slots, width), f32)] * 2
        + [jax.ShapeDtypeStruct((slots, columns), bf16)] * (len(halves) // 2),
        in_specs=[vmem] * some + [far] * 3 + [vmem] * len(halves),
        out_specs=[far, far] + [vmem] * (4 + len(halves) // 2),
        scratch_shapes=[
            pltpu.VMEM((slots, width), bf16),
            pltpu.VMEM((slots, width), bf16),
            pltpu.VMEM((2, some, span, width), bf16),
            pltpu.SemaphoreType.DMA((3,)),
            pltpu.SemaphoreType.DMA((2, some)),
        ],
        compiler_params=params,
        cost_estimate=pl.CostEstimate(
            flops=4 * some * heads * span * width,
            bytes_accessed=8 * some * span * width,
            transcendentals=some * heads * span,
        ),
        name="early",
    )(*early, hbm(query_two), hbm(key_two), hbm(value_two), *halves)
    key_cache, value_cache, *carried = results[:6]
    out_one = results[6] if halves else lax.psum(partial_one, "tp")

    partial_two, key_cache, value_cache = pl.pallas_call(
        functools.partial(late_kernel, LATE, span),
        out_shape=[jax.ShapeDtypeStruct((slots, columns), bf16), cache, cache],
        in_specs=[vmem] * (len(late) + 5) + [far] * 2,
        out_specs=[vmem, far, far],
        input_output_aliases={len(late) + 5: 1, len(late) + 6: 2},
        scratch_shapes=[
            pltpu.VMEM((2, LATE, span, width), bf16),
            pltpu.VMEM((slots, heads, width), f32),
            pltpu.SemaphoreType.DMA((2, LATE)),
        ],
        compiler_params=params,
        cost_estimate=pl.CostEstimate(flops=flops, bytes_accessed=moved, transcendentals=LATE * heads * span),
        name="late",
    )(
        *late,
        *[near(x) for x in carried[1:]],
        near(weight),
        near(carried[0]),
        hbm(key_cache),
        hbm(value_cache),
    )
    if tp == 2:
        both = partial_two.astype(f32) + swap(partial_two).astype(f32)
        out_two = both.astype(bf16)
    else:
        out_two = lax.psum(partial_two, "tp")
    shape = (slots * pages, kv_heads, size, width)
    return (out_one, out_two, key_cache.reshape(shape), value_cache.reshape(shape))


def solution(mesh):
    sizes = dict(mesh.shape)
    return jax.shard_map(
        functools.partial(shards, sizes["inst"], sizes["tp"]),
        mesh=mesh,
        in_specs=(
            P("inst", "tp", None),
            P("inst", "tp", None),
            P("inst", "tp", None),
            P("inst", "tp", None, None),
            P("inst", "tp", None, None),
            P("inst", None),
            P("inst"),
            P("inst"),
            P("inst"),
            P("inst", "tp", None),
            P("inst", "tp", None),
            P("inst", "tp", None),
            P("tp", None),
        ),
        out_specs=(
            P("inst", None),
            P("inst", None),
            P("inst", "tp", None, None),
            P("inst", "tp", None, None),
        ),
        check_vma=False,
    )
```

```python
import functools

import jax
import jax.numpy as jnp
from jax import lax
from jax.experimental import pallas as pl
from jax.experimental.pallas import tpu as pltpu
from jax.sharding import PartitionSpec as P

NEG = -1e30
TILE = 16
SPLIT = 64
CHUNKS = 8
AHEAD = 5
LATE = 5
VMEM_BYTES = 24 * 1024 * 1024


def row_of(block, at):
    rows = lax.broadcasted_iota(jnp.int32, block.shape, 0)
    return jnp.sum(jnp.where(rows == at, block, 0.0), axis=0, keepdims=True)


def row_at(block, position):
    base = pl.multiple_of(position // TILE * TILE, TILE)
    return row_of(block[pl.ds(base, TILE), :].astype(jnp.float32), position % TILE)


def put_row(block, row, position):
    base = pl.multiple_of(position // TILE * TILE, TILE)
    part = block[pl.ds(base, TILE), :]
    at = lax.broadcasted_iota(jnp.int32, part.shape, 0)
    mixed = jnp.where(at == position % TILE, row, part.astype(jnp.float32))
    block[pl.ds(base, TILE), :] = mixed.astype(jnp.bfloat16)


def put_last(block, row):
    end = block.shape[0]
    part = block[end - TILE : end, :]
    at = lax.broadcasted_iota(jnp.int32, part.shape, 0)
    mixed = jnp.where(at == TILE - 1, row, part.astype(jnp.float32))
    block[end - TILE : end, :] = mixed.astype(jnp.bfloat16)


def last_row(block):
    end = block.shape[0]
    return block[end - TILE : end, :].astype(jnp.float32)[TILE - 1 : TILE, :]


def invert(dest, source, n):
    def note(r, carry):
        source[dest[r]] = r
        return carry

    lax.fori_loop(0, n, note, 0)


def begin(pairs, sem):
    copies = [pltpu.make_async_copy(a, b, sem.at[i]) for i, (a, b) in enumerate(pairs)]
    for copy in copies:
        copy.start()
    return copies


def finish(copies):
    for copy in copies:
        copy.wait()


def parcels_of(refs, span):
    return [(ref.at[pl.ds(0, span)], ref.at[pl.ds(span, span)]) for ref in refs]


def sources(source, steps):
    me = lax.axis_index("inst")
    return [source[me ^ s] for s in steps]


def pack_kernel(n, steps, pages, *refs):
    count = len(steps)
    far, outs = refs[:8], refs[8 : 8 + count]
    table, lengths, dest, slot, key_one, value_one, key_pool, value_pool, source, sems = refs[8 + count :]
    copies = begin(list(zip(far, (table, lengths, dest, slot, key_one, value_one, key_pool, value_pool))), sems)
    size = key_pool.shape[1]
    parcels = parcels_of(outs, pages * size)
    finish(copies[:6])
    invert(dest, source, n)
    at = sources(source, steps)
    tokens = (key_one[...].astype(jnp.float32), value_one[...].astype(jnp.float32))
    lanes = lax.broadcasted_iota(jnp.int32, (1, key_one.shape[1]), 1)
    for which, pool in ((0, key_pool), (1, value_pool)):
        copies[6 + which].wait()
        for r, parcel in zip(at, parcels):
            for p in range(pages):
                parcel[which][p * size : (p + 1) * size, :] = pool[table[p, r]]
            put_row(parcel[which], row_of(tokens[which], r), lengths[r])
            if which == 0:
                put_row(parcel[0], last_row(parcel[0]), lengths[r] + 1)
                note = jnp.where(lanes < SPLIT, slot[r], lengths[r]).astype(jnp.float32)
                put_last(parcel[0], note)


def attend(queries, keys, values, counts):
    width = queries[0].shape[1]
    scores = []
    for q, k, count in zip(queries, keys, counts):
        s = lax.dot_general(q, k, (((1,), (1,)), ((), ())), preferred_element_type=jnp.float32)
        live = lax.broadcasted_iota(jnp.int32, s.shape, 1) < count
        scores.append(jnp.where(live, s * width ** (-0.5), NEG))
    group = scores[0].shape[0]
    score = jnp.concatenate(scores, axis=0)
    top = jnp.max(score, axis=-1, keepdims=True)
    expo = jnp.exp(score - top)
    weights = (expo / jnp.sum(expo, axis=-1, keepdims=True)).astype(jnp.bfloat16)
    return [
        jnp.dot(weights[i * group : (i + 1) * group], v, preferred_element_type=jnp.float32)
        for i, v in enumerate(values)
    ]


def project(mixed, weight, out):
    heads = mixed.shape[1]
    rows = jnp.concatenate([mixed[:, h, :] for h in range(heads)], axis=1).astype(jnp.bfloat16)
    width = weight.shape[1] // CHUNKS
    for c in range(CHUNKS):
        part = jnp.dot(
            rows, weight[:, c * width : (c + 1) * width], preferred_element_type=jnp.float32
        )
        out[:, c * width : (c + 1) * width] = part.astype(jnp.bfloat16)


def first_kernel(steps, span, *refs):
    n = len(steps)
    far, parcels, out, weight = refs[:4], refs[4 : 4 + n], refs[4 + n], refs[5 + n]
    lengths, dest, query, source, mixed, sems = refs[6 + n :]
    copies = begin(list(zip(far, (lengths, dest, query, weight))), sems)
    parcels = parcels_of(parcels, span)
    finish(copies[:3])
    invert(dest, source, n)
    at = sources(source, steps)
    results = attend(
        [query[r] for r in at],
        [parcel[0][...] for parcel in parcels],
        [parcel[1][...] for parcel in parcels],
        [lengths[r] + 1 for r in at],
    )
    for r, result in zip(at, results):
        mixed[r] = result
    copies[3].wait()
    project(mixed, weight, out)


def place(arrived, query, key_two, value_two, key_cache, value_cache, held, mixed, osems):
    count = len(arrived)
    slots = []
    lengths = []
    for parcel in arrived:
        note = last_row(parcel[0])
        lanes = lax.broadcasted_iota(jnp.int32, note.shape, 1)
        slots.append(jnp.max(jnp.where(lanes < SPLIT, note, 0.0)).astype(jnp.int32))
        lengths.append(jnp.max(jnp.where(lanes < SPLIT, 0.0, note)).astype(jnp.int32))
    for i, parcel in enumerate(arrived):
        held[0, i] = parcel[0][...]
        held[1, i] = parcel[1][...]
        put_last(held.at[0, i], row_at(parcel[0], lengths[i] + 1))
    outgoing = []
    for i in range(count):
        for which, (token, cache) in enumerate(((key_two, key_cache), (value_two, value_cache))):
            put_row(held.at[which, i], token[pl.ds(slots[i], 1), :], lengths[i] + 1)
            copy = pltpu.make_async_copy(held.at[which, i], cache.at[slots[i]], osems.at[which, i])
            copy.start()
            outgoing.append(copy)
    results = attend(
        [query[j] for j in slots],
        [held[0, i] for i in range(count)],
        [held[1, i] for i in range(count)],
        [length + 2 for length in lengths],
    )
    for j, result in zip(slots, results):
        mixed[j] = result
    return outgoing


def early_kernel(count, span, pair, *refs):
    arrived, far, halves = refs[:count], refs[count : count + 3], refs[count + 3 : count + 3 + pair]
    key_cache, value_cache, mixed, query, new_k, new_v = refs[count + 3 + pair : count + 9 + pair]
    key_two, value_two, held, sems, osems = refs[-5:]
    copies = begin(list(zip(far, (query, key_two, value_two))), sems)
    if pair:
        out = refs[count + 9 + pair]
        both = halves[0][...].astype(jnp.float32) + halves[1][...].astype(jnp.float32)
        out[...] = both.astype(jnp.bfloat16)
    finish(copies)
    new_k[...] = key_two[...].astype(jnp.float32)
    new_v[...] = value_two[...].astype(jnp.float32)
    parcels = parcels_of(arrived, span)
    finish(place(parcels, query, new_k, new_v, key_cache, value_cache, held, mixed, osems))


def late_kernel(count, span, *refs):
    arrived, (query, new_k, new_v, weight, before) = refs[:count], refs[count : count + 5]
    out, key_cache, value_cache, held, mixed, osems = refs[count + 7 :]
    mixed[...] = before[...]
    parcels = parcels_of(arrived, span)
    outgoing = place(parcels, query, new_k, new_v, key_cache, value_cache, held, mixed, osems)
    project(mixed, weight, out)
    finish(outgoing)


def swap(partial):
    return lax.ppermute(partial, "tp", [(0, 1), (1, 0)])


def near(x):
    return pltpu.with_memory_space_constraint(x, pltpu.VMEM)


def hbm(x):
    return pltpu.with_memory_space_constraint(x, pltpu.HBM)


def step_order(n):
    half = n // 2
    crossing = list(range(half, n))
    staying = list(range(1, half))
    order = []
    for kind in "cncncncncncncnc":
        queue = crossing if kind == "c" else staying
        if queue:
            order.append(queue.pop(0))
    while crossing or staying:
        order += crossing[:1] + staying[:1]
        del crossing[:1], staying[:1]
    return order


def shards(
    n,
    tp,
    query_one,
    key_one,
    value_one,
    key_pages,
    value_pages,
    page_table,
    lengths,
    dest_instance,
    dest_slot,
    query_two,
    key_two,
    value_two,
    out_weight,
):
    slots, pages = page_table.shape
    pool, kv_heads, size, width = key_pages.shape
    heads = query_one.shape[1]
    depth, columns = out_weight.shape
    span = pages * size
    assert kv_heads == 1 and slots == n and n >= 16 and span <= 256
    key_pages = key_pages.reshape(pool, size, width)
    value_pages = value_pages.reshape(pool, size, width)
    key_one = key_one.reshape(slots, width)
    value_one = value_one.reshape(slots, width)
    key_two = key_two.reshape(slots, width)
    value_two = value_two.reshape(slots, width)

    vmem = pl.BlockSpec(memory_space=pltpu.VMEM)
    far = pl.BlockSpec(memory_space=pltpu.HBM)
    params = pltpu.CompilerParams(vmem_limit_bytes=VMEM_BYTES)
    bf16, f32, i32 = jnp.bfloat16, jnp.float32, jnp.int32
    rows = 2 * span
    order = step_order(n)
    steps = [0] + order

    def block(height):
        return jax.ShapeDtypeStruct((height, width), bf16)

    shapes = [block(rows)] * n

    def pack(chosen):
        return pl.pallas_call(
            functools.partial(pack_kernel, n, chosen, pages),
            out_shape=[jax.ShapeDtypeStruct((rows, width), bf16)] * len(chosen),
            in_specs=[far] * 8,
            out_specs=[vmem] * len(chosen),
            scratch_shapes=[
                pltpu.SMEM((pages, slots), i32),
                pltpu.SMEM((slots,), i32),
                pltpu.SMEM((slots,), i32),
                pltpu.SMEM((slots,), i32),
                pltpu.VMEM((slots, width), bf16),
                pltpu.VMEM((slots, width), bf16),
                pltpu.VMEM((pool, size, width), bf16),
                pltpu.VMEM((pool, size, width), bf16),
                pltpu.SMEM((n,), i32),
                pltpu.SemaphoreType.DMA((8,)),
            ],
            compiler_params=params,
            cost_estimate=pl.CostEstimate(
                flops=0, bytes_accessed=4 * len(chosen) * rows * width, transcendentals=0
            ),
            name="pack",
        )(
            hbm(page_table.T),
            hbm(lengths),
            hbm(dest_instance),
            hbm(dest_slot),
            hbm(key_one),
            hbm(value_one),
            hbm(key_pages),
            hbm(value_pages),
        )

    steps = step_order(n) + [0]
    packed = pack(steps[:AHEAD]) + pack(steps[AHEAD:])

    flops = 4 * slots * heads * span * width + 2 * slots * depth * columns
    moved = 2 * depth * columns + 4 * slots * span * width
    def send(i, *after):
        block = lax.optimization_barrier((packed[i], *after))[0] if after else packed[i]
        return lax.ppermute(block, "inst", [(d, d ^ steps[i]) for d in range(n)])

    arrived = [send(i) for i in range(AHEAD)]
    partial_one, weight = pl.pallas_call(
        functools.partial(first_kernel, steps, span),
        out_shape=[
            jax.ShapeDtypeStruct((slots, columns), bf16),
            jax.ShapeDtypeStruct((depth, columns), bf16),
        ],
        in_specs=[far] * 4 + [vmem] * len(shapes),
        out_specs=[vmem, vmem],
        scratch_shapes=[
            pltpu.SMEM((slots,), i32),
            pltpu.SMEM((slots,), i32),
            pltpu.VMEM((slots, heads, width), bf16),
            pltpu.SMEM((n,), i32),
            pltpu.VMEM((slots, heads, width), f32),
            pltpu.SemaphoreType.DMA((4,)),
        ],
        compiler_params=params,
        cost_estimate=pl.CostEstimate(flops=flops, bytes_accessed=moved, transcendentals=slots * heads * span),
        name="first",
    )(hbm(lengths), hbm(dest_instance), hbm(query_one), hbm(out_weight), *packed)

    arrived += [send(i, partial_one) for i in range(AHEAD, n - 1)]
    early, late = [packed[-1]] + arrived[:-LATE], arrived[-LATE:]
    halves = []
    if tp == 2:
        halves = [partial_one, swap(lax.optimization_barrier((partial_one, arrived[0]))[0])]

    cache = jax.ShapeDtypeStruct((slots, span, width), bf16)
    mixed = jax.ShapeDtypeStruct((slots, heads, width), f32)
    some = len(early)
    results = pl.pallas_call(
        functools.partial(early_kernel, some, span, len(halves)),
        out_shape=[cache, cache, mixed]
        + [jax.ShapeDtypeStruct((slots, heads, width), bf16)]
        + [jax.ShapeDtypeStruct((slots, width), f32)] * 2
        + [jax.ShapeDtypeStruct((slots, columns), bf16)] * (len(halves) // 2),
        in_specs=[vmem] * some + [far] * 3 + [vmem] * len(halves),
        out_specs=[far, far] + [vmem] * (4 + len(halves) // 2),
        scratch_shapes=[
            pltpu.VMEM((slots, width), bf16),
            pltpu.VMEM((slots, width), bf16),
            pltpu.VMEM((2, some, span, width), bf16),
            pltpu.SemaphoreType.DMA((3,)),
            pltpu.SemaphoreType.DMA((2, some)),
        ],
        compiler_params=params,
        cost_estimate=pl.CostEstimate(
            flops=4 * some * heads * span * width,
            bytes_accessed=8 * some * span * width,
            transcendentals=some * heads * span,
        ),
        name="early",
    )(*early, hbm(query_two), hbm(key_two), hbm(value_two), *halves)
    key_cache, value_cache, *carried = results[:6]
    out_one = results[6] if halves else lax.psum(partial_one, "tp")

    partial_two, key_cache, value_cache = pl.pallas_call(
        functools.partial(late_kernel, LATE, span),
        out_shape=[jax.ShapeDtypeStruct((slots, columns), bf16), cache, cache],
        in_specs=[vmem] * (len(late) + 5) + [far] * 2,
        out_specs=[vmem, far, far],
        input_output_aliases={len(late) + 5: 1, len(late) + 6: 2},
        scratch_shapes=[
            pltpu.VMEM((2, LATE, span, width), bf16),
            pltpu.VMEM((slots, heads, width), f32),
            pltpu.SemaphoreType.DMA((2, LATE)),
        ],
        compiler_params=params,
        cost_estimate=pl.CostEstimate(flops=flops, bytes_accessed=moved, transcendentals=LATE * heads * span),
        name="late",
    )(
        *late,
        *[near(x) for x in carried[1:]],
        near(weight),
        near(carried[0]),
        hbm(key_cache),
        hbm(value_cache),
    )
    if tp == 2:
        both = partial_two.astype(f32) + swap(partial_two).astype(f32)
        out_two = both.astype(bf16)
    else:
        out_two = lax.psum(partial_two, "tp")
    shape = (slots * pages, kv_heads, size, width)
    return (out_one, out_two, key_cache.reshape(shape), value_cache.reshape(shape))


def solution(mesh):
    sizes = dict(mesh.shape)
    return jax.shard_map(
        functools.partial(shards, sizes["inst"], sizes["tp"]),
        mesh=mesh,
        in_specs=(
            P("inst", "tp", None),
            P("inst", "tp", None),
            P("inst", "tp", None),
            P("inst", "tp", None, None),
            P("inst", "tp", None, None),
            P("inst", None),
            P("inst"),
            P("inst"),
            P("inst"),
            P("inst", "tp", None),
            P("inst", "tp", None),
            P("inst", "tp", None),
            P("tp", None),
        ),
        out_specs=(
            P("inst", None),
            P("inst", None),
            P("inst", "tp", None, None),
            P("inst", "tp", None, None),
        ),
        check_vma=False,
    )
```

```python
import functools

import jax
import jax.numpy as jnp
from jax import lax
from jax.experimental import pallas as pl
from jax.experimental.pallas import tpu as pltpu
from jax.sharding import PartitionSpec as P

NEG = -1e30
TILE = 16
SPLIT = 64
CHUNKS = 8
AHEAD = 5
LATE = 4
VMEM_BYTES = 24 * 1024 * 1024


def row_of(block, at):
    rows = lax.broadcasted_iota(jnp.int32, block.shape, 0)
    return jnp.sum(jnp.where(rows == at, block, 0.0), axis=0, keepdims=True)


def row_at(block, position):
    base = pl.multiple_of(position // TILE * TILE, TILE)
    return row_of(block[pl.ds(base, TILE), :].astype(jnp.float32), position % TILE)


def put_row(block, row, position):
    base = pl.multiple_of(position // TILE * TILE, TILE)
    part = block[pl.ds(base, TILE), :]
    at = lax.broadcasted_iota(jnp.int32, part.shape, 0)
    mixed = jnp.where(at == position % TILE, row, part.astype(jnp.float32))
    block[pl.ds(base, TILE), :] = mixed.astype(jnp.bfloat16)


def put_last(block, row):
    end = block.shape[0]
    part = block[end - TILE : end, :]
    at = lax.broadcasted_iota(jnp.int32, part.shape, 0)
    mixed = jnp.where(at == TILE - 1, row, part.astype(jnp.float32))
    block[end - TILE : end, :] = mixed.astype(jnp.bfloat16)


def last_row(block):
    end = block.shape[0]
    return block[end - TILE : end, :].astype(jnp.float32)[TILE - 1 : TILE, :]


def invert(dest, source, n):
    def note(r, carry):
        source[dest[r]] = r
        return carry

    lax.fori_loop(0, n, note, 0)


def begin(pairs, sem):
    copies = [pltpu.make_async_copy(a, b, sem.at[i]) for i, (a, b) in enumerate(pairs)]
    for copy in copies:
        copy.start()
    return copies


def finish(copies):
    for copy in copies:
        copy.wait()


def parcels_of(refs, span):
    return [(ref.at[pl.ds(0, span)], ref.at[pl.ds(span, span)]) for ref in refs]


def sources(source, steps):
    me = lax.axis_index("inst")
    return [source[me ^ s] for s in steps]


def pack_kernel(n, steps, pages, *refs):
    count = len(steps)
    far, outs = refs[:8], refs[8 : 8 + count]
    table, lengths, dest, slot, key_one, value_one, key_pool, value_pool, source, sems = refs[8 + count :]
    copies = begin(list(zip(far, (table, lengths, dest, slot, key_one, value_one, key_pool, value_pool))), sems)
    size = key_pool.shape[1]
    parcels = parcels_of(outs, pages * size)
    finish(copies[:6])
    invert(dest, source, n)
    at = sources(source, steps)
    tokens = (key_one[...].astype(jnp.float32), value_one[...].astype(jnp.float32))
    lanes = lax.broadcasted_iota(jnp.int32, (1, key_one.shape[1]), 1)
    for which, pool in ((0, key_pool), (1, value_pool)):
        copies[6 + which].wait()
        for r, parcel in zip(at, parcels):
            for p in range(pages):
                parcel[which][p * size : (p + 1) * size, :] = pool[table[p, r]]
            put_row(parcel[which], row_of(tokens[which], r), lengths[r])
            if which == 0:
                put_row(parcel[0], last_row(parcel[0]), lengths[r] + 1)
                note = jnp.where(lanes < SPLIT, slot[r], lengths[r]).astype(jnp.float32)
                put_last(parcel[0], note)


def attend(queries, keys, values, counts):
    width = queries[0].shape[1]
    scores = []
    for q, k, count in zip(queries, keys, counts):
        s = lax.dot_general(q, k, (((1,), (1,)), ((), ())), preferred_element_type=jnp.float32)
        live = lax.broadcasted_iota(jnp.int32, s.shape, 1) < count
        scores.append(jnp.where(live, s * width ** (-0.5), NEG))
    group = scores[0].shape[0]
    score = jnp.concatenate(scores, axis=0)
    top = jnp.max(score, axis=-1, keepdims=True)
    expo = jnp.exp(score - top)
    weights = (expo / jnp.sum(expo, axis=-1, keepdims=True)).astype(jnp.bfloat16)
    return [
        jnp.dot(weights[i * group : (i + 1) * group], v, preferred_element_type=jnp.float32)
        for i, v in enumerate(values)
    ]


def project(mixed, weight, out):
    heads = mixed.shape[1]
    rows = jnp.concatenate([mixed[:, h, :] for h in range(heads)], axis=1).astype(jnp.bfloat16)
    width = weight.shape[1] // CHUNKS
    for c in range(CHUNKS):
        part = jnp.dot(
            rows, weight[:, c * width : (c + 1) * width], preferred_element_type=jnp.float32
        )
        out[:, c * width : (c + 1) * width] = part.astype(jnp.bfloat16)


def first_kernel(steps, span, *refs):
    n = len(steps)
    far, parcels, out, weight = refs[:4], refs[4 : 4 + n], refs[4 + n], refs[5 + n]
    lengths, dest, query, source, mixed, sems = refs[6 + n :]
    copies = begin(list(zip(far, (lengths, dest, query, weight))), sems)
    parcels = parcels_of(parcels, span)
    finish(copies[:3])
    invert(dest, source, n)
    at = sources(source, steps)
    results = attend(
        [query[r] for r in at],
        [parcel[0][...] for parcel in parcels],
        [parcel[1][...] for parcel in parcels],
        [lengths[r] + 1 for r in at],
    )
    for r, result in zip(at, results):
        mixed[r] = result
    copies[3].wait()
    project(mixed, weight, out)


def place(arrived, query, key_two, value_two, key_cache, value_cache, held, mixed, osems):
    count = len(arrived)
    slots = []
    lengths = []
    for parcel in arrived:
        note = last_row(parcel[0])
        lanes = lax.broadcasted_iota(jnp.int32, note.shape, 1)
        slots.append(jnp.max(jnp.where(lanes < SPLIT, note, 0.0)).astype(jnp.int32))
        lengths.append(jnp.max(jnp.where(lanes < SPLIT, 0.0, note)).astype(jnp.int32))
    for i, parcel in enumerate(arrived):
        held[0, i] = parcel[0][...]
        held[1, i] = parcel[1][...]
        put_last(held.at[0, i], row_at(parcel[0], lengths[i] + 1))
    outgoing = []
    for i in range(count):
        for which, (token, cache) in enumerate(((key_two, key_cache), (value_two, value_cache))):
            put_row(held.at[which, i], token[pl.ds(slots[i], 1), :], lengths[i] + 1)
            copy = pltpu.make_async_copy(held.at[which, i], cache.at[slots[i]], osems.at[which, i])
            copy.start()
            outgoing.append(copy)
    results = attend(
        [query[j] for j in slots],
        [held[0, i] for i in range(count)],
        [held[1, i] for i in range(count)],
        [length + 2 for length in lengths],
    )
    for j, result in zip(slots, results):
        mixed[j] = result
    return outgoing


def early_kernel(count, span, *refs):
    arrived, far = refs[:count], refs[count : count + 3]
    key_cache, value_cache, mixed, query, new_k, new_v = refs[count + 3 : count + 9]
    key_two, value_two, held, sems, osems = refs[-5:]
    copies = begin(list(zip(far, (query, key_two, value_two))), sems)
    finish(copies)
    new_k[...] = key_two[...].astype(jnp.float32)
    new_v[...] = value_two[...].astype(jnp.float32)
    parcels = parcels_of(arrived, span)
    finish(place(parcels, query, new_k, new_v, key_cache, value_cache, held, mixed, osems))


def late_kernel(count, span, pair, *refs):
    arrived, (query, new_k, new_v, weight, before) = refs[:count], refs[count : count + 5]
    halves, (out, key_cache, value_cache) = refs[count + 7 : count + 7 + pair], refs[count + 7 + pair : count + 10 + pair]
    held, mixed, osems = refs[-3:]
    mixed[...] = before[...]
    parcels = parcels_of(arrived, span)
    outgoing = place(parcels, query, new_k, new_v, key_cache, value_cache, held, mixed, osems)
    if pair:
        both = halves[0][...].astype(jnp.float32) + halves[1][...].astype(jnp.float32)
        refs[count + 10 + pair][...] = both.astype(jnp.bfloat16)
    project(mixed, weight, out)
    finish(outgoing)


def swap(partial):
    return lax.ppermute(partial, "tp", [(0, 1), (1, 0)])


def near(x):
    return pltpu.with_memory_space_constraint(x, pltpu.VMEM)


def hbm(x):
    return pltpu.with_memory_space_constraint(x, pltpu.HBM)


def step_order(n):
    half = n // 2
    crossing = list(range(half, n))[::-1]
    staying = list(range(1, half))[::-1]
    order = []
    for kind in "cnccncnccncncnn":
        queue = crossing if kind == "c" else staying
        if queue:
            order.append(queue.pop(0))
    while crossing or staying:
        order += crossing[:1] + staying[:1]
        del crossing[:1], staying[:1]
    return order


def shards(
    n,
    tp,
    query_one,
    key_one,
    value_one,
    key_pages,
    value_pages,
    page_table,
    lengths,
    dest_instance,
    dest_slot,
    query_two,
    key_two,
    value_two,
    out_weight,
):
    slots, pages = page_table.shape
    pool, kv_heads, size, width = key_pages.shape
    heads = query_one.shape[1]
    depth, columns = out_weight.shape
    span = pages * size
    assert kv_heads == 1 and slots == n and n >= 16 and span <= 256
    key_pages = key_pages.reshape(pool, size, width)
    value_pages = value_pages.reshape(pool, size, width)
    key_one = key_one.reshape(slots, width)
    value_one = value_one.reshape(slots, width)
    key_two = key_two.reshape(slots, width)
    value_two = value_two.reshape(slots, width)

    vmem = pl.BlockSpec(memory_space=pltpu.VMEM)
    far = pl.BlockSpec(memory_space=pltpu.HBM)
    params = pltpu.CompilerParams(vmem_limit_bytes=VMEM_BYTES)
    bf16, f32, i32 = jnp.bfloat16, jnp.float32, jnp.int32
    rows = 2 * span
    order = step_order(n)
    steps = [0] + order

    def block(height):
        return jax.ShapeDtypeStruct((height, width), bf16)

    shapes = [block(rows)] * n

    def pack(chosen):
        return pl.pallas_call(
            functools.partial(pack_kernel, n, chosen, pages),
            out_shape=[jax.ShapeDtypeStruct((rows, width), bf16)] * len(chosen),
            in_specs=[far] * 8,
            out_specs=[vmem] * len(chosen),
            scratch_shapes=[
                pltpu.SMEM((pages, slots), i32),
                pltpu.SMEM((slots,), i32),
                pltpu.SMEM((slots,), i32),
                pltpu.SMEM((slots,), i32),
                pltpu.VMEM((slots, width), bf16),
                pltpu.VMEM((slots, width), bf16),
                pltpu.VMEM((pool, size, width), bf16),
                pltpu.VMEM((pool, size, width), bf16),
                pltpu.SMEM((n,), i32),
                pltpu.SemaphoreType.DMA((8,)),
            ],
            compiler_params=params,
            cost_estimate=pl.CostEstimate(
                flops=0, bytes_accessed=4 * len(chosen) * rows * width, transcendentals=0
            ),
            name="pack",
        )(
            hbm(page_table.T),
            hbm(lengths),
            hbm(dest_instance),
            hbm(dest_slot),
            hbm(key_one),
            hbm(value_one),
            hbm(key_pages),
            hbm(value_pages),
        )

    steps = step_order(n) + [0]
    packed = pack(steps[:AHEAD]) + pack(steps[AHEAD:])

    flops = 4 * slots * heads * span * width + 2 * slots * depth * columns
    moved = 2 * depth * columns + 4 * slots * span * width
    def send(i, *after):
        block = lax.optimization_barrier((packed[i], *after))[0] if after else packed[i]
        return lax.ppermute(block, "inst", [(d, d ^ steps[i]) for d in range(n)])

    arrived = [send(i) for i in range(AHEAD)]
    partial_one, weight = pl.pallas_call(
        functools.partial(first_kernel, steps, span),
        out_shape=[
            jax.ShapeDtypeStruct((slots, columns), bf16),
            jax.ShapeDtypeStruct((depth, columns), bf16),
        ],
        in_specs=[far] * 4 + [vmem] * len(shapes),
        out_specs=[vmem, vmem],
        scratch_shapes=[
            pltpu.SMEM((slots,), i32),
            pltpu.SMEM((slots,), i32),
            pltpu.VMEM((slots, heads, width), bf16),
            pltpu.SMEM((n,), i32),
            pltpu.VMEM((slots, heads, width), f32),
            pltpu.SemaphoreType.DMA((4,)),
        ],
        compiler_params=params,
        cost_estimate=pl.CostEstimate(flops=flops, bytes_accessed=moved, transcendentals=slots * heads * span),
        name="first",
    )(hbm(lengths), hbm(dest_instance), hbm(query_one), hbm(out_weight), *packed)

    arrived += [send(i, partial_one) for i in range(AHEAD, n - 1)]
    early, late = [packed[-1]] + arrived[:-LATE], arrived[-LATE:]
    halves = []
    if tp == 2:
        halves = [partial_one, swap(lax.optimization_barrier((partial_one, arrived[0]))[0])]

    cache = jax.ShapeDtypeStruct((slots, span, width), bf16)
    mixed = jax.ShapeDtypeStruct((slots, heads, width), f32)
    some = len(early)
    results = pl.pallas_call(
        functools.partial(early_kernel, some, span),
        out_shape=[cache, cache, mixed]
        + [jax.ShapeDtypeStruct((slots, heads, width), bf16)]
        + [jax.ShapeDtypeStruct((slots, width), f32)] * 2,
        in_specs=[vmem] * some + [far] * 3,
        out_specs=[far, far] + [vmem] * 4,
        scratch_shapes=[
            pltpu.VMEM((slots, width), bf16),
            pltpu.VMEM((slots, width), bf16),
            pltpu.VMEM((2, some, span, width), bf16),
            pltpu.SemaphoreType.DMA((3,)),
            pltpu.SemaphoreType.DMA((2, some)),
        ],
        compiler_params=params,
        cost_estimate=pl.CostEstimate(
            flops=4 * some * heads * span * width,
            bytes_accessed=8 * some * span * width,
            transcendentals=some * heads * span,
        ),
        name="early",
    )(*early, hbm(query_two), hbm(key_two), hbm(value_two))
    key_cache, value_cache, *carried = results

    partial_two, key_cache, value_cache, *sums = pl.pallas_call(
        functools.partial(late_kernel, LATE, span, len(halves)),
        out_shape=[jax.ShapeDtypeStruct((slots, columns), bf16), cache, cache]
        + [jax.ShapeDtypeStruct((slots, columns), bf16)] * (len(halves) // 2),
        in_specs=[vmem] * (len(late) + 5) + [far] * 2 + [vmem] * len(halves),
        out_specs=[vmem, far, far] + [vmem] * (len(halves) // 2),
        input_output_aliases={len(late) + 5: 1, len(late) + 6: 2},
        scratch_shapes=[
            pltpu.VMEM((2, LATE, span, width), bf16),
            pltpu.VMEM((slots, heads, width), f32),
            pltpu.SemaphoreType.DMA((2, LATE)),
        ],
        compiler_params=params,
        cost_estimate=pl.CostEstimate(flops=flops, bytes_accessed=moved, transcendentals=LATE * heads * span),
        name="late",
    )(
        *late,
        *[near(x) for x in carried[1:]],
        near(weight),
        near(carried[0]),
        hbm(key_cache),
        hbm(value_cache),
        *halves,
    )
    out_one = sums[0] if sums else lax.psum(partial_one, "tp")
    if tp == 2:
        both = partial_two.astype(f32) + swap(partial_two).astype(f32)
        out_two = both.astype(bf16)
    else:
        out_two = lax.psum(partial_two, "tp")
    shape = (slots * pages, kv_heads, size, width)
    return (out_one, out_two, key_cache.reshape(shape), value_cache.reshape(shape))


def solution(mesh):
    sizes = dict(mesh.shape)
    return jax.shard_map(
        functools.partial(shards, sizes["inst"], sizes["tp"]),
        mesh=mesh,
        in_specs=(
            P("inst", "tp", None),
            P("inst", "tp", None),
            P("inst", "tp", None),
            P("inst", "tp", None, None),
            P("inst", "tp", None, None),
            P("inst", None),
            P("inst"),
            P("inst"),
            P("inst"),
            P("inst", "tp", None),
            P("inst", "tp", None),
            P("inst", "tp", None),
            P("tp", None),
        ),
        out_specs=(
            P("inst", None),
            P("inst", None),
            P("inst", "tp", None, None),
            P("inst", "tp", None, None),
        ),
        check_vma=False,
    )
```

```python
import functools

import jax
import jax.numpy as jnp
from jax import lax
from jax.experimental import pallas as pl
from jax.experimental.pallas import tpu as pltpu
from jax.sharding import PartitionSpec as P

NEG = -1e30
TILE = 16
SPLIT = 64
CHUNKS = 8
AHEAD = 5
LATE = 5
VMEM_BYTES = 24 * 1024 * 1024


def row_of(block, at):
    rows = lax.broadcasted_iota(jnp.int32, block.shape, 0)
    return jnp.sum(jnp.where(rows == at, block, 0.0), axis=0, keepdims=True)


def row_at(block, position):
    base = pl.multiple_of(position // TILE * TILE, TILE)
    return row_of(block[pl.ds(base, TILE), :].astype(jnp.float32), position % TILE)


def put_row(block, row, position):
    base = pl.multiple_of(position // TILE * TILE, TILE)
    part = block[pl.ds(base, TILE), :]
    at = lax.broadcasted_iota(jnp.int32, part.shape, 0)
    mixed = jnp.where(at == position % TILE, row, part.astype(jnp.float32))
    block[pl.ds(base, TILE), :] = mixed.astype(jnp.bfloat16)


def put_last(block, row):
    end = block.shape[0]
    part = block[end - TILE : end, :]
    at = lax.broadcasted_iota(jnp.int32, part.shape, 0)
    mixed = jnp.where(at == TILE - 1, row, part.astype(jnp.float32))
    block[end - TILE : end, :] = mixed.astype(jnp.bfloat16)


def last_row(block):
    end = block.shape[0]
    return block[end - TILE : end, :].astype(jnp.float32)[TILE - 1 : TILE, :]


def invert(dest, source, n):
    def note(r, carry):
        source[dest[r]] = r
        return carry

    lax.fori_loop(0, n, note, 0)


def begin(pairs, sem):
    copies = [pltpu.make_async_copy(a, b, sem.at[i]) for i, (a, b) in enumerate(pairs)]
    for copy in copies:
        copy.start()
    return copies


def finish(copies):
    for copy in copies:
        copy.wait()


def parcels_of(refs, span):
    return [(ref.at[pl.ds(0, span)], ref.at[pl.ds(span, span)]) for ref in refs]


def sources(source, steps):
    me = lax.axis_index("inst")
    return [source[me ^ s] for s in steps]


def pack_kernel(n, steps, pages, *refs):
    count = len(steps)
    far, outs = refs[:8], refs[8 : 8 + count]
    table, lengths, dest, slot, key_one, value_one, key_pool, value_pool, source, sems = refs[8 + count :]
    copies = begin(list(zip(far, (table, lengths, dest, slot, key_one, value_one, key_pool, value_pool))), sems)
    size = key_pool.shape[1]
    parcels = parcels_of(outs, pages * size)
    finish(copies[:6])
    invert(dest, source, n)
    at = sources(source, steps)
    tokens = (key_one[...].astype(jnp.float32), value_one[...].astype(jnp.float32))
    lanes = lax.broadcasted_iota(jnp.int32, (1, key_one.shape[1]), 1)
    for which, pool in ((0, key_pool), (1, value_pool)):
        copies[6 + which].wait()
        for r, parcel in zip(at, parcels):
            for p in range(pages):
                parcel[which][p * size : (p + 1) * size, :] = pool[table[p, r]]
            put_row(parcel[which], row_of(tokens[which], r), lengths[r])
            if which == 0:
                put_row(parcel[0], last_row(parcel[0]), lengths[r] + 1)
                note = jnp.where(lanes < SPLIT, slot[r], lengths[r]).astype(jnp.float32)
                put_last(parcel[0], note)


def attend(queries, keys, values, counts):
    width = queries[0].shape[1]
    scores = []
    for q, k, count in zip(queries, keys, counts):
        s = lax.dot_general(q, k, (((1,), (1,)), ((), ())), preferred_element_type=jnp.float32)
        live = lax.broadcasted_iota(jnp.int32, s.shape, 1) < count
        scores.append(jnp.where(live, s * width ** (-0.5), NEG))
    group = scores[0].shape[0]
    score = jnp.concatenate(scores, axis=0)
    top = jnp.max(score, axis=-1, keepdims=True)
    expo = jnp.exp(score - top)
    weights = (expo / jnp.sum(expo, axis=-1, keepdims=True)).astype(jnp.bfloat16)
    return [
        jnp.dot(weights[i * group : (i + 1) * group], v, preferred_element_type=jnp.float32)
        for i, v in enumerate(values)
    ]


def project(mixed, weight, out):
    heads = mixed.shape[1]
    rows = jnp.concatenate([mixed[:, h, :] for h in range(heads)], axis=1).astype(jnp.bfloat16)
    width = weight.shape[1] // CHUNKS
    for c in range(CHUNKS):
        part = jnp.dot(
            rows, weight[:, c * width : (c + 1) * width], preferred_element_type=jnp.float32
        )
        out[:, c * width : (c + 1) * width] = part.astype(jnp.bfloat16)


def first_kernel(steps, span, *refs):
    n = len(steps)
    far, parcels, out, weight = refs[:4], refs[4 : 4 + n], refs[4 + n], refs[5 + n]
    lengths, dest, query, source, mixed, sems = refs[6 + n :]
    copies = begin(list(zip(far, (lengths, dest, query, weight))), sems)
    parcels = parcels_of(parcels, span)
    finish(copies[:3])
    invert(dest, source, n)
    at = sources(source, steps)
    results = attend(
        [query[r] for r in at],
        [parcel[0][...] for parcel in parcels],
        [parcel[1][...] for parcel in parcels],
        [lengths[r] + 1 for r in at],
    )
    for r, result in zip(at, results):
        mixed[r] = result
    copies[3].wait()
    project(mixed, weight, out)


def place(arrived, query, key_two, value_two, key_cache, value_cache, held, mixed, osems):
    count = len(arrived)
    slots = []
    lengths = []
    for parcel in arrived:
        note = last_row(parcel[0])
        lanes = lax.broadcasted_iota(jnp.int32, note.shape, 1)
        slots.append(jnp.max(jnp.where(lanes < SPLIT, note, 0.0)).astype(jnp.int32))
        lengths.append(jnp.max(jnp.where(lanes < SPLIT, 0.0, note)).astype(jnp.int32))
    for i, parcel in enumerate(arrived):
        held[0, i] = parcel[0][...]
        held[1, i] = parcel[1][...]
        put_last(held.at[0, i], row_at(parcel[0], lengths[i] + 1))
    outgoing = []
    for i in range(count):
        for which, (token, cache) in enumerate(((key_two, key_cache), (value_two, value_cache))):
            put_row(held.at[which, i], token[pl.ds(slots[i], 1), :], lengths[i] + 1)
            copy = pltpu.make_async_copy(held.at[which, i], cache.at[slots[i]], osems.at[which, i])
            copy.start()
            outgoing.append(copy)
    results = attend(
        [query[j] for j in slots],
        [held[0, i] for i in range(count)],
        [held[1, i] for i in range(count)],
        [length + 2 for length in lengths],
    )
    for j, result in zip(slots, results):
        mixed[j] = result
    return outgoing


def early_kernel(count, span, *refs):
    arrived, far = refs[:count], refs[count : count + 3]
    key_cache, value_cache, mixed, query, new_k, new_v = refs[count + 3 : count + 9]
    key_two, value_two, held, sems, osems = refs[-5:]
    copies = begin(list(zip(far, (query, key_two, value_two))), sems)
    finish(copies)
    new_k[...] = key_two[...].astype(jnp.float32)
    new_v[...] = value_two[...].astype(jnp.float32)
    parcels = parcels_of(arrived, span)
    finish(place(parcels, query, new_k, new_v, key_cache, value_cache, held, mixed, osems))


def late_kernel(count, span, *refs):
    arrived, (query, new_k, new_v, weight, before) = refs[:count], refs[count : count + 5]
    out, key_cache, value_cache, held, mixed, osems = refs[count + 7 :]
    mixed[...] = before[...]
    parcels = parcels_of(arrived, span)
    outgoing = place(parcels, query, new_k, new_v, key_cache, value_cache, held, mixed, osems)
    project(mixed, weight, out)
    finish(outgoing)


def total(partial, size):
    if size == 2:
        other = lax.ppermute(partial, "tp", [(0, 1), (1, 0)])
        return (partial.astype(jnp.float32) + other.astype(jnp.float32)).astype(jnp.bfloat16)
    return lax.psum(partial, "tp")


def near(x):
    return pltpu.with_memory_space_constraint(x, pltpu.VMEM)


def hbm(x):
    return pltpu.with_memory_space_constraint(x, pltpu.HBM)


def step_order(n):
    half = n // 2
    crossing = [half] + list(range(half + 1, n))[::-1]
    staying = list(range(1, half))[::-1]
    order = []
    for kind in "cnccncnccncncnn":
        queue = crossing if kind == "c" else staying
        if queue:
            order.append(queue.pop(0))
    while crossing or staying:
        order += crossing[:1] + staying[:1]
        del crossing[:1], staying[:1]
    return order


def shards(
    n,
    tp,
    query_one,
    key_one,
    value_one,
    key_pages,
    value_pages,
    page_table,
    lengths,
    dest_instance,
    dest_slot,
    query_two,
    key_two,
    value_two,
    out_weight,
):
    slots, pages = page_table.shape
    pool, kv_heads, size, width = key_pages.shape
    heads = query_one.shape[1]
    depth, columns = out_weight.shape
    span = pages * size
    assert kv_heads == 1 and slots == n and n >= 16 and span <= 256
    key_pages = key_pages.reshape(pool, size, width)
    value_pages = value_pages.reshape(pool, size, width)
    key_one = key_one.reshape(slots, width)
    value_one = value_one.reshape(slots, width)
    key_two = key_two.reshape(slots, width)
    value_two = value_two.reshape(slots, width)

    vmem = pl.BlockSpec(memory_space=pltpu.VMEM)
    far = pl.BlockSpec(memory_space=pltpu.HBM)
    params = pltpu.CompilerParams(vmem_limit_bytes=VMEM_BYTES)
    bf16, f32, i32 = jnp.bfloat16, jnp.float32, jnp.int32
    rows = 2 * span
    order = step_order(n)
    steps = [0] + order

    def block(height):
        return jax.ShapeDtypeStruct((height, width), bf16)

    shapes = [block(rows)] * n

    def pack(chosen):
        return pl.pallas_call(
            functools.partial(pack_kernel, n, chosen, pages),
            out_shape=[jax.ShapeDtypeStruct((rows, width), bf16)] * len(chosen),
            in_specs=[far] * 8,
            out_specs=[vmem] * len(chosen),
            scratch_shapes=[
                pltpu.SMEM((pages, slots), i32),
                pltpu.SMEM((slots,), i32),
                pltpu.SMEM((slots,), i32),
                pltpu.SMEM((slots,), i32),
                pltpu.VMEM((slots, width), bf16),
                pltpu.VMEM((slots, width), bf16),
                pltpu.VMEM((pool, size, width), bf16),
                pltpu.VMEM((pool, size, width), bf16),
                pltpu.SMEM((n,), i32),
                pltpu.SemaphoreType.DMA((8,)),
            ],
            compiler_params=params,
            cost_estimate=pl.CostEstimate(
                flops=0, bytes_accessed=4 * len(chosen) * rows * width, transcendentals=0
            ),
            name="pack",
        )(
            hbm(page_table.T),
            hbm(lengths),
            hbm(dest_instance),
            hbm(dest_slot),
            hbm(key_one),
            hbm(value_one),
            hbm(key_pages),
            hbm(value_pages),
        )

    steps = step_order(n) + [0]
    packed = pack(steps[:AHEAD]) + pack(steps[AHEAD:])

    flops = 4 * slots * heads * span * width + 2 * slots * depth * columns
    moved = 2 * depth * columns + 4 * slots * span * width
    def send(i, *after):
        block = lax.optimization_barrier((packed[i], *after))[0] if after else packed[i]
        return lax.ppermute(block, "inst", [(d, d ^ steps[i]) for d in range(n)])

    arrived = [send(i) for i in range(AHEAD)]
    partial_one, weight = pl.pallas_call(
        functools.partial(first_kernel, steps, span),
        out_shape=[
            jax.ShapeDtypeStruct((slots, columns), bf16),
            jax.ShapeDtypeStruct((depth, columns), bf16),
        ],
        in_specs=[far] * 4 + [vmem] * len(shapes),
        out_specs=[vmem, vmem],
        scratch_shapes=[
            pltpu.SMEM((slots,), i32),
            pltpu.SMEM((slots,), i32),
            pltpu.VMEM((slots, heads, width), bf16),
            pltpu.SMEM((n,), i32),
            pltpu.VMEM((slots, heads, width), f32),
            pltpu.SemaphoreType.DMA((4,)),
        ],
        compiler_params=params,
        cost_estimate=pl.CostEstimate(flops=flops, bytes_accessed=moved, transcendentals=slots * heads * span),
        name="first",
    )(hbm(lengths), hbm(dest_instance), hbm(query_one), hbm(out_weight), *packed)

    arrived += [send(i, partial_one) for i in range(AHEAD, n - 1)]
    early, late = [packed[-1]] + arrived[:-LATE], arrived[-LATE:]
    cache = jax.ShapeDtypeStruct((slots, span, width), bf16)
    mixed = jax.ShapeDtypeStruct((slots, heads, width), f32)
    some = len(early)
    results = pl.pallas_call(
        functools.partial(early_kernel, some, span),
        out_shape=[cache, cache, mixed]
        + [jax.ShapeDtypeStruct((slots, heads, width), bf16)]
        + [jax.ShapeDtypeStruct((slots, width), f32)] * 2,
        in_specs=[vmem] * some + [far] * 3,
        out_specs=[far, far] + [vmem] * 4,
        scratch_shapes=[
            pltpu.VMEM((slots, width), bf16),
            pltpu.VMEM((slots, width), bf16),
            pltpu.VMEM((2, some, span, width), bf16),
            pltpu.SemaphoreType.DMA((3,)),
            pltpu.SemaphoreType.DMA((2, some)),
        ],
        compiler_params=params,
        cost_estimate=pl.CostEstimate(
            flops=4 * some * heads * span * width,
            bytes_accessed=8 * some * span * width,
            transcendentals=some * heads * span,
        ),
        name="early",
    )(*early, hbm(query_two), hbm(key_two), hbm(value_two))
    key_cache, value_cache, *carried = results
    partial_one = lax.optimization_barrier((partial_one, carried[0]))[0]
    out_one = total(partial_one, tp)

    partial_two, key_cache, value_cache = pl.pallas_call(
        functools.partial(late_kernel, LATE, span),
        out_shape=[jax.ShapeDtypeStruct((slots, columns), bf16), cache, cache],
        in_specs=[vmem] * (len(late) + 5) + [far] * 2,
        out_specs=[vmem, far, far],
        input_output_aliases={len(late) + 5: 1, len(late) + 6: 2},
        scratch_shapes=[
            pltpu.VMEM((2, LATE, span, width), bf16),
            pltpu.VMEM((slots, heads, width), f32),
            pltpu.SemaphoreType.DMA((2, LATE)),
        ],
        compiler_params=params,
        cost_estimate=pl.CostEstimate(flops=flops, bytes_accessed=moved, transcendentals=LATE * heads * span),
        name="late",
    )(
        *late,
        *[near(x) for x in carried[1:]],
        near(weight),
        near(carried[0]),
        hbm(key_cache),
        hbm(value_cache),
    )
    out_two = total(partial_two, tp)
    shape = (slots * pages, kv_heads, size, width)
    return (out_one, out_two, key_cache.reshape(shape), value_cache.reshape(shape))


def solution(mesh):
    sizes = dict(mesh.shape)
    return jax.shard_map(
        functools.partial(shards, sizes["inst"], sizes["tp"]),
        mesh=mesh,
        in_specs=(
            P("inst", "tp", None),
            P("inst", "tp", None),
            P("inst", "tp", None),
            P("inst", "tp", None, None),
            P("inst", "tp", None, None),
            P("inst", None),
            P("inst"),
            P("inst"),
            P("inst"),
            P("inst", "tp", None),
            P("inst", "tp", None),
            P("inst", "tp", None),
            P("tp", None),
        ),
        out_specs=(
            P("inst", None),
            P("inst", None),
            P("inst", "tp", None, None),
            P("inst", "tp", None, None),
        ),
        check_vma=False,
    )
```

```python
import functools

import jax
import jax.numpy as jnp
from jax import lax
from jax.experimental import pallas as pl
from jax.experimental.pallas import tpu as pltpu
from jax.sharding import PartitionSpec as P

NEG = -1e30
TILE = 16
SPLIT = 64
CHUNKS = 8
AHEAD = 5
LATE = 5
VMEM_BYTES = 24 * 1024 * 1024


def row_of(block, at):
    rows = lax.broadcasted_iota(jnp.int32, block.shape, 0)
    return jnp.sum(jnp.where(rows == at, block, 0.0), axis=0, keepdims=True)


def row_at(block, position):
    base = pl.multiple_of(position // TILE * TILE, TILE)
    return row_of(block[pl.ds(base, TILE), :].astype(jnp.float32), position % TILE)


def put_row(block, row, position):
    base = pl.multiple_of(position // TILE * TILE, TILE)
    part = block[pl.ds(base, TILE), :]
    at = lax.broadcasted_iota(jnp.int32, part.shape, 0)
    mixed = jnp.where(at == position % TILE, row, part.astype(jnp.float32))
    block[pl.ds(base, TILE), :] = mixed.astype(jnp.bfloat16)


def put_last(block, row):
    end = block.shape[0]
    part = block[end - TILE : end, :]
    at = lax.broadcasted_iota(jnp.int32, part.shape, 0)
    mixed = jnp.where(at == TILE - 1, row, part.astype(jnp.float32))
    block[end - TILE : end, :] = mixed.astype(jnp.bfloat16)


def last_row(block):
    end = block.shape[0]
    return block[end - TILE : end, :].astype(jnp.float32)[TILE - 1 : TILE, :]


def invert(dest, source, n):
    def note(r, carry):
        source[dest[r]] = r
        return carry

    lax.fori_loop(0, n, note, 0)


def begin(pairs, sem):
    copies = [pltpu.make_async_copy(a, b, sem.at[i]) for i, (a, b) in enumerate(pairs)]
    for copy in copies:
        copy.start()
    return copies


def finish(copies):
    for copy in copies:
        copy.wait()


def parcels_of(refs, span):
    return [(ref.at[pl.ds(0, span)], ref.at[pl.ds(span, span)]) for ref in refs]


def sources(source, steps):
    me = lax.axis_index("inst")
    return [source[me ^ s] for s in steps]


def pack_kernel(n, steps, pages, *refs):
    count = len(steps)
    far, outs = refs[:8], refs[8 : 8 + count]
    table, lengths, dest, slot, key_one, value_one, key_pool, value_pool, source, sems = refs[8 + count :]
    copies = begin(list(zip(far, (table, lengths, dest, slot, key_one, value_one, key_pool, value_pool))), sems)
    size = key_pool.shape[1]
    parcels = parcels_of(outs, pages * size)
    finish(copies[:6])
    invert(dest, source, n)
    at = sources(source, steps)
    tokens = (key_one[...].astype(jnp.float32), value_one[...].astype(jnp.float32))
    lanes = lax.broadcasted_iota(jnp.int32, (1, key_one.shape[1]), 1)
    for which, pool in ((0, key_pool), (1, value_pool)):
        copies[6 + which].wait()
        for r, parcel in zip(at, parcels):
            for p in range(pages):
                parcel[which][p * size : (p + 1) * size, :] = pool[table[p, r]]
            put_row(parcel[which], row_of(tokens[which], r), lengths[r])
            if which == 0:
                put_row(parcel[0], last_row(parcel[0]), lengths[r] + 1)
                note = jnp.where(lanes < SPLIT, slot[r], lengths[r]).astype(jnp.float32)
                put_last(parcel[0], note)


def attend(queries, keys, values, counts):
    width = queries[0].shape[1]
    scores = []
    for q, k, count in zip(queries, keys, counts):
        s = lax.dot_general(q, k, (((1,), (1,)), ((), ())), preferred_element_type=jnp.float32)
        live = lax.broadcasted_iota(jnp.int32, s.shape, 1) < count
        scores.append(jnp.where(live, s * width ** (-0.5), NEG))
    group = scores[0].shape[0]
    score = jnp.concatenate(scores, axis=0)
    top = jnp.max(score, axis=-1, keepdims=True)
    expo = jnp.exp(score - top)
    weights = (expo / jnp.sum(expo, axis=-1, keepdims=True)).astype(jnp.bfloat16)
    return [
        jnp.dot(weights[i * group : (i + 1) * group], v, preferred_element_type=jnp.float32)
        for i, v in enumerate(values)
    ]


def project(mixed, weight, out):
    heads = mixed.shape[1]
    rows = jnp.concatenate([mixed[:, h, :] for h in range(heads)], axis=1).astype(jnp.bfloat16)
    width = weight.shape[1] // CHUNKS
    for c in range(CHUNKS):
        part = jnp.dot(
            rows, weight[:, c * width : (c + 1) * width], preferred_element_type=jnp.float32
        )
        out[:, c * width : (c + 1) * width] = part.astype(jnp.bfloat16)


def first_kernel(steps, span, *refs):
    n = len(steps)
    far, parcels, out, weight = refs[:4], refs[4 : 4 + n], refs[4 + n], refs[5 + n]
    lengths, dest, query, source, mixed, sems = refs[6 + n :]
    copies = begin(list(zip(far, (lengths, dest, query, weight))), sems)
    parcels = parcels_of(parcels, span)
    finish(copies[:3])
    invert(dest, source, n)
    at = sources(source, steps)
    results = attend(
        [query[r] for r in at],
        [parcel[0][...] for parcel in parcels],
        [parcel[1][...] for parcel in parcels],
        [lengths[r] + 1 for r in at],
    )
    for r, result in zip(at, results):
        mixed[r] = result
    copies[3].wait()
    project(mixed, weight, out)


def place(arrived, query, key_two, value_two, key_cache, value_cache, held, mixed, osems):
    count = len(arrived)
    slots = []
    lengths = []
    for parcel in arrived:
        note = last_row(parcel[0])
        lanes = lax.broadcasted_iota(jnp.int32, note.shape, 1)
        slots.append(jnp.max(jnp.where(lanes < SPLIT, note, 0.0)).astype(jnp.int32))
        lengths.append(jnp.max(jnp.where(lanes < SPLIT, 0.0, note)).astype(jnp.int32))
    for i, parcel in enumerate(arrived):
        held[0, i] = parcel[0][...]
        held[1, i] = parcel[1][...]
        put_last(held.at[0, i], row_at(parcel[0], lengths[i] + 1))
    outgoing = []
    for i in range(count):
        for which, (token, cache) in enumerate(((key_two, key_cache), (value_two, value_cache))):
            put_row(held.at[which, i], token[pl.ds(slots[i], 1), :], lengths[i] + 1)
            copy = pltpu.make_async_copy(held.at[which, i], cache.at[slots[i]], osems.at[which, i])
            copy.start()
            outgoing.append(copy)
    results = attend(
        [query[j] for j in slots],
        [held[0, i] for i in range(count)],
        [held[1, i] for i in range(count)],
        [length + 2 for length in lengths],
    )
    for j, result in zip(slots, results):
        mixed[j] = result
    return outgoing


def early_kernel(count, span, *refs):
    arrived, far = refs[:count], refs[count : count + 3]
    key_cache, value_cache, mixed, query, new_k, new_v = refs[count + 3 : count + 9]
    key_two, value_two, held, sems, osems = refs[-5:]
    copies = begin(list(zip(far, (query, key_two, value_two))), sems)
    finish(copies)
    new_k[...] = key_two[...].astype(jnp.float32)
    new_v[...] = value_two[...].astype(jnp.float32)
    parcels = parcels_of(arrived, span)
    finish(place(parcels, query, new_k, new_v, key_cache, value_cache, held, mixed, osems))


def late_kernel(count, span, *refs):
    arrived, (query, new_k, new_v, weight, before) = refs[:count], refs[count : count + 5]
    out, key_cache, value_cache, held, mixed, osems = refs[count + 7 :]
    mixed[...] = before[...]
    parcels = parcels_of(arrived, span)
    outgoing = place(parcels, query, new_k, new_v, key_cache, value_cache, held, mixed, osems)
    project(mixed, weight, out)
    finish(outgoing)


def total(partial, size):
    if size == 2:
        other = lax.ppermute(partial, "tp", [(0, 1), (1, 0)])
        return (partial.astype(jnp.float32) + other.astype(jnp.float32)).astype(jnp.bfloat16)
    return lax.psum(partial, "tp")


def near(x):
    return pltpu.with_memory_space_constraint(x, pltpu.VMEM)


def hbm(x):
    return pltpu.with_memory_space_constraint(x, pltpu.HBM)


def step_order(n):
    half = n // 2
    crossing = [half] + list(range(half + 1, n))[::-1]
    staying = list(range(1, half))[::-1]
    order = []
    for kind in "cncncncncncncnc":
        queue = crossing if kind == "c" else staying
        if queue:
            order.append(queue.pop(0))
    while crossing or staying:
        order += crossing[:1] + staying[:1]
        del crossing[:1], staying[:1]
    return order


def shards(
    n,
    tp,
    query_one,
    key_one,
    value_one,
    key_pages,
    value_pages,
    page_table,
    lengths,
    dest_instance,
    dest_slot,
    query_two,
    key_two,
    value_two,
    out_weight,
):
    slots, pages = page_table.shape
    pool, kv_heads, size, width = key_pages.shape
    heads = query_one.shape[1]
    depth, columns = out_weight.shape
    span = pages * size
    assert kv_heads == 1 and slots == n and n >= 16 and span <= 256
    key_pages = key_pages.reshape(pool, size, width)
    value_pages = value_pages.reshape(pool, size, width)
    key_one = key_one.reshape(slots, width)
    value_one = value_one.reshape(slots, width)
    key_two = key_two.reshape(slots, width)
    value_two = value_two.reshape(slots, width)

    vmem = pl.BlockSpec(memory_space=pltpu.VMEM)
    far = pl.BlockSpec(memory_space=pltpu.HBM)
    params = pltpu.CompilerParams(vmem_limit_bytes=VMEM_BYTES)
    bf16, f32, i32 = jnp.bfloat16, jnp.float32, jnp.int32
    rows = 2 * span
    order = step_order(n)
    steps = [0] + order

    def block(height):
        return jax.ShapeDtypeStruct((height, width), bf16)

    shapes = [block(rows)] * n

    def pack(chosen):
        return pl.pallas_call(
            functools.partial(pack_kernel, n, chosen, pages),
            out_shape=[jax.ShapeDtypeStruct((rows, width), bf16)] * len(chosen),
            in_specs=[far] * 8,
            out_specs=[vmem] * len(chosen),
            scratch_shapes=[
                pltpu.SMEM((pages, slots), i32),
                pltpu.SMEM((slots,), i32),
                pltpu.SMEM((slots,), i32),
                pltpu.SMEM((slots,), i32),
                pltpu.VMEM((slots, width), bf16),
                pltpu.VMEM((slots, width), bf16),
                pltpu.VMEM((pool, size, width), bf16),
                pltpu.VMEM((pool, size, width), bf16),
                pltpu.SMEM((n,), i32),
                pltpu.SemaphoreType.DMA((8,)),
            ],
            compiler_params=params,
            cost_estimate=pl.CostEstimate(
                flops=0, bytes_accessed=4 * len(chosen) * rows * width, transcendentals=0
            ),
            name="pack",
        )(
            hbm(page_table.T),
            hbm(lengths),
            hbm(dest_instance),
            hbm(dest_slot),
            hbm(key_one),
            hbm(value_one),
            hbm(key_pages),
            hbm(value_pages),
        )

    steps = step_order(n) + [0]
    packed = pack(steps[:AHEAD]) + pack(steps[AHEAD:])

    flops = 4 * slots * heads * span * width + 2 * slots * depth * columns
    moved = 2 * depth * columns + 4 * slots * span * width
    def send(i, *after):
        block = lax.optimization_barrier((packed[i], *after))[0] if after else packed[i]
        return lax.ppermute(block, "inst", [(d, d ^ steps[i]) for d in range(n)])

    arrived = [send(i) for i in range(AHEAD)]
    partial_one, weight = pl.pallas_call(
        functools.partial(first_kernel, steps, span),
        out_shape=[
            jax.ShapeDtypeStruct((slots, columns), bf16),
            jax.ShapeDtypeStruct((depth, columns), bf16),
        ],
        in_specs=[far] * 4 + [vmem] * len(shapes),
        out_specs=[vmem, vmem],
        scratch_shapes=[
            pltpu.SMEM((slots,), i32),
            pltpu.SMEM((slots,), i32),
            pltpu.VMEM((slots, heads, width), bf16),
            pltpu.SMEM((n,), i32),
            pltpu.VMEM((slots, heads, width), f32),
            pltpu.SemaphoreType.DMA((4,)),
        ],
        compiler_params=params,
        cost_estimate=pl.CostEstimate(flops=flops, bytes_accessed=moved, transcendentals=slots * heads * span),
        name="first",
    )(hbm(lengths), hbm(dest_instance), hbm(query_one), hbm(out_weight), *packed)

    arrived += [send(i, partial_one) for i in range(AHEAD, n - 1)]
    early, late = [packed[-1]] + arrived[:-LATE], arrived[-LATE:]
    cache = jax.ShapeDtypeStruct((slots, span, width), bf16)
    mixed = jax.ShapeDtypeStruct((slots, heads, width), f32)
    some = len(early)
    results = pl.pallas_call(
        functools.partial(early_kernel, some, span),
        out_shape=[cache, cache, mixed]
        + [jax.ShapeDtypeStruct((slots, heads, width), bf16)]
        + [jax.ShapeDtypeStruct((slots, width), f32)] * 2,
        in_specs=[vmem] * some + [far] * 3,
        out_specs=[far, far] + [vmem] * 4,
        scratch_shapes=[
            pltpu.VMEM((slots, width), bf16),
            pltpu.VMEM((slots, width), bf16),
            pltpu.VMEM((2, some, span, width), bf16),
            pltpu.SemaphoreType.DMA((3,)),
            pltpu.SemaphoreType.DMA((2, some)),
        ],
        compiler_params=params,
        cost_estimate=pl.CostEstimate(
            flops=4 * some * heads * span * width,
            bytes_accessed=8 * some * span * width,
            transcendentals=some * heads * span,
        ),
        name="early",
    )(*early, hbm(query_two), hbm(key_two), hbm(value_two))
    key_cache, value_cache, *carried = results
    partial_one = lax.optimization_barrier((partial_one, carried[0]))[0]
    out_one = total(partial_one, tp)

    partial_two, key_cache, value_cache = pl.pallas_call(
        functools.partial(late_kernel, LATE, span),
        out_shape=[jax.ShapeDtypeStruct((slots, columns), bf16), cache, cache],
        in_specs=[vmem] * (len(late) + 5) + [far] * 2,
        out_specs=[vmem, far, far],
        input_output_aliases={len(late) + 5: 1, len(late) + 6: 2},
        scratch_shapes=[
            pltpu.VMEM((2, LATE, span, width), bf16),
            pltpu.VMEM((slots, heads, width), f32),
            pltpu.SemaphoreType.DMA((2, LATE)),
        ],
        compiler_params=params,
        cost_estimate=pl.CostEstimate(flops=flops, bytes_accessed=moved, transcendentals=LATE * heads * span),
        name="late",
    )(
        *late,
        *[near(x) for x in carried[1:]],
        near(weight),
        near(carried[0]),
        hbm(key_cache),
        hbm(value_cache),
    )
    out_two = total(partial_two, tp)
    shape = (slots * pages, kv_heads, size, width)
    return (out_one, out_two, key_cache.reshape(shape), value_cache.reshape(shape))


def solution(mesh):
    sizes = dict(mesh.shape)
    return jax.shard_map(
        functools.partial(shards, sizes["inst"], sizes["tp"]),
        mesh=mesh,
        in_specs=(
            P("inst", "tp", None),
            P("inst", "tp", None),
            P("inst", "tp", None),
            P("inst", "tp", None, None),
            P("inst", "tp", None, None),
            P("inst", None),
            P("inst"),
            P("inst"),
            P("inst"),
            P("inst", "tp", None),
            P("inst", "tp", None),
            P("inst", "tp", None),
            P("tp", None),
        ),
        out_specs=(
            P("inst", None),
            P("inst", None),
            P("inst", "tp", None, None),
            P("inst", "tp", None, None),
        ),
        check_vma=False,
    )
```

```python
import functools

import jax
import jax.numpy as jnp
from jax import lax
from jax.experimental import pallas as pl
from jax.experimental.pallas import tpu as pltpu
from jax.sharding import PartitionSpec as P

NEG = -1e30
TILE = 16
SPLIT = 64
CHUNKS = 8
AHEAD = 5
LATE = 5
VMEM_BYTES = 24 * 1024 * 1024


def row_of(block, at):
    rows = lax.broadcasted_iota(jnp.int32, block.shape, 0)
    return jnp.sum(jnp.where(rows == at, block, 0.0), axis=0, keepdims=True)


def row_at(block, position):
    base = pl.multiple_of(position // TILE * TILE, TILE)
    return row_of(block[pl.ds(base, TILE), :].astype(jnp.float32), position % TILE)


def put_row(block, row, position):
    base = pl.multiple_of(position // TILE * TILE, TILE)
    part = block[pl.ds(base, TILE), :]
    at = lax.broadcasted_iota(jnp.int32, part.shape, 0)
    mixed = jnp.where(at == position % TILE, row, part.astype(jnp.float32))
    block[pl.ds(base, TILE), :] = mixed.astype(jnp.bfloat16)


def put_last(block, row):
    end = block.shape[0]
    part = block[end - TILE : end, :]
    at = lax.broadcasted_iota(jnp.int32, part.shape, 0)
    mixed = jnp.where(at == TILE - 1, row, part.astype(jnp.float32))
    block[end - TILE : end, :] = mixed.astype(jnp.bfloat16)


def last_row(block):
    end = block.shape[0]
    return block[end - TILE : end, :].astype(jnp.float32)[TILE - 1 : TILE, :]


def invert(dest, source, n):
    def note(r, carry):
        source[dest[r]] = r
        return carry

    lax.fori_loop(0, n, note, 0)


def begin(pairs, sem):
    copies = [pltpu.make_async_copy(a, b, sem.at[i]) for i, (a, b) in enumerate(pairs)]
    for copy in copies:
        copy.start()
    return copies


def finish(copies):
    for copy in copies:
        copy.wait()


def parcels_of(refs, span):
    return [(ref.at[pl.ds(0, span)], ref.at[pl.ds(span, span)]) for ref in refs]


def sources(source, steps):
    me = lax.axis_index("inst")
    return [source[me ^ s] for s in steps]


def pack_kernel(n, steps, pages, *refs):
    count = len(steps)
    far, outs = refs[:8], refs[8 : 8 + count]
    table, lengths, dest, slot, key_one, value_one, key_pool, value_pool, source, sems = refs[8 + count :]
    copies = begin(list(zip(far, (table, lengths, dest, slot, key_one, value_one, key_pool, value_pool))), sems)
    size = key_pool.shape[1]
    parcels = parcels_of(outs, pages * size)
    finish(copies[:6])
    invert(dest, source, n)
    at = sources(source, steps)
    tokens = (key_one[...].astype(jnp.float32), value_one[...].astype(jnp.float32))
    lanes = lax.broadcasted_iota(jnp.int32, (1, key_one.shape[1]), 1)
    for which, pool in ((0, key_pool), (1, value_pool)):
        copies[6 + which].wait()
        for r, parcel in zip(at, parcels):
            for p in range(pages):
                parcel[which][p * size : (p + 1) * size, :] = pool[table[p, r]]
            put_row(parcel[which], row_of(tokens[which], r), lengths[r])
            if which == 0:
                put_row(parcel[0], last_row(parcel[0]), lengths[r] + 1)
                note = jnp.where(lanes < SPLIT, slot[r], lengths[r]).astype(jnp.float32)
                put_last(parcel[0], note)


def attend(queries, keys, values, counts):
    width = queries[0].shape[1]
    scores = []
    for q, k, count in zip(queries, keys, counts):
        s = lax.dot_general(q, k, (((1,), (1,)), ((), ())), preferred_element_type=jnp.float32)
        live = lax.broadcasted_iota(jnp.int32, s.shape, 1) < count
        scores.append(jnp.where(live, s * width ** (-0.5), NEG))
    group = scores[0].shape[0]
    score = jnp.concatenate(scores, axis=0)
    top = jnp.max(score, axis=-1, keepdims=True)
    expo = jnp.exp(score - top)
    weights = (expo / jnp.sum(expo, axis=-1, keepdims=True)).astype(jnp.bfloat16)
    return [
        jnp.dot(weights[i * group : (i + 1) * group], v, preferred_element_type=jnp.float32)
        for i, v in enumerate(values)
    ]


def project(mixed, weight, out):
    heads = mixed.shape[1]
    rows = jnp.concatenate([mixed[:, h, :] for h in range(heads)], axis=1).astype(jnp.bfloat16)
    width = weight.shape[1] // CHUNKS
    for c in range(CHUNKS):
        part = jnp.dot(
            rows, weight[:, c * width : (c + 1) * width], preferred_element_type=jnp.float32
        )
        out[:, c * width : (c + 1) * width] = part.astype(jnp.bfloat16)


def first_kernel(steps, span, *refs):
    n = len(steps)
    far, parcels, out, weight = refs[:4], refs[4 : 4 + n], refs[4 + n], refs[5 + n]
    lengths, dest, query, source, mixed, sems = refs[6 + n :]
    copies = begin(list(zip(far, (lengths, dest, query, weight))), sems)
    parcels = parcels_of(parcels, span)
    finish(copies[:3])
    invert(dest, source, n)
    at = sources(source, steps)
    results = attend(
        [query[r] for r in at],
        [parcel[0][...] for parcel in parcels],
        [parcel[1][...] for parcel in parcels],
        [lengths[r] + 1 for r in at],
    )
    for r, result in zip(at, results):
        mixed[r] = result
    copies[3].wait()
    project(mixed, weight, out)


def place(arrived, query, key_two, value_two, key_cache, value_cache, held, mixed, osems):
    count = len(arrived)
    slots = []
    lengths = []
    for parcel in arrived:
        note = last_row(parcel[0])
        lanes = lax.broadcasted_iota(jnp.int32, note.shape, 1)
        slots.append(jnp.max(jnp.where(lanes < SPLIT, note, 0.0)).astype(jnp.int32))
        lengths.append(jnp.max(jnp.where(lanes < SPLIT, 0.0, note)).astype(jnp.int32))
    for i, parcel in enumerate(arrived):
        held[0, i] = parcel[0][...]
        held[1, i] = parcel[1][...]
        put_last(held.at[0, i], row_at(parcel[0], lengths[i] + 1))
    outgoing = []
    for i in range(count):
        for which, (token, cache) in enumerate(((key_two, key_cache), (value_two, value_cache))):
            put_row(held.at[which, i], token[pl.ds(slots[i], 1), :], lengths[i] + 1)
            copy = pltpu.make_async_copy(held.at[which, i], cache.at[slots[i]], osems.at[which, i])
            copy.start()
            outgoing.append(copy)
    results = attend(
        [query[j] for j in slots],
        [held[0, i] for i in range(count)],
        [held[1, i] for i in range(count)],
        [length + 2 for length in lengths],
    )
    for j, result in zip(slots, results):
        mixed[j] = result
    return outgoing


def early_kernel(count, span, *refs):
    arrived, far = refs[:count], refs[count : count + 3]
    key_cache, value_cache, mixed, query, new_k, new_v = refs[count + 3 : count + 9]
    key_two, value_two, held, sems, osems = refs[-5:]
    copies = begin(list(zip(far, (query, key_two, value_two))), sems)
    finish(copies)
    new_k[...] = key_two[...].astype(jnp.float32)
    new_v[...] = value_two[...].astype(jnp.float32)
    parcels = parcels_of(arrived, span)
    finish(place(parcels, query, new_k, new_v, key_cache, value_cache, held, mixed, osems))


def late_kernel(count, span, *refs):
    arrived, (query, new_k, new_v, weight, before) = refs[:count], refs[count : count + 5]
    out, key_cache, value_cache, held, mixed, osems = refs[count + 7 :]
    mixed[...] = before[...]
    parcels = parcels_of(arrived, span)
    outgoing = place(parcels, query, new_k, new_v, key_cache, value_cache, held, mixed, osems)
    project(mixed, weight, out)
    finish(outgoing)


def total(partial, size):
    if size == 2:
        other = lax.ppermute(partial, "tp", [(0, 1), (1, 0)])
        return (partial.astype(jnp.float32) + other.astype(jnp.float32)).astype(jnp.bfloat16)
    return lax.psum(partial, "tp")


def near(x):
    return pltpu.with_memory_space_constraint(x, pltpu.VMEM)


def hbm(x):
    return pltpu.with_memory_space_constraint(x, pltpu.HBM)


def step_order(n):
    half = n // 2
    lead = [half, half + half // 2, half + 1]
    crossing = lead + [s for s in range(n - 1, half, -1) if s not in lead]
    lead = [1, half // 2]
    staying = lead + [s for s in range(half - 1, 0, -1) if s not in lead]
    order = []
    for kind in "ccncncncncncncn":
        queue = crossing if kind == "c" else staying
        if queue:
            order.append(queue.pop(0))
    while crossing or staying:
        order += crossing[:1] + staying[:1]
        del crossing[:1], staying[:1]
    return order


def shards(
    n,
    tp,
    query_one,
    key_one,
    value_one,
    key_pages,
    value_pages,
    page_table,
    lengths,
    dest_instance,
    dest_slot,
    query_two,
    key_two,
    value_two,
    out_weight,
):
    slots, pages = page_table.shape
    pool, kv_heads, size, width = key_pages.shape
    heads = query_one.shape[1]
    depth, columns = out_weight.shape
    span = pages * size
    assert kv_heads == 1 and slots == n and n >= 16 and span <= 256
    key_pages = key_pages.reshape(pool, size, width)
    value_pages = value_pages.reshape(pool, size, width)
    key_one = key_one.reshape(slots, width)
    value_one = value_one.reshape(slots, width)
    key_two = key_two.reshape(slots, width)
    value_two = value_two.reshape(slots, width)

    vmem = pl.BlockSpec(memory_space=pltpu.VMEM)
    far = pl.BlockSpec(memory_space=pltpu.HBM)
    params = pltpu.CompilerParams(vmem_limit_bytes=VMEM_BYTES)
    bf16, f32, i32 = jnp.bfloat16, jnp.float32, jnp.int32
    rows = 2 * span
    order = step_order(n)
    steps = [0] + order

    def block(height):
        return jax.ShapeDtypeStruct((height, width), bf16)

    shapes = [block(rows)] * n

    def pack(chosen):
        return pl.pallas_call(
            functools.partial(pack_kernel, n, chosen, pages),
            out_shape=[jax.ShapeDtypeStruct((rows, width), bf16)] * len(chosen),
            in_specs=[far] * 8,
            out_specs=[vmem] * len(chosen),
            scratch_shapes=[
                pltpu.SMEM((pages, slots), i32),
                pltpu.SMEM((slots,), i32),
                pltpu.SMEM((slots,), i32),
                pltpu.SMEM((slots,), i32),
                pltpu.VMEM((slots, width), bf16),
                pltpu.VMEM((slots, width), bf16),
                pltpu.VMEM((pool, size, width), bf16),
                pltpu.VMEM((pool, size, width), bf16),
                pltpu.SMEM((n,), i32),
                pltpu.SemaphoreType.DMA((8,)),
            ],
            compiler_params=params,
            cost_estimate=pl.CostEstimate(
                flops=0, bytes_accessed=4 * len(chosen) * rows * width, transcendentals=0
            ),
            name="pack",
        )(
            hbm(page_table.T),
            hbm(lengths),
            hbm(dest_instance),
            hbm(dest_slot),
            hbm(key_one),
            hbm(value_one),
            hbm(key_pages),
            hbm(value_pages),
        )

    steps = step_order(n) + [0]
    packed = pack(steps[:AHEAD]) + pack(steps[AHEAD:])

    flops = 4 * slots * heads * span * width + 2 * slots * depth * columns
    moved = 2 * depth * columns + 4 * slots * span * width
    def send(i, *after):
        block = lax.optimization_barrier((packed[i], *after))[0] if after else packed[i]
        return lax.ppermute(block, "inst", [(d, d ^ steps[i]) for d in range(n)])

    arrived = [send(i) for i in range(AHEAD)]
    partial_one, weight = pl.pallas_call(
        functools.partial(first_kernel, steps, span),
        out_shape=[
            jax.ShapeDtypeStruct((slots, columns), bf16),
            jax.ShapeDtypeStruct((depth, columns), bf16),
        ],
        in_specs=[far] * 4 + [vmem] * len(shapes),
        out_specs=[vmem, vmem],
        scratch_shapes=[
            pltpu.SMEM((slots,), i32),
            pltpu.SMEM((slots,), i32),
            pltpu.VMEM((slots, heads, width), bf16),
            pltpu.SMEM((n,), i32),
            pltpu.VMEM((slots, heads, width), f32),
            pltpu.SemaphoreType.DMA((4,)),
        ],
        compiler_params=params,
        cost_estimate=pl.CostEstimate(flops=flops, bytes_accessed=moved, transcendentals=slots * heads * span),
        name="first",
    )(hbm(lengths), hbm(dest_instance), hbm(query_one), hbm(out_weight), *packed)

    arrived += [send(i, partial_one) for i in range(AHEAD, n - 1)]
    early, late = [packed[-1]] + arrived[:-LATE], arrived[-LATE:]
    cache = jax.ShapeDtypeStruct((slots, span, width), bf16)
    mixed = jax.ShapeDtypeStruct((slots, heads, width), f32)
    some = len(early)
    results = pl.pallas_call(
        functools.partial(early_kernel, some, span),
        out_shape=[cache, cache, mixed]
        + [jax.ShapeDtypeStruct((slots, heads, width), bf16)]
        + [jax.ShapeDtypeStruct((slots, width), f32)] * 2,
        in_specs=[vmem] * some + [far] * 3,
        out_specs=[far, far] + [vmem] * 4,
        scratch_shapes=[
            pltpu.VMEM((slots, width), bf16),
            pltpu.VMEM((slots, width), bf16),
            pltpu.VMEM((2, some, span, width), bf16),
            pltpu.SemaphoreType.DMA((3,)),
            pltpu.SemaphoreType.DMA((2, some)),
        ],
        compiler_params=params,
        cost_estimate=pl.CostEstimate(
            flops=4 * some * heads * span * width,
            bytes_accessed=8 * some * span * width,
            transcendentals=some * heads * span,
        ),
        name="early",
    )(*early, hbm(query_two), hbm(key_two), hbm(value_two))
    key_cache, value_cache, *carried = results
    partial_one = lax.optimization_barrier((partial_one, carried[0]))[0]
    out_one = total(partial_one, tp)

    partial_two, key_cache, value_cache = pl.pallas_call(
        functools.partial(late_kernel, LATE, span),
        out_shape=[jax.ShapeDtypeStruct((slots, columns), bf16), cache, cache],
        in_specs=[vmem] * (len(late) + 5) + [far] * 2,
        out_specs=[vmem, far, far],
        input_output_aliases={len(late) + 5: 1, len(late) + 6: 2},
        scratch_shapes=[
            pltpu.VMEM((2, LATE, span, width), bf16),
            pltpu.VMEM((slots, heads, width), f32),
            pltpu.SemaphoreType.DMA((2, LATE)),
        ],
        compiler_params=params,
        cost_estimate=pl.CostEstimate(flops=flops, bytes_accessed=moved, transcendentals=LATE * heads * span),
        name="late",
    )(
        *late,
        *[near(x) for x in carried[1:]],
        near(weight),
        near(carried[0]),
        hbm(key_cache),
        hbm(value_cache),
    )
    out_two = total(partial_two, tp)
    shape = (slots * pages, kv_heads, size, width)
    return (out_one, out_two, key_cache.reshape(shape), value_cache.reshape(shape))


def solution(mesh):
    sizes = dict(mesh.shape)
    return jax.shard_map(
        functools.partial(shards, sizes["inst"], sizes["tp"]),
        mesh=mesh,
        in_specs=(
            P("inst", "tp", None),
            P("inst", "tp", None),
            P("inst", "tp", None),
            P("inst", "tp", None, None),
            P("inst", "tp", None, None),
            P("inst", None),
            P("inst"),
            P("inst"),
            P("inst"),
            P("inst", "tp", None),
            P("inst", "tp", None),
            P("inst", "tp", None),
            P("tp", None),
        ),
        out_specs=(
            P("inst", None),
            P("inst", None),
            P("inst", "tp", None, None),
            P("inst", "tp", None, None),
        ),
        check_vma=False,
    )
```

```python
import functools

import jax
import jax.numpy as jnp
from jax import lax
from jax.experimental import pallas as pl
from jax.experimental.pallas import tpu as pltpu
from jax.sharding import PartitionSpec as P

NEG = -1e30
TILE = 16
SPLIT = 64
CHUNKS = 8
AHEAD = 5
LATE = 5
VMEM_BYTES = 24 * 1024 * 1024


def row_of(block, at):
    rows = lax.broadcasted_iota(jnp.int32, block.shape, 0)
    return jnp.sum(jnp.where(rows == at, block, 0.0), axis=0, keepdims=True)


def row_at(block, position):
    base = pl.multiple_of(position // TILE * TILE, TILE)
    return row_of(block[pl.ds(base, TILE), :].astype(jnp.float32), position % TILE)


def put_row(block, row, position):
    base = pl.multiple_of(position // TILE * TILE, TILE)
    part = block[pl.ds(base, TILE), :]
    at = lax.broadcasted_iota(jnp.int32, part.shape, 0)
    mixed = jnp.where(at == position % TILE, row, part.astype(jnp.float32))
    block[pl.ds(base, TILE), :] = mixed.astype(jnp.bfloat16)


def put_last(block, row):
    end = block.shape[0]
    part = block[end - TILE : end, :]
    at = lax.broadcasted_iota(jnp.int32, part.shape, 0)
    mixed = jnp.where(at == TILE - 1, row, part.astype(jnp.float32))
    block[end - TILE : end, :] = mixed.astype(jnp.bfloat16)


def last_row(block):
    end = block.shape[0]
    return block[end - TILE : end, :].astype(jnp.float32)[TILE - 1 : TILE, :]


def invert(dest, source, n):
    def note(r, carry):
        source[dest[r]] = r
        return carry

    lax.fori_loop(0, n, note, 0)


def begin(pairs, sem):
    copies = [pltpu.make_async_copy(a, b, sem.at[i]) for i, (a, b) in enumerate(pairs)]
    for copy in copies:
        copy.start()
    return copies


def finish(copies):
    for copy in copies:
        copy.wait()


def parcels_of(refs, span):
    return [(ref.at[pl.ds(0, span)], ref.at[pl.ds(span, span)]) for ref in refs]


def sources(source, steps):
    me = lax.axis_index("inst")
    return [source[me ^ s] for s in steps]


def pack_kernel(n, steps, pages, *refs):
    count = len(steps)
    far, outs = refs[:8], refs[8 : 8 + count]
    table, lengths, dest, slot, key_one, value_one, key_pool, value_pool, source, sems = refs[8 + count :]
    copies = begin(list(zip(far, (table, lengths, dest, slot, key_one, value_one, key_pool, value_pool))), sems)
    size = key_pool.shape[1]
    parcels = parcels_of(outs, pages * size)
    finish(copies[:6])
    invert(dest, source, n)
    at = sources(source, steps)
    tokens = (key_one[...].astype(jnp.float32), value_one[...].astype(jnp.float32))
    lanes = lax.broadcasted_iota(jnp.int32, (1, key_one.shape[1]), 1)
    for which, pool in ((0, key_pool), (1, value_pool)):
        copies[6 + which].wait()
        for r, parcel in zip(at, parcels):
            for p in range(pages):
                parcel[which][p * size : (p + 1) * size, :] = pool[table[p, r]]
            put_row(parcel[which], row_of(tokens[which], r), lengths[r])
            if which == 0:
                put_row(parcel[0], last_row(parcel[0]), lengths[r] + 1)
                note = jnp.where(lanes < SPLIT, slot[r], lengths[r]).astype(jnp.float32)
                put_last(parcel[0], note)


def attend(queries, keys, values, counts):
    width = queries[0].shape[1]
    scores = []
    for q, k, count in zip(queries, keys, counts):
        s = lax.dot_general(q, k, (((1,), (1,)), ((), ())), preferred_element_type=jnp.float32)
        live = lax.broadcasted_iota(jnp.int32, s.shape, 1) < count
        scores.append(jnp.where(live, s * width ** (-0.5), NEG))
    group = scores[0].shape[0]
    score = jnp.concatenate(scores, axis=0)
    top = jnp.max(score, axis=-1, keepdims=True)
    expo = jnp.exp(score - top)
    weights = (expo / jnp.sum(expo, axis=-1, keepdims=True)).astype(jnp.bfloat16)
    return [
        jnp.dot(weights[i * group : (i + 1) * group], v, preferred_element_type=jnp.float32)
        for i, v in enumerate(values)
    ]


def project(mixed, weight, out):
    heads = mixed.shape[1]
    rows = jnp.concatenate([mixed[:, h, :] for h in range(heads)], axis=1).astype(jnp.bfloat16)
    width = weight.shape[1] // CHUNKS
    for c in range(CHUNKS):
        part = jnp.dot(
            rows, weight[:, c * width : (c + 1) * width], preferred_element_type=jnp.float32
        )
        out[:, c * width : (c + 1) * width] = part.astype(jnp.bfloat16)


def first_kernel(steps, span, *refs):
    n = len(steps)
    far, parcels, out, weight = refs[:4], refs[4 : 4 + n], refs[4 + n], refs[5 + n]
    lengths, dest, query, source, mixed, sems = refs[6 + n :]
    copies = begin(list(zip(far, (lengths, dest, query, weight))), sems)
    parcels = parcels_of(parcels, span)
    finish(copies[:3])
    invert(dest, source, n)
    at = sources(source, steps)
    results = attend(
        [query[r] for r in at],
        [parcel[0][...] for parcel in parcels],
        [parcel[1][...] for parcel in parcels],
        [lengths[r] + 1 for r in at],
    )
    for r, result in zip(at, results):
        mixed[r] = result
    copies[3].wait()
    project(mixed, weight, out)


def place(arrived, query, key_two, value_two, key_cache, value_cache, held, mixed, osems):
    count = len(arrived)
    slots = []
    lengths = []
    for parcel in arrived:
        note = last_row(parcel[0])
        lanes = lax.broadcasted_iota(jnp.int32, note.shape, 1)
        slots.append(jnp.max(jnp.where(lanes < SPLIT, note, 0.0)).astype(jnp.int32))
        lengths.append(jnp.max(jnp.where(lanes < SPLIT, 0.0, note)).astype(jnp.int32))
    for i, parcel in enumerate(arrived):
        held[0, i] = parcel[0][...]
        held[1, i] = parcel[1][...]
        put_last(held.at[0, i], row_at(parcel[0], lengths[i] + 1))
    outgoing = []
    for i in range(count):
        for which, (token, cache) in enumerate(((key_two, key_cache), (value_two, value_cache))):
            put_row(held.at[which, i], token[pl.ds(slots[i], 1), :], lengths[i] + 1)
            copy = pltpu.make_async_copy(held.at[which, i], cache.at[slots[i]], osems.at[which, i])
            copy.start()
            outgoing.append(copy)
    results = attend(
        [query[j] for j in slots],
        [held[0, i] for i in range(count)],
        [held[1, i] for i in range(count)],
        [length + 2 for length in lengths],
    )
    for j, result in zip(slots, results):
        mixed[j] = result
    return outgoing


def early_kernel(count, span, *refs):
    arrived, far = refs[:count], refs[count : count + 3]
    key_cache, value_cache, mixed, query, new_k, new_v = refs[count + 3 : count + 9]
    key_two, value_two, held, sems, osems = refs[-5:]
    copies = begin(list(zip(far, (query, key_two, value_two))), sems)
    finish(copies)
    new_k[...] = key_two[...].astype(jnp.float32)
    new_v[...] = value_two[...].astype(jnp.float32)
    parcels = parcels_of(arrived, span)
    finish(place(parcels, query, new_k, new_v, key_cache, value_cache, held, mixed, osems))


def late_kernel(count, span, *refs):
    arrived, (query, new_k, new_v, weight, before) = refs[:count], refs[count : count + 5]
    out, key_cache, value_cache, held, mixed, osems = refs[count + 7 :]
    mixed[...] = before[...]
    parcels = parcels_of(arrived, span)
    outgoing = place(parcels, query, new_k, new_v, key_cache, value_cache, held, mixed, osems)
    project(mixed, weight, out)
    finish(outgoing)


def total(partial, size):
    if size == 2:
        other = lax.ppermute(partial, "tp", [(0, 1), (1, 0)])
        return (partial.astype(jnp.float32) + other.astype(jnp.float32)).astype(jnp.bfloat16)
    return lax.psum(partial, "tp")


def near(x):
    return pltpu.with_memory_space_constraint(x, pltpu.VMEM)


def hbm(x):
    return pltpu.with_memory_space_constraint(x, pltpu.HBM)


def step_order(n):
    half = n // 2
    crossing = [half] + list(range(half + 1, n))[::-1]
    staying = list(range(1, half))[::-1]
    order = []
    for kind in "ccncncncncncncn":
        queue = crossing if kind == "c" else staying
        if queue:
            order.append(queue.pop(0))
    while crossing or staying:
        order += crossing[:1] + staying[:1]
        del crossing[:1], staying[:1]
    return order


def shards(
    n,
    tp,
    query_one,
    key_one,
    value_one,
    key_pages,
    value_pages,
    page_table,
    lengths,
    dest_instance,
    dest_slot,
    query_two,
    key_two,
    value_two,
    out_weight,
):
    slots, pages = page_table.shape
    pool, kv_heads, size, width = key_pages.shape
    heads = query_one.shape[1]
    depth, columns = out_weight.shape
    span = pages * size
    assert kv_heads == 1 and slots == n and n >= 16 and span <= 256
    key_pages = key_pages.reshape(pool, size, width)
    value_pages = value_pages.reshape(pool, size, width)
    key_one = key_one.reshape(slots, width)
    value_one = value_one.reshape(slots, width)
    key_two = key_two.reshape(slots, width)
    value_two = value_two.reshape(slots, width)

    vmem = pl.BlockSpec(memory_space=pltpu.VMEM)
    far = pl.BlockSpec(memory_space=pltpu.HBM)
    params = pltpu.CompilerParams(vmem_limit_bytes=VMEM_BYTES)
    bf16, f32, i32 = jnp.bfloat16, jnp.float32, jnp.int32
    rows = 2 * span
    order = step_order(n)
    steps = [0] + order

    def block(height):
        return jax.ShapeDtypeStruct((height, width), bf16)

    shapes = [block(rows)] * n

    def pack(chosen):
        return pl.pallas_call(
            functools.partial(pack_kernel, n, chosen, pages),
            out_shape=[jax.ShapeDtypeStruct((rows, width), bf16)] * len(chosen),
            in_specs=[far] * 8,
            out_specs=[vmem] * len(chosen),
            scratch_shapes=[
                pltpu.SMEM((pages, slots), i32),
                pltpu.SMEM((slots,), i32),
                pltpu.SMEM((slots,), i32),
                pltpu.SMEM((slots,), i32),
                pltpu.VMEM((slots, width), bf16),
                pltpu.VMEM((slots, width), bf16),
                pltpu.VMEM((pool, size, width), bf16),
                pltpu.VMEM((pool, size, width), bf16),
                pltpu.SMEM((n,), i32),
                pltpu.SemaphoreType.DMA((8,)),
            ],
            compiler_params=params,
            cost_estimate=pl.CostEstimate(
                flops=0, bytes_accessed=4 * len(chosen) * rows * width, transcendentals=0
            ),
            name="pack",
        )(
            hbm(page_table.T),
            hbm(lengths),
            hbm(dest_instance),
            hbm(dest_slot),
            hbm(key_one),
            hbm(value_one),
            hbm(key_pages),
            hbm(value_pages),
        )

    steps = step_order(n) + [0]
    packed = pack(steps[:AHEAD]) + pack(steps[AHEAD:])

    flops = 4 * slots * heads * span * width + 2 * slots * depth * columns
    moved = 2 * depth * columns + 4 * slots * span * width
    def send(i, *after):
        block = lax.optimization_barrier((packed[i], *after))[0] if after else packed[i]
        return lax.ppermute(block, "inst", [(d, d ^ steps[i]) for d in range(n)])

    arrived = [send(i) for i in range(AHEAD)]
    partial_one, weight = pl.pallas_call(
        functools.partial(first_kernel, steps, span),
        out_shape=[
            jax.ShapeDtypeStruct((slots, columns), bf16),
            jax.ShapeDtypeStruct((depth, columns), bf16),
        ],
        in_specs=[far] * 4 + [vmem] * len(shapes),
        out_specs=[vmem, vmem],
        scratch_shapes=[
            pltpu.SMEM((slots,), i32),
            pltpu.SMEM((slots,), i32),
            pltpu.VMEM((slots, heads, width), bf16),
            pltpu.SMEM((n,), i32),
            pltpu.VMEM((slots, heads, width), f32),
            pltpu.SemaphoreType.DMA((4,)),
        ],
        compiler_params=params,
        cost_estimate=pl.CostEstimate(flops=flops, bytes_accessed=moved, transcendentals=slots * heads * span),
        name="first",
    )(hbm(lengths), hbm(dest_instance), hbm(query_one), hbm(out_weight), *packed)

    arrived += [send(i, partial_one) for i in range(AHEAD, n - 1)]
    early, late = [packed[-1]] + arrived[:-LATE], arrived[-LATE:]
    cache = jax.ShapeDtypeStruct((slots, span, width), bf16)
    mixed = jax.ShapeDtypeStruct((slots, heads, width), f32)
    some = len(early)
    results = pl.pallas_call(
        functools.partial(early_kernel, some, span),
        out_shape=[cache, cache, mixed]
        + [jax.ShapeDtypeStruct((slots, heads, width), bf16)]
        + [jax.ShapeDtypeStruct((slots, width), f32)] * 2,
        in_specs=[vmem] * some + [far] * 3,
        out_specs=[far, far] + [vmem] * 4,
        scratch_shapes=[
            pltpu.VMEM((slots, width), bf16),
            pltpu.VMEM((slots, width), bf16),
            pltpu.VMEM((2, some, span, width), bf16),
            pltpu.SemaphoreType.DMA((3,)),
            pltpu.SemaphoreType.DMA((2, some)),
        ],
        compiler_params=params,
        cost_estimate=pl.CostEstimate(
            flops=4 * some * heads * span * width,
            bytes_accessed=8 * some * span * width,
            transcendentals=some * heads * span,
        ),
        name="early",
    )(*early, hbm(query_two), hbm(key_two), hbm(value_two))
    key_cache, value_cache, *carried = results
    partial_one = lax.optimization_barrier((partial_one, carried[0]))[0]
    out_one = total(partial_one, tp)

    partial_two, key_cache, value_cache = pl.pallas_call(
        functools.partial(late_kernel, LATE, span),
        out_shape=[jax.ShapeDtypeStruct((slots, columns), bf16), cache, cache],
        in_specs=[vmem] * (len(late) + 5) + [far] * 2,
        out_specs=[vmem, far, far],
        input_output_aliases={len(late) + 5: 1, len(late) + 6: 2},
        scratch_shapes=[
            pltpu.VMEM((2, LATE, span, width), bf16),
            pltpu.VMEM((slots, heads, width), f32),
            pltpu.SemaphoreType.DMA((2, LATE)),
        ],
        compiler_params=params,
        cost_estimate=pl.CostEstimate(flops=flops, bytes_accessed=moved, transcendentals=LATE * heads * span),
        name="late",
    )(
        *late,
        *[near(x) for x in carried[1:]],
        near(weight),
        near(carried[0]),
        hbm(key_cache),
        hbm(value_cache),
    )
    out_two = total(partial_two, tp)
    shape = (slots * pages, kv_heads, size, width)
    return (out_one, out_two, key_cache.reshape(shape), value_cache.reshape(shape))


def solution(mesh):
    sizes = dict(mesh.shape)
    return jax.shard_map(
        functools.partial(shards, sizes["inst"], sizes["tp"]),
        mesh=mesh,
        in_specs=(
            P("inst", "tp", None),
            P("inst", "tp", None),
            P("inst", "tp", None),
            P("inst", "tp", None, None),
            P("inst", "tp", None, None),
            P("inst", None),
            P("inst"),
            P("inst"),
            P("inst"),
            P("inst", "tp", None),
            P("inst", "tp", None),
            P("inst", "tp", None),
            P("tp", None),
        ),
        out_specs=(
            P("inst", None),
            P("inst", None),
            P("inst", "tp", None, None),
            P("inst", "tp", None, None),
        ),
        check_vma=False,
    )
```

```python
import functools

import jax
import jax.numpy as jnp
from jax import lax
from jax.experimental import pallas as pl
from jax.experimental.pallas import tpu as pltpu
from jax.sharding import PartitionSpec as P

NEG = -1e30
Z = 4
TILE = 16
SPLIT = 64
CHUNKS = 8
AHEAD = 5
LATE = 5
VMEM_BYTES = 24 * 1024 * 1024


def row_of(block, at):
    rows = lax.broadcasted_iota(jnp.int32, block.shape, 0)
    return jnp.sum(jnp.where(rows == at, block, 0.0), axis=0, keepdims=True)


def row_at(block, position):
    base = pl.multiple_of(position // TILE * TILE, TILE)
    return row_of(block[pl.ds(base, TILE), :].astype(jnp.float32), position % TILE)


def put_row(block, row, position):
    base = pl.multiple_of(position // TILE * TILE, TILE)
    part = block[pl.ds(base, TILE), :]
    at = lax.broadcasted_iota(jnp.int32, part.shape, 0)
    mixed = jnp.where(at == position % TILE, row, part.astype(jnp.float32))
    block[pl.ds(base, TILE), :] = mixed.astype(jnp.bfloat16)


def put_last(block, row):
    end = block.shape[0]
    part = block[end - TILE : end, :]
    at = lax.broadcasted_iota(jnp.int32, part.shape, 0)
    mixed = jnp.where(at == TILE - 1, row, part.astype(jnp.float32))
    block[end - TILE : end, :] = mixed.astype(jnp.bfloat16)


def last_row(block):
    end = block.shape[0]
    return block[end - TILE : end, :].astype(jnp.float32)[TILE - 1 : TILE, :]


def invert(dest, source, n):
    def note(r, carry):
        source[dest[r]] = r
        return carry

    lax.fori_loop(0, n, note, 0)


def begin(pairs, sem):
    copies = [pltpu.make_async_copy(a, b, sem.at[i]) for i, (a, b) in enumerate(pairs)]
    for copy in copies:
        copy.start()
    return copies


def finish(copies):
    for copy in copies:
        copy.wait()


def parcels_of(refs, span):
    return [(ref.at[pl.ds(0, span)], ref.at[pl.ds(span, span)]) for ref in refs]


def sources(source, steps):
    n = source.shape[0]
    me = lax.axis_index("inst")
    return [source[target(me, step, n)] for step in steps]


def pack_kernel(n, steps, pages, *refs):
    count = len(steps)
    far, outs = refs[:8], refs[8 : 8 + count]
    table, lengths, dest, slot, key_one, value_one, key_pool, value_pool, source, sems = refs[8 + count :]
    copies = begin(list(zip(far, (table, lengths, dest, slot, key_one, value_one, key_pool, value_pool))), sems)
    size = key_pool.shape[1]
    parcels = parcels_of(outs, pages * size)
    finish(copies[:6])
    invert(dest, source, n)
    at = sources(source, steps)
    tokens = (key_one[...].astype(jnp.float32), value_one[...].astype(jnp.float32))
    lanes = lax.broadcasted_iota(jnp.int32, (1, key_one.shape[1]), 1)
    for which, pool in ((0, key_pool), (1, value_pool)):
        copies[6 + which].wait()
        for r, parcel in zip(at, parcels):
            for p in range(pages):
                parcel[which][p * size : (p + 1) * size, :] = pool[table[p, r]]
            put_row(parcel[which], row_of(tokens[which], r), lengths[r])
            if which == 0:
                put_row(parcel[0], last_row(parcel[0]), lengths[r] + 1)
                note = jnp.where(lanes < SPLIT, slot[r], lengths[r]).astype(jnp.float32)
                put_last(parcel[0], note)


def attend(queries, keys, values, counts):
    width = queries[0].shape[1]
    scores = []
    for q, k, count in zip(queries, keys, counts):
        s = lax.dot_general(q, k, (((1,), (1,)), ((), ())), preferred_element_type=jnp.float32)
        live = lax.broadcasted_iota(jnp.int32, s.shape, 1) < count
        scores.append(jnp.where(live, s * width ** (-0.5), NEG))
    group = scores[0].shape[0]
    score = jnp.concatenate(scores, axis=0)
    top = jnp.max(score, axis=-1, keepdims=True)
    expo = jnp.exp(score - top)
    weights = (expo / jnp.sum(expo, axis=-1, keepdims=True)).astype(jnp.bfloat16)
    return [
        jnp.dot(weights[i * group : (i + 1) * group], v, preferred_element_type=jnp.float32)
        for i, v in enumerate(values)
    ]


def project(mixed, weight, out):
    heads = mixed.shape[1]
    rows = jnp.concatenate([mixed[:, h, :] for h in range(heads)], axis=1).astype(jnp.bfloat16)
    width = weight.shape[1] // CHUNKS
    for c in range(CHUNKS):
        part = jnp.dot(
            rows, weight[:, c * width : (c + 1) * width], preferred_element_type=jnp.float32
        )
        out[:, c * width : (c + 1) * width] = part.astype(jnp.bfloat16)


def first_kernel(steps, span, *refs):
    n = len(steps)
    far, parcels, out, weight = refs[:4], refs[4 : 4 + n], refs[4 + n], refs[5 + n]
    lengths, dest, query, source, mixed, sems = refs[6 + n :]
    copies = begin(list(zip(far, (lengths, dest, query, weight))), sems)
    parcels = parcels_of(parcels, span)
    finish(copies[:3])
    invert(dest, source, n)
    at = sources(source, steps)
    results = attend(
        [query[r] for r in at],
        [parcel[0][...] for parcel in parcels],
        [parcel[1][...] for parcel in parcels],
        [lengths[r] + 1 for r in at],
    )
    for r, result in zip(at, results):
        mixed[r] = result
    copies[3].wait()
    project(mixed, weight, out)


def place(arrived, query, key_two, value_two, key_cache, value_cache, held, mixed, osems):
    count = len(arrived)
    slots = []
    lengths = []
    for parcel in arrived:
        note = last_row(parcel[0])
        lanes = lax.broadcasted_iota(jnp.int32, note.shape, 1)
        slots.append(jnp.max(jnp.where(lanes < SPLIT, note, 0.0)).astype(jnp.int32))
        lengths.append(jnp.max(jnp.where(lanes < SPLIT, 0.0, note)).astype(jnp.int32))
    for i, parcel in enumerate(arrived):
        held[0, i] = parcel[0][...]
        held[1, i] = parcel[1][...]
        put_last(held.at[0, i], row_at(parcel[0], lengths[i] + 1))
    outgoing = []
    for i in range(count):
        for which, (token, cache) in enumerate(((key_two, key_cache), (value_two, value_cache))):
            put_row(held.at[which, i], token[pl.ds(slots[i], 1), :], lengths[i] + 1)
            copy = pltpu.make_async_copy(held.at[which, i], cache.at[slots[i]], osems.at[which, i])
            copy.start()
            outgoing.append(copy)
    results = attend(
        [query[j] for j in slots],
        [held[0, i] for i in range(count)],
        [held[1, i] for i in range(count)],
        [length + 2 for length in lengths],
    )
    for j, result in zip(slots, results):
        mixed[j] = result
    return outgoing


def early_kernel(count, span, *refs):
    arrived, far = refs[:count], refs[count : count + 3]
    key_cache, value_cache, mixed, query, new_k, new_v = refs[count + 3 : count + 9]
    key_two, value_two, held, sems, osems = refs[-5:]
    copies = begin(list(zip(far, (query, key_two, value_two))), sems)
    finish(copies)
    new_k[...] = key_two[...].astype(jnp.float32)
    new_v[...] = value_two[...].astype(jnp.float32)
    parcels = parcels_of(arrived, span)
    finish(place(parcels, query, new_k, new_v, key_cache, value_cache, held, mixed, osems))


def late_kernel(count, span, *refs):
    arrived, (query, new_k, new_v, weight, before) = refs[:count], refs[count : count + 5]
    out, key_cache, value_cache, held, mixed, osems = refs[count + 7 :]
    mixed[...] = before[...]
    parcels = parcels_of(arrived, span)
    outgoing = place(parcels, query, new_k, new_v, key_cache, value_cache, held, mixed, osems)
    project(mixed, weight, out)
    finish(outgoing)


def total(partial, size):
    if size == 2:
        other = lax.ppermute(partial, "tp", [(0, 1), (1, 0)])
        return (partial.astype(jnp.float32) + other.astype(jnp.float32)).astype(jnp.bfloat16)
    return lax.psum(partial, "tp")


def near(x):
    return pltpu.with_memory_space_constraint(x, pltpu.VMEM)


def hbm(x):
    return pltpu.with_memory_space_constraint(x, pltpu.HBM)


def step_order(n):
    part = n // Z
    order = [(2, 0)]
    for b in range(part - 1, 0, -1):
        order += [(1, b), (2, b), (3, b), (0, b)]
    return order + [(1, 0), (3, 0)]


def target(at, step, n):
    part = n // Z
    return (at // part + step[0]) % Z * part + (at % part ^ step[1])


def shards(
    n,
    tp,
    query_one,
    key_one,
    value_one,
    key_pages,
    value_pages,
    page_table,
    lengths,
    dest_instance,
    dest_slot,
    query_two,
    key_two,
    value_two,
    out_weight,
):
    slots, pages = page_table.shape
    pool, kv_heads, size, width = key_pages.shape
    heads = query_one.shape[1]
    depth, columns = out_weight.shape
    span = pages * size
    assert kv_heads == 1 and slots == n and n % 16 == 0 and span <= 256
    key_pages = key_pages.reshape(pool, size, width)
    value_pages = value_pages.reshape(pool, size, width)
    key_one = key_one.reshape(slots, width)
    value_one = value_one.reshape(slots, width)
    key_two = key_two.reshape(slots, width)
    value_two = value_two.reshape(slots, width)

    vmem = pl.BlockSpec(memory_space=pltpu.VMEM)
    far = pl.BlockSpec(memory_space=pltpu.HBM)
    params = pltpu.CompilerParams(vmem_limit_bytes=VMEM_BYTES)
    bf16, f32, i32 = jnp.bfloat16, jnp.float32, jnp.int32
    rows = 2 * span
    order = step_order(n)
    steps = [0] + order

    def block(height):
        return jax.ShapeDtypeStruct((height, width), bf16)

    shapes = [block(rows)] * n

    def pack(chosen):
        return pl.pallas_call(
            functools.partial(pack_kernel, n, chosen, pages),
            out_shape=[jax.ShapeDtypeStruct((rows, width), bf16)] * len(chosen),
            in_specs=[far] * 8,
            out_specs=[vmem] * len(chosen),
            scratch_shapes=[
                pltpu.SMEM((pages, slots), i32),
                pltpu.SMEM((slots,), i32),
                pltpu.SMEM((slots,), i32),
                pltpu.SMEM((slots,), i32),
                pltpu.VMEM((slots, width), bf16),
                pltpu.VMEM((slots, width), bf16),
                pltpu.VMEM((pool, size, width), bf16),
                pltpu.VMEM((pool, size, width), bf16),
                pltpu.SMEM((n,), i32),
                pltpu.SemaphoreType.DMA((8,)),
            ],
            compiler_params=params,
            cost_estimate=pl.CostEstimate(
                flops=0, bytes_accessed=4 * len(chosen) * rows * width, transcendentals=0
            ),
            name="pack",
        )(
            hbm(page_table.T),
            hbm(lengths),
            hbm(dest_instance),
            hbm(dest_slot),
            hbm(key_one),
            hbm(value_one),
            hbm(key_pages),
            hbm(value_pages),
        )

    steps = step_order(n) + [(0, 0)]
    packed = pack(steps[:AHEAD]) + pack(steps[AHEAD:])

    flops = 4 * slots * heads * span * width + 2 * slots * depth * columns
    moved = 2 * depth * columns + 4 * slots * span * width
    def send(i, *after):
        block = lax.optimization_barrier((packed[i], *after))[0] if after else packed[i]
        return lax.ppermute(block, "inst", [(d, target(d, steps[i], n)) for d in range(n)])

    arrived = [send(i) for i in range(AHEAD)]
    partial_one, weight = pl.pallas_call(
        functools.partial(first_kernel, steps, span),
        out_shape=[
            jax.ShapeDtypeStruct((slots, columns), bf16),
            jax.ShapeDtypeStruct((depth, columns), bf16),
        ],
        in_specs=[far] * 4 + [vmem] * len(shapes),
        out_specs=[vmem, vmem],
        scratch_shapes=[
            pltpu.SMEM((slots,), i32),
            pltpu.SMEM((slots,), i32),
            pltpu.VMEM((slots, heads, width), bf16),
            pltpu.SMEM((n,), i32),
            pltpu.VMEM((slots, heads, width), f32),
            pltpu.SemaphoreType.DMA((4,)),
        ],
        compiler_params=params,
        cost_estimate=pl.CostEstimate(flops=flops, bytes_accessed=moved, transcendentals=slots * heads * span),
        name="first",
    )(hbm(lengths), hbm(dest_instance), hbm(query_one), hbm(out_weight), *packed)

    arrived += [send(i, partial_one) for i in range(AHEAD, n - 1)]
    early, late = [packed[-1]] + arrived[:-LATE], arrived[-LATE:]
    cache = jax.ShapeDtypeStruct((slots, span, width), bf16)
    mixed = jax.ShapeDtypeStruct((slots, heads, width), f32)
    some = len(early)
    results = pl.pallas_call(
        functools.partial(early_kernel, some, span),
        out_shape=[cache, cache, mixed]
        + [jax.ShapeDtypeStruct((slots, heads, width), bf16)]
        + [jax.ShapeDtypeStruct((slots, width), f32)] * 2,
        in_specs=[vmem] * some + [far] * 3,
        out_specs=[far, far] + [vmem] * 4,
        scratch_shapes=[
            pltpu.VMEM((slots, width), bf16),
            pltpu.VMEM((slots, width), bf16),
            pltpu.VMEM((2, some, span, width), bf16),
            pltpu.SemaphoreType.DMA((3,)),
            pltpu.SemaphoreType.DMA((2, some)),
        ],
        compiler_params=params,
        cost_estimate=pl.CostEstimate(
            flops=4 * some * heads * span * width,
            bytes_accessed=8 * some * span * width,
            transcendentals=some * heads * span,
        ),
        name="early",
    )(*early, hbm(query_two), hbm(key_two), hbm(value_two))
    key_cache, value_cache, *carried = results
    partial_one = lax.optimization_barrier((partial_one, carried[0]))[0]
    out_one = total(partial_one, tp)

    partial_two, key_cache, value_cache = pl.pallas_call(
        functools.partial(late_kernel, LATE, span),
        out_shape=[jax.ShapeDtypeStruct((slots, columns), bf16), cache, cache],
        in_specs=[vmem] * (len(late) + 5) + [far] * 2,
        out_specs=[vmem, far, far],
        input_output_aliases={len(late) + 5: 1, len(late) + 6: 2},
        scratch_shapes=[
            pltpu.VMEM((2, LATE, span, width), bf16),
            pltpu.VMEM((slots, heads, width), f32),
            pltpu.SemaphoreType.DMA((2, LATE)),
        ],
        compiler_params=params,
        cost_estimate=pl.CostEstimate(flops=flops, bytes_accessed=moved, transcendentals=LATE * heads * span),
        name="late",
    )(
        *late,
        *[near(x) for x in carried[1:]],
        near(weight),
        near(carried[0]),
        hbm(key_cache),
        hbm(value_cache),
    )
    out_two = total(partial_two, tp)
    shape = (slots * pages, kv_heads, size, width)
    return (out_one, out_two, key_cache.reshape(shape), value_cache.reshape(shape))


def solution(mesh):
    sizes = dict(mesh.shape)
    return jax.shard_map(
        functools.partial(shards, sizes["inst"], sizes["tp"]),
        mesh=mesh,
        in_specs=(
            P("inst", "tp", None),
            P("inst", "tp", None),
            P("inst", "tp", None),
            P("inst", "tp", None, None),
            P("inst", "tp", None, None),
            P("inst", None),
            P("inst"),
            P("inst"),
            P("inst"),
            P("inst", "tp", None),
            P("inst", "tp", None),
            P("inst", "tp", None),
            P("tp", None),
        ),
        out_specs=(
            P("inst", None),
            P("inst", None),
            P("inst", "tp", None, None),
            P("inst", "tp", None, None),
        ),
        check_vma=False,
    )
```

```python
import functools

import jax
import jax.numpy as jnp
from jax import lax
from jax.experimental import pallas as pl
from jax.experimental.pallas import tpu as pltpu
from jax.sharding import PartitionSpec as P

NEG = -1e30
Z = 4
TILE = 16
SPLIT = 64
CHUNKS = 8
AHEAD = 5
LATE = 5
VMEM_BYTES = 24 * 1024 * 1024


def row_of(block, at):
    rows = lax.broadcasted_iota(jnp.int32, block.shape, 0)
    return jnp.sum(jnp.where(rows == at, block, 0.0), axis=0, keepdims=True)


def row_at(block, position):
    base = pl.multiple_of(position // TILE * TILE, TILE)
    return row_of(block[pl.ds(base, TILE), :].astype(jnp.float32), position % TILE)


def put_row(block, row, position):
    base = pl.multiple_of(position // TILE * TILE, TILE)
    part = block[pl.ds(base, TILE), :]
    at = lax.broadcasted_iota(jnp.int32, part.shape, 0)
    mixed = jnp.where(at == position % TILE, row, part.astype(jnp.float32))
    block[pl.ds(base, TILE), :] = mixed.astype(jnp.bfloat16)


def put_last(block, row):
    end = block.shape[0]
    part = block[end - TILE : end, :]
    at = lax.broadcasted_iota(jnp.int32, part.shape, 0)
    mixed = jnp.where(at == TILE - 1, row, part.astype(jnp.float32))
    block[end - TILE : end, :] = mixed.astype(jnp.bfloat16)


def last_row(block):
    end = block.shape[0]
    return block[end - TILE : end, :].astype(jnp.float32)[TILE - 1 : TILE, :]


def invert(dest, source, n):
    def note(r, carry):
        source[dest[r]] = r
        return carry

    lax.fori_loop(0, n, note, 0)


def begin(pairs, sem):
    copies = [pltpu.make_async_copy(a, b, sem.at[i]) for i, (a, b) in enumerate(pairs)]
    for copy in copies:
        copy.start()
    return copies


def finish(copies):
    for copy in copies:
        copy.wait()


def parcels_of(refs, span):
    return [(ref.at[pl.ds(0, span)], ref.at[pl.ds(span, span)]) for ref in refs]


def sources(source, steps):
    n = source.shape[0]
    me = lax.axis_index("inst")
    return [source[target(me, step, n)] for step in steps]


def pack_kernel(n, steps, pages, *refs):
    count = len(steps)
    far, outs = refs[:8], refs[8 : 8 + count]
    table, lengths, dest, slot, key_one, value_one, key_pool, value_pool, source, sems = refs[8 + count :]
    copies = begin(list(zip(far, (table, lengths, dest, slot, key_one, value_one, key_pool, value_pool))), sems)
    size = key_pool.shape[1]
    parcels = parcels_of(outs, pages * size)
    finish(copies[:6])
    invert(dest, source, n)
    at = sources(source, steps)
    tokens = (key_one[...].astype(jnp.float32), value_one[...].astype(jnp.float32))
    lanes = lax.broadcasted_iota(jnp.int32, (1, key_one.shape[1]), 1)
    for which, pool in ((0, key_pool), (1, value_pool)):
        copies[6 + which].wait()
        for r, parcel in zip(at, parcels):
            for p in range(pages):
                parcel[which][p * size : (p + 1) * size, :] = pool[table[p, r]]
            put_row(parcel[which], row_of(tokens[which], r), lengths[r])
            if which == 0:
                put_row(parcel[0], last_row(parcel[0]), lengths[r] + 1)
                note = jnp.where(lanes < SPLIT, slot[r], lengths[r]).astype(jnp.float32)
                put_last(parcel[0], note)


def attend(queries, keys, values, counts):
    width = queries[0].shape[1]
    scores = []
    for q, k, count in zip(queries, keys, counts):
        s = lax.dot_general(q, k, (((1,), (1,)), ((), ())), preferred_element_type=jnp.float32)
        live = lax.broadcasted_iota(jnp.int32, s.shape, 1) < count
        scores.append(jnp.where(live, s * width ** (-0.5), NEG))
    group = scores[0].shape[0]
    score = jnp.concatenate(scores, axis=0)
    top = jnp.max(score, axis=-1, keepdims=True)
    expo = jnp.exp(score - top)
    weights = (expo / jnp.sum(expo, axis=-1, keepdims=True)).astype(jnp.bfloat16)
    return [
        jnp.dot(weights[i * group : (i + 1) * group], v, preferred_element_type=jnp.float32)
        for i, v in enumerate(values)
    ]


def project(mixed, weight, out):
    heads = mixed.shape[1]
    rows = jnp.concatenate([mixed[:, h, :] for h in range(heads)], axis=1).astype(jnp.bfloat16)
    width = weight.shape[1] // CHUNKS
    for c in range(CHUNKS):
        part = jnp.dot(
            rows, weight[:, c * width : (c + 1) * width], preferred_element_type=jnp.float32
        )
        out[:, c * width : (c + 1) * width] = part.astype(jnp.bfloat16)


def first_kernel(steps, span, *refs):
    n = len(steps)
    far, parcels, out, weight = refs[:4], refs[4 : 4 + n], refs[4 + n], refs[5 + n]
    lengths, dest, query, source, mixed, sems = refs[6 + n :]
    copies = begin(list(zip(far, (lengths, dest, query, weight))), sems)
    parcels = parcels_of(parcels, span)
    finish(copies[:3])
    invert(dest, source, n)
    at = sources(source, steps)
    results = attend(
        [query[r] for r in at],
        [parcel[0][...] for parcel in parcels],
        [parcel[1][...] for parcel in parcels],
        [lengths[r] + 1 for r in at],
    )
    for r, result in zip(at, results):
        mixed[r] = result
    copies[3].wait()
    project(mixed, weight, out)


def place(arrived, query, key_two, value_two, key_cache, value_cache, held, mixed, osems):
    count = len(arrived)
    slots = []
    lengths = []
    for parcel in arrived:
        note = last_row(parcel[0])
        lanes = lax.broadcasted_iota(jnp.int32, note.shape, 1)
        slots.append(jnp.max(jnp.where(lanes < SPLIT, note, 0.0)).astype(jnp.int32))
        lengths.append(jnp.max(jnp.where(lanes < SPLIT, 0.0, note)).astype(jnp.int32))
    for i, parcel in enumerate(arrived):
        held[0, i] = parcel[0][...]
        held[1, i] = parcel[1][...]
        put_last(held.at[0, i], row_at(parcel[0], lengths[i] + 1))
    outgoing = []
    for i in range(count):
        for which, (token, cache) in enumerate(((key_two, key_cache), (value_two, value_cache))):
            put_row(held.at[which, i], token[pl.ds(slots[i], 1), :], lengths[i] + 1)
            copy = pltpu.make_async_copy(held.at[which, i], cache.at[slots[i]], osems.at[which, i])
            copy.start()
            outgoing.append(copy)
    results = attend(
        [query[j] for j in slots],
        [held[0, i] for i in range(count)],
        [held[1, i] for i in range(count)],
        [length + 2 for length in lengths],
    )
    for j, result in zip(slots, results):
        mixed[j] = result
    return outgoing


def early_kernel(count, span, *refs):
    arrived, far = refs[:count], refs[count : count + 3]
    key_cache, value_cache, mixed, query, new_k, new_v = refs[count + 3 : count + 9]
    key_two, value_two, held, sems, osems = refs[-5:]
    copies = begin(list(zip(far, (query, key_two, value_two))), sems)
    finish(copies)
    new_k[...] = key_two[...].astype(jnp.float32)
    new_v[...] = value_two[...].astype(jnp.float32)
    parcels = parcels_of(arrived, span)
    finish(place(parcels, query, new_k, new_v, key_cache, value_cache, held, mixed, osems))


def late_kernel(count, span, *refs):
    arrived, (query, new_k, new_v, weight, before) = refs[:count], refs[count : count + 5]
    out, key_cache, value_cache, held, mixed, osems = refs[count + 7 :]
    mixed[...] = before[...]
    parcels = parcels_of(arrived, span)
    outgoing = place(parcels, query, new_k, new_v, key_cache, value_cache, held, mixed, osems)
    project(mixed, weight, out)
    finish(outgoing)


def total(partial, size):
    if size == 2:
        other = lax.ppermute(partial, "tp", [(0, 1), (1, 0)])
        return (partial.astype(jnp.float32) + other.astype(jnp.float32)).astype(jnp.bfloat16)
    return lax.psum(partial, "tp")


def near(x):
    return pltpu.with_memory_space_constraint(x, pltpu.VMEM)


def hbm(x):
    return pltpu.with_memory_space_constraint(x, pltpu.HBM)


def step_order(n):
    down = range(n // Z - 1, -1, -1)
    turns = [(a, b) for b in down for a in (1, 3)]
    return [(2, 0)] + turns + [(a, b) for b in down if b for a in (0, 2)]


def target(at, step, n):
    part = n // Z
    return (at // part + step[0]) % Z * part + (at % part ^ step[1])


def shards(
    n,
    tp,
    query_one,
    key_one,
    value_one,
    key_pages,
    value_pages,
    page_table,
    lengths,
    dest_instance,
    dest_slot,
    query_two,
    key_two,
    value_two,
    out_weight,
):
    slots, pages = page_table.shape
    pool, kv_heads, size, width = key_pages.shape
    heads = query_one.shape[1]
    depth, columns = out_weight.shape
    span = pages * size
    assert kv_heads == 1 and slots == n and n % 16 == 0 and span <= 256
    key_pages = key_pages.reshape(pool, size, width)
    value_pages = value_pages.reshape(pool, size, width)
    key_one = key_one.reshape(slots, width)
    value_one = value_one.reshape(slots, width)
    key_two = key_two.reshape(slots, width)
    value_two = value_two.reshape(slots, width)

    vmem = pl.BlockSpec(memory_space=pltpu.VMEM)
    far = pl.BlockSpec(memory_space=pltpu.HBM)
    params = pltpu.CompilerParams(vmem_limit_bytes=VMEM_BYTES)
    bf16, f32, i32 = jnp.bfloat16, jnp.float32, jnp.int32
    rows = 2 * span
    order = step_order(n)
    steps = [0] + order

    def block(height):
        return jax.ShapeDtypeStruct((height, width), bf16)

    shapes = [block(rows)] * n

    def pack(chosen):
        return pl.pallas_call(
            functools.partial(pack_kernel, n, chosen, pages),
            out_shape=[jax.ShapeDtypeStruct((rows, width), bf16)] * len(chosen),
            in_specs=[far] * 8,
            out_specs=[vmem] * len(chosen),
            scratch_shapes=[
                pltpu.SMEM((pages, slots), i32),
                pltpu.SMEM((slots,), i32),
                pltpu.SMEM((slots,), i32),
                pltpu.SMEM((slots,), i32),
                pltpu.VMEM((slots, width), bf16),
                pltpu.VMEM((slots, width), bf16),
                pltpu.VMEM((pool, size, width), bf16),
                pltpu.VMEM((pool, size, width), bf16),
                pltpu.SMEM((n,), i32),
                pltpu.SemaphoreType.DMA((8,)),
            ],
            compiler_params=params,
            cost_estimate=pl.CostEstimate(
                flops=0, bytes_accessed=4 * len(chosen) * rows * width, transcendentals=0
            ),
            name="pack",
        )(
            hbm(page_table.T),
            hbm(lengths),
            hbm(dest_instance),
            hbm(dest_slot),
            hbm(key_one),
            hbm(value_one),
            hbm(key_pages),
            hbm(value_pages),
        )

    steps = step_order(n) + [(0, 0)]
    packed = pack(steps[:AHEAD]) + pack(steps[AHEAD:])

    flops = 4 * slots * heads * span * width + 2 * slots * depth * columns
    moved = 2 * depth * columns + 4 * slots * span * width
    def send(i, *after):
        block = lax.optimization_barrier((packed[i], *after))[0] if after else packed[i]
        return lax.ppermute(block, "inst", [(d, target(d, steps[i], n)) for d in range(n)])

    arrived = [send(i) for i in range(AHEAD)]
    partial_one, weight = pl.pallas_call(
        functools.partial(first_kernel, steps, span),
        out_shape=[
            jax.ShapeDtypeStruct((slots, columns), bf16),
            jax.ShapeDtypeStruct((depth, columns), bf16),
        ],
        in_specs=[far] * 4 + [vmem] * len(shapes),
        out_specs=[vmem, vmem],
        scratch_shapes=[
            pltpu.SMEM((slots,), i32),
            pltpu.SMEM((slots,), i32),
            pltpu.VMEM((slots, heads, width), bf16),
            pltpu.SMEM((n,), i32),
            pltpu.VMEM((slots, heads, width), f32),
            pltpu.SemaphoreType.DMA((4,)),
        ],
        compiler_params=params,
        cost_estimate=pl.CostEstimate(flops=flops, bytes_accessed=moved, transcendentals=slots * heads * span),
        name="first",
    )(hbm(lengths), hbm(dest_instance), hbm(query_one), hbm(out_weight), *packed)

    arrived += [send(i, partial_one) for i in range(AHEAD, n - 1)]
    early, late = [packed[-1]] + arrived[:-LATE], arrived[-LATE:]
    cache = jax.ShapeDtypeStruct((slots, span, width), bf16)
    mixed = jax.ShapeDtypeStruct((slots, heads, width), f32)
    some = len(early)
    results = pl.pallas_call(
        functools.partial(early_kernel, some, span),
        out_shape=[cache, cache, mixed]
        + [jax.ShapeDtypeStruct((slots, heads, width), bf16)]
        + [jax.ShapeDtypeStruct((slots, width), f32)] * 2,
        in_specs=[vmem] * some + [far] * 3,
        out_specs=[far, far] + [vmem] * 4,
        scratch_shapes=[
            pltpu.VMEM((slots, width), bf16),
            pltpu.VMEM((slots, width), bf16),
            pltpu.VMEM((2, some, span, width), bf16),
            pltpu.SemaphoreType.DMA((3,)),
            pltpu.SemaphoreType.DMA((2, some)),
        ],
        compiler_params=params,
        cost_estimate=pl.CostEstimate(
            flops=4 * some * heads * span * width,
            bytes_accessed=8 * some * span * width,
            transcendentals=some * heads * span,
        ),
        name="early",
    )(*early, hbm(query_two), hbm(key_two), hbm(value_two))
    key_cache, value_cache, *carried = results
    partial_one = lax.optimization_barrier((partial_one, carried[0]))[0]
    out_one = total(partial_one, tp)

    partial_two, key_cache, value_cache = pl.pallas_call(
        functools.partial(late_kernel, LATE, span),
        out_shape=[jax.ShapeDtypeStruct((slots, columns), bf16), cache, cache],
        in_specs=[vmem] * (len(late) + 5) + [far] * 2,
        out_specs=[vmem, far, far],
        input_output_aliases={len(late) + 5: 1, len(late) + 6: 2},
        scratch_shapes=[
            pltpu.VMEM((2, LATE, span, width), bf16),
            pltpu.VMEM((slots, heads, width), f32),
            pltpu.SemaphoreType.DMA((2, LATE)),
        ],
        compiler_params=params,
        cost_estimate=pl.CostEstimate(flops=flops, bytes_accessed=moved, transcendentals=LATE * heads * span),
        name="late",
    )(
        *late,
        *[near(x) for x in carried[1:]],
        near(weight),
        near(carried[0]),
        hbm(key_cache),
        hbm(value_cache),
    )
    out_two = total(partial_two, tp)
    shape = (slots * pages, kv_heads, size, width)
    return (out_one, out_two, key_cache.reshape(shape), value_cache.reshape(shape))


def solution(mesh):
    sizes = dict(mesh.shape)
    return jax.shard_map(
        functools.partial(shards, sizes["inst"], sizes["tp"]),
        mesh=mesh,
        in_specs=(
            P("inst", "tp", None),
            P("inst", "tp", None),
            P("inst", "tp", None),
            P("inst", "tp", None, None),
            P("inst", "tp", None, None),
            P("inst", None),
            P("inst"),
            P("inst"),
            P("inst"),
            P("inst", "tp", None),
            P("inst", "tp", None),
            P("inst", "tp", None),
            P("tp", None),
        ),
        out_specs=(
            P("inst", None),
            P("inst", None),
            P("inst", "tp", None, None),
            P("inst", "tp", None, None),
        ),
        check_vma=False,
    )
```

```python
import functools

import jax
import jax.numpy as jnp
from jax import lax
from jax.experimental import pallas as pl
from jax.experimental.pallas import tpu as pltpu
from jax.sharding import PartitionSpec as P

NEG = -1e30
TILE = 16
SPLIT = 64
CHUNKS = 8
AHEAD = 5
LATE = 5
VMEM_BYTES = 24 * 1024 * 1024


def row_of(block, at):
    rows = lax.broadcasted_iota(jnp.int32, block.shape, 0)
    return jnp.sum(jnp.where(rows == at, block, 0.0), axis=0, keepdims=True)


def row_at(block, position):
    base = pl.multiple_of(position // TILE * TILE, TILE)
    return row_of(block[pl.ds(base, TILE), :].astype(jnp.float32), position % TILE)


def put_row(block, row, position):
    base = pl.multiple_of(position // TILE * TILE, TILE)
    part = block[pl.ds(base, TILE), :]
    at = lax.broadcasted_iota(jnp.int32, part.shape, 0)
    mixed = jnp.where(at == position % TILE, row, part.astype(jnp.float32))
    block[pl.ds(base, TILE), :] = mixed.astype(jnp.bfloat16)


def put_last(block, row):
    end = block.shape[0]
    part = block[end - TILE : end, :]
    at = lax.broadcasted_iota(jnp.int32, part.shape, 0)
    mixed = jnp.where(at == TILE - 1, row, part.astype(jnp.float32))
    block[end - TILE : end, :] = mixed.astype(jnp.bfloat16)


def last_row(block):
    end = block.shape[0]
    return block[end - TILE : end, :].astype(jnp.float32)[TILE - 1 : TILE, :]


def invert(dest, source, n):
    def note(r, carry):
        source[dest[r]] = r
        return carry

    lax.fori_loop(0, n, note, 0)


def begin(pairs, sem):
    copies = [pltpu.make_async_copy(a, b, sem.at[i]) for i, (a, b) in enumerate(pairs)]
    for copy in copies:
        copy.start()
    return copies


def finish(copies):
    for copy in copies:
        copy.wait()


def parcels_of(refs, span):
    return [(ref.at[pl.ds(0, span)], ref.at[pl.ds(span, span)]) for ref in refs]


def sources(source, steps):
    me = lax.axis_index("inst")
    return [source[me ^ s] for s in steps]


def pack_kernel(n, steps, pages, *refs):
    count = len(steps)
    far, outs = refs[:8], refs[8 : 8 + count]
    table, lengths, dest, slot, key_one, value_one, key_pool, value_pool, source, sems = refs[8 + count :]
    copies = begin(list(zip(far, (table, lengths, dest, slot, key_one, value_one, key_pool, value_pool))), sems)
    size = key_pool.shape[1]
    parcels = parcels_of(outs, pages * size)
    finish(copies[:6])
    invert(dest, source, n)
    at = sources(source, steps)
    tokens = (key_one[...].astype(jnp.float32), value_one[...].astype(jnp.float32))
    lanes = lax.broadcasted_iota(jnp.int32, (1, key_one.shape[1]), 1)
    for which, pool in ((0, key_pool), (1, value_pool)):
        copies[6 + which].wait()
        for r, parcel in zip(at, parcels):
            for p in range(pages):
                parcel[which][p * size : (p + 1) * size, :] = pool[table[p, r]]
            put_row(parcel[which], row_of(tokens[which], r), lengths[r])
            if which == 0:
                put_row(parcel[0], last_row(parcel[0]), lengths[r] + 1)
                note = jnp.where(lanes < SPLIT, slot[r], lengths[r]).astype(jnp.float32)
                put_last(parcel[0], note)


def attend(queries, keys, values, counts):
    width = queries[0].shape[1]
    scores = []
    for q, k, count in zip(queries, keys, counts):
        s = lax.dot_general(q, k, (((1,), (1,)), ((), ())), preferred_element_type=jnp.float32)
        live = lax.broadcasted_iota(jnp.int32, s.shape, 1) < count
        scores.append(jnp.where(live, s * width ** (-0.5), NEG))
    group = scores[0].shape[0]
    score = jnp.concatenate(scores, axis=0)
    top = jnp.max(score, axis=-1, keepdims=True)
    expo = jnp.exp(score - top)
    weights = (expo / jnp.sum(expo, axis=-1, keepdims=True)).astype(jnp.bfloat16)
    return [
        jnp.dot(weights[i * group : (i + 1) * group], v, preferred_element_type=jnp.float32)
        for i, v in enumerate(values)
    ]


def project(mixed, weight, out):
    heads = mixed.shape[1]
    rows = jnp.concatenate([mixed[:, h, :] for h in range(heads)], axis=1).astype(jnp.bfloat16)
    width = weight.shape[1] // CHUNKS
    for c in range(CHUNKS):
        part = jnp.dot(
            rows, weight[:, c * width : (c + 1) * width], preferred_element_type=jnp.float32
        )
        out[:, c * width : (c + 1) * width] = part.astype(jnp.bfloat16)


def first_kernel(steps, span, *refs):
    n = len(steps)
    far, parcels, out, weight = refs[:4], refs[4 : 4 + n], refs[4 + n], refs[5 + n]
    lengths, dest, query, source, mixed, sems = refs[6 + n :]
    copies = begin(list(zip(far, (lengths, dest, query, weight))), sems)
    parcels = parcels_of(parcels, span)
    finish(copies[:3])
    invert(dest, source, n)
    at = sources(source, steps)
    results = attend(
        [query[r] for r in at],
        [parcel[0][...] for parcel in parcels],
        [parcel[1][...] for parcel in parcels],
        [lengths[r] + 1 for r in at],
    )
    for r, result in zip(at, results):
        mixed[r] = result
    copies[3].wait()
    project(mixed, weight, out)


def place(arrived, query, key_two, value_two, key_cache, value_cache, held, mixed, osems):
    count = len(arrived)
    slots = []
    lengths = []
    for parcel in arrived:
        note = last_row(parcel[0])
        lanes = lax.broadcasted_iota(jnp.int32, note.shape, 1)
        slots.append(jnp.max(jnp.where(lanes < SPLIT, note, 0.0)).astype(jnp.int32))
        lengths.append(jnp.max(jnp.where(lanes < SPLIT, 0.0, note)).astype(jnp.int32))
    for i, parcel in enumerate(arrived):
        held[0, i] = parcel[0][...]
        held[1, i] = parcel[1][...]
        put_last(held.at[0, i], row_at(parcel[0], lengths[i] + 1))
    outgoing = []
    for i in range(count):
        for which, (token, cache) in enumerate(((key_two, key_cache), (value_two, value_cache))):
            put_row(held.at[which, i], token[pl.ds(slots[i], 1), :], lengths[i] + 1)
            copy = pltpu.make_async_copy(held.at[which, i], cache.at[slots[i]], osems.at[which, i])
            copy.start()
            outgoing.append(copy)
    results = attend(
        [query[j] for j in slots],
        [held[0, i] for i in range(count)],
        [held[1, i] for i in range(count)],
        [length + 2 for length in lengths],
    )
    for j, result in zip(slots, results):
        mixed[j] = result
    return outgoing


def early_kernel(count, span, *refs):
    arrived, far = refs[:count], refs[count : count + 3]
    key_cache, value_cache, mixed, query, new_k, new_v = refs[count + 3 : count + 9]
    key_two, value_two, held, sems, osems = refs[-5:]
    copies = begin(list(zip(far, (query, key_two, value_two))), sems)
    finish(copies)
    new_k[...] = key_two[...].astype(jnp.float32)
    new_v[...] = value_two[...].astype(jnp.float32)
    parcels = parcels_of(arrived, span)
    finish(place(parcels, query, new_k, new_v, key_cache, value_cache, held, mixed, osems))


def late_kernel(count, span, *refs):
    arrived, (query, new_k, new_v, weight, before) = refs[:count], refs[count : count + 5]
    out, key_cache, value_cache, held, mixed, osems = refs[count + 7 :]
    mixed[...] = before[...]
    parcels = parcels_of(arrived, span)
    outgoing = place(parcels, query, new_k, new_v, key_cache, value_cache, held, mixed, osems)
    project(mixed, weight, out)
    finish(outgoing)


def total(partial, size):
    if size == 2:
        other = lax.ppermute(partial, "tp", [(0, 1), (1, 0)])
        return (partial.astype(jnp.float32) + other.astype(jnp.float32)).astype(jnp.bfloat16)
    return lax.psum(partial, "tp")


def near(x):
    return pltpu.with_memory_space_constraint(x, pltpu.VMEM)


def hbm(x):
    return pltpu.with_memory_space_constraint(x, pltpu.HBM)


def step_order(n):
    half = n // 2
    crossing = list(range(half, n))
    staying = list(range(1, half))
    order = []
    for kind in "cncncncncncncnc":
        queue = crossing if kind == "c" else staying
        if queue:
            order.append(queue.pop(0))
    while crossing or staying:
        order += crossing[:1] + staying[:1]
        del crossing[:1], staying[:1]
    return order


def shards(
    n,
    tp,
    query_one,
    key_one,
    value_one,
    key_pages,
    value_pages,
    page_table,
    lengths,
    dest_instance,
    dest_slot,
    query_two,
    key_two,
    value_two,
    out_weight,
):
    slots, pages = page_table.shape
    pool, kv_heads, size, width = key_pages.shape
    heads = query_one.shape[1]
    depth, columns = out_weight.shape
    span = pages * size
    assert kv_heads == 1 and slots == n and n >= 16 and span <= 256
    key_pages = key_pages.reshape(pool, size, width)
    value_pages = value_pages.reshape(pool, size, width)
    key_one = key_one.reshape(slots, width)
    value_one = value_one.reshape(slots, width)
    key_two = key_two.reshape(slots, width)
    value_two = value_two.reshape(slots, width)

    vmem = pl.BlockSpec(memory_space=pltpu.VMEM)
    far = pl.BlockSpec(memory_space=pltpu.HBM)
    params = pltpu.CompilerParams(vmem_limit_bytes=VMEM_BYTES)
    bf16, f32, i32 = jnp.bfloat16, jnp.float32, jnp.int32
    rows = 2 * span
    order = step_order(n)
    steps = [0] + order

    def block(height):
        return jax.ShapeDtypeStruct((height, width), bf16)

    shapes = [block(rows)] * n

    def pack(chosen):
        return pl.pallas_call(
            functools.partial(pack_kernel, n, chosen, pages),
            out_shape=[jax.ShapeDtypeStruct((rows, width), bf16)] * len(chosen),
            in_specs=[far] * 8,
            out_specs=[vmem] * len(chosen),
            scratch_shapes=[
                pltpu.SMEM((pages, slots), i32),
                pltpu.SMEM((slots,), i32),
                pltpu.SMEM((slots,), i32),
                pltpu.SMEM((slots,), i32),
                pltpu.VMEM((slots, width), bf16),
                pltpu.VMEM((slots, width), bf16),
                pltpu.VMEM((pool, size, width), bf16),
                pltpu.VMEM((pool, size, width), bf16),
                pltpu.SMEM((n,), i32),
                pltpu.SemaphoreType.DMA((8,)),
            ],
            compiler_params=params,
            cost_estimate=pl.CostEstimate(
                flops=0, bytes_accessed=4 * len(chosen) * rows * width, transcendentals=0
            ),
            name="pack",
        )(
            hbm(page_table.T),
            hbm(lengths),
            hbm(dest_instance),
            hbm(dest_slot),
            hbm(key_one),
            hbm(value_one),
            hbm(key_pages),
            hbm(value_pages),
        )

    steps = step_order(n) + [0]
    packed = pack(steps[:AHEAD]) + pack(steps[AHEAD:])

    flops = 4 * slots * heads * span * width + 2 * slots * depth * columns
    moved = 2 * depth * columns + 4 * slots * span * width
    def send(i, *after):
        block = lax.optimization_barrier((packed[i], *after))[0] if after else packed[i]
        return lax.ppermute(block, "inst", [(d, d ^ steps[i]) for d in range(n)])

    arrived = [send(i) for i in range(AHEAD)]
    partial_one, weight = pl.pallas_call(
        functools.partial(first_kernel, steps, span),
        out_shape=[
            jax.ShapeDtypeStruct((slots, columns), bf16),
            jax.ShapeDtypeStruct((depth, columns), bf16),
        ],
        in_specs=[far] * 4 + [vmem] * len(shapes),
        out_specs=[vmem, vmem],
        scratch_shapes=[
            pltpu.SMEM((slots,), i32),
            pltpu.SMEM((slots,), i32),
            pltpu.VMEM((slots, heads, width), bf16),
            pltpu.SMEM((n,), i32),
            pltpu.VMEM((slots, heads, width), f32),
            pltpu.SemaphoreType.DMA((4,)),
        ],
        compiler_params=params,
        cost_estimate=pl.CostEstimate(flops=flops, bytes_accessed=moved, transcendentals=slots * heads * span),
        name="first",
    )(hbm(lengths), hbm(dest_instance), hbm(query_one), hbm(out_weight), *packed)

    arrived += [send(i, partial_one) for i in range(AHEAD, n - 1)]
    early, late = [packed[-1]] + arrived[:-LATE], arrived[-LATE:]
    cache = jax.ShapeDtypeStruct((slots, span, width), bf16)
    mixed = jax.ShapeDtypeStruct((slots, heads, width), f32)
    some = len(early)
    results = pl.pallas_call(
        functools.partial(early_kernel, some, span),
        out_shape=[cache, cache, mixed]
        + [jax.ShapeDtypeStruct((slots, heads, width), bf16)]
        + [jax.ShapeDtypeStruct((slots, width), f32)] * 2,
        in_specs=[vmem] * some + [far] * 3,
        out_specs=[far, far] + [vmem] * 4,
        scratch_shapes=[
            pltpu.VMEM((slots, width), bf16),
            pltpu.VMEM((slots, width), bf16),
            pltpu.VMEM((2, some, span, width), bf16),
            pltpu.SemaphoreType.DMA((3,)),
            pltpu.SemaphoreType.DMA((2, some)),
        ],
        compiler_params=params,
        cost_estimate=pl.CostEstimate(
            flops=4 * some * heads * span * width,
            bytes_accessed=8 * some * span * width,
            transcendentals=some * heads * span,
        ),
        name="early",
    )(*early, hbm(query_two), hbm(key_two), hbm(value_two))
    key_cache, value_cache, *carried = results
    partial_one = lax.optimization_barrier((partial_one, carried[0]))[0]
    out_one = total(partial_one, tp)

    partial_two, key_cache, value_cache = pl.pallas_call(
        functools.partial(late_kernel, LATE, span),
        out_shape=[jax.ShapeDtypeStruct((slots, columns), bf16), cache, cache],
        in_specs=[vmem] * (len(late) + 5) + [far] * 2,
        out_specs=[vmem, far, far],
        input_output_aliases={len(late) + 5: 1, len(late) + 6: 2},
        scratch_shapes=[
            pltpu.VMEM((2, LATE, span, width), bf16),
            pltpu.VMEM((slots, heads, width), f32),
            pltpu.SemaphoreType.DMA((2, LATE)),
        ],
        compiler_params=params,
        cost_estimate=pl.CostEstimate(flops=flops, bytes_accessed=moved, transcendentals=LATE * heads * span),
        name="late",
    )(
        *late,
        *[near(x) for x in carried[1:]],
        near(weight),
        near(carried[0]),
        hbm(key_cache),
        hbm(value_cache),
    )
    out_two = total(partial_two, tp)
    shape = (slots * pages, kv_heads, size, width)
    return (out_one, out_two, key_cache.reshape(shape), value_cache.reshape(shape))


def solution(mesh):
    sizes = dict(mesh.shape)
    return jax.shard_map(
        functools.partial(shards, sizes["inst"], sizes["tp"]),
        mesh=mesh,
        in_specs=(
            P("inst", "tp", None),
            P("inst", "tp", None),
            P("inst", "tp", None),
            P("inst", "tp", None, None),
            P("inst", "tp", None, None),
            P("inst", None),
            P("inst"),
            P("inst"),
            P("inst"),
            P("inst", "tp", None),
            P("inst", "tp", None),
            P("inst", "tp", None),
            P("tp", None),
        ),
        out_specs=(
            P("inst", None),
            P("inst", None),
            P("inst", "tp", None, None),
            P("inst", "tp", None, None),
        ),
        check_vma=False,
    )
```

```python
import functools

import jax
import jax.numpy as jnp
from jax import lax
from jax.experimental import pallas as pl
from jax.experimental.pallas import tpu as pltpu
from jax.sharding import PartitionSpec as P

NEG = -1e30
TILE = 16
SPLIT = 64
CHUNKS = 8
AHEAD = 5
LATE = 5
VMEM_BYTES = 24 * 1024 * 1024


def row_of(block, at):
    rows = lax.broadcasted_iota(jnp.int32, block.shape, 0)
    return jnp.sum(jnp.where(rows == at, block, 0.0), axis=0, keepdims=True)


def row_at(block, position):
    base = pl.multiple_of(position // TILE * TILE, TILE)
    return row_of(block[pl.ds(base, TILE), :].astype(jnp.float32), position % TILE)


def put_row(block, row, position):
    base = pl.multiple_of(position // TILE * TILE, TILE)
    part = block[pl.ds(base, TILE), :]
    at = lax.broadcasted_iota(jnp.int32, part.shape, 0)
    mixed = jnp.where(at == position % TILE, row, part.astype(jnp.float32))
    block[pl.ds(base, TILE), :] = mixed.astype(jnp.bfloat16)


def put_last(block, row):
    end = block.shape[0]
    part = block[end - TILE : end, :]
    at = lax.broadcasted_iota(jnp.int32, part.shape, 0)
    mixed = jnp.where(at == TILE - 1, row, part.astype(jnp.float32))
    block[end - TILE : end, :] = mixed.astype(jnp.bfloat16)


def last_row(block):
    end = block.shape[0]
    return block[end - TILE : end, :].astype(jnp.float32)[TILE - 1 : TILE, :]


def invert(dest, source, n):
    def note(r, carry):
        source[dest[r]] = r
        return carry

    lax.fori_loop(0, n, note, 0)


def begin(pairs, sem):
    copies = [pltpu.make_async_copy(a, b, sem.at[i]) for i, (a, b) in enumerate(pairs)]
    for copy in copies:
        copy.start()
    return copies


def finish(copies):
    for copy in copies:
        copy.wait()


def parcels_of(refs, span):
    return [(ref.at[pl.ds(0, span)], ref.at[pl.ds(span, span)]) for ref in refs]


def sources(source, steps):
    me = lax.axis_index("inst")
    return [source[me ^ s] for s in steps]


def pack_kernel(n, steps, pages, *refs):
    count = len(steps)
    far, outs = refs[:8], refs[8 : 8 + count]
    table, lengths, dest, slot, key_one, value_one, key_pool, value_pool, source, sems = refs[8 + count :]
    copies = begin(list(zip(far, (table, lengths, dest, slot, key_one, value_one, key_pool, value_pool))), sems)
    size = key_pool.shape[1]
    parcels = parcels_of(outs, pages * size)
    finish(copies[:6])
    invert(dest, source, n)
    at = sources(source, steps)
    tokens = (key_one[...].astype(jnp.float32), value_one[...].astype(jnp.float32))
    lanes = lax.broadcasted_iota(jnp.int32, (1, key_one.shape[1]), 1)
    for which, pool in ((0, key_pool), (1, value_pool)):
        copies[6 + which].wait()
        for r, parcel in zip(at, parcels):
            for p in range(pages):
                parcel[which][p * size : (p + 1) * size, :] = pool[table[p, r]]
            put_row(parcel[which], row_of(tokens[which], r), lengths[r])
            if which == 0:
                put_row(parcel[0], last_row(parcel[0]), lengths[r] + 1)
                note = jnp.where(lanes < SPLIT, slot[r], lengths[r]).astype(jnp.float32)
                put_last(parcel[0], note)


def attend(queries, keys, values, counts):
    width = queries[0].shape[1]
    scores = []
    for q, k, count in zip(queries, keys, counts):
        s = lax.dot_general(q, k, (((1,), (1,)), ((), ())), preferred_element_type=jnp.float32)
        live = lax.broadcasted_iota(jnp.int32, s.shape, 1) < count
        scores.append(jnp.where(live, s * width ** (-0.5), NEG))
    group = scores[0].shape[0]
    score = jnp.concatenate(scores, axis=0)
    top = jnp.max(score, axis=-1, keepdims=True)
    expo = jnp.exp(score - top)
    weights = (expo / jnp.sum(expo, axis=-1, keepdims=True)).astype(jnp.bfloat16)
    return [
        jnp.dot(weights[i * group : (i + 1) * group], v, preferred_element_type=jnp.float32)
        for i, v in enumerate(values)
    ]


def project(mixed, weight, out):
    heads = mixed.shape[1]
    rows = jnp.concatenate([mixed[:, h, :] for h in range(heads)], axis=1).astype(jnp.bfloat16)
    width = weight.shape[1] // CHUNKS
    for c in range(CHUNKS):
        part = jnp.dot(
            rows, weight[:, c * width : (c + 1) * width], preferred_element_type=jnp.float32
        )
        out[:, c * width : (c + 1) * width] = part.astype(jnp.bfloat16)


def first_kernel(steps, span, *refs):
    n = len(steps)
    far, parcels, out, weight = refs[:4], refs[4 : 4 + n], refs[4 + n], refs[5 + n]
    lengths, dest, query, source, mixed, sems = refs[6 + n :]
    copies = begin(list(zip(far, (lengths, dest, query, weight))), sems)
    parcels = parcels_of(parcels, span)
    finish(copies[:3])
    invert(dest, source, n)
    at = sources(source, steps)
    results = attend(
        [query[r] for r in at],
        [parcel[0][...] for parcel in parcels],
        [parcel[1][...] for parcel in parcels],
        [lengths[r] + 1 for r in at],
    )
    for r, result in zip(at, results):
        mixed[r] = result
    copies[3].wait()
    project(mixed, weight, out)


def place(arrived, query, key_two, value_two, key_cache, value_cache, held, mixed, osems):
    count = len(arrived)
    slots = []
    lengths = []
    for parcel in arrived:
        note = last_row(parcel[0])
        lanes = lax.broadcasted_iota(jnp.int32, note.shape, 1)
        slots.append(jnp.max(jnp.where(lanes < SPLIT, note, 0.0)).astype(jnp.int32))
        lengths.append(jnp.max(jnp.where(lanes < SPLIT, 0.0, note)).astype(jnp.int32))
    for i, parcel in enumerate(arrived):
        held[0, i] = parcel[0][...]
        held[1, i] = parcel[1][...]
        put_last(held.at[0, i], row_at(parcel[0], lengths[i] + 1))
    outgoing = []
    for i in range(count):
        for which, (token, cache) in enumerate(((key_two, key_cache), (value_two, value_cache))):
            put_row(held.at[which, i], token[pl.ds(slots[i], 1), :], lengths[i] + 1)
            copy = pltpu.make_async_copy(held.at[which, i], cache.at[slots[i]], osems.at[which, i])
            copy.start()
            outgoing.append(copy)
    results = attend(
        [query[j] for j in slots],
        [held[0, i] for i in range(count)],
        [held[1, i] for i in range(count)],
        [length + 2 for length in lengths],
    )
    for j, result in zip(slots, results):
        mixed[j] = result
    return outgoing


def early_kernel(count, span, *refs):
    arrived, far = refs[:count], refs[count : count + 3]
    key_cache, value_cache, mixed, query, new_k, new_v = refs[count + 3 : count + 9]
    key_two, value_two, held, sems, osems = refs[-5:]
    copies = begin(list(zip(far, (query, key_two, value_two))), sems)
    finish(copies)
    new_k[...] = key_two[...].astype(jnp.float32)
    new_v[...] = value_two[...].astype(jnp.float32)
    parcels = parcels_of(arrived, span)
    finish(place(parcels, query, new_k, new_v, key_cache, value_cache, held, mixed, osems))


def late_kernel(count, span, *refs):
    arrived, (query, new_k, new_v, weight, before) = refs[:count], refs[count : count + 5]
    out, key_cache, value_cache, held, mixed, osems = refs[count + 7 :]
    mixed[...] = before[...]
    parcels = parcels_of(arrived, span)
    outgoing = place(parcels, query, new_k, new_v, key_cache, value_cache, held, mixed, osems)
    project(mixed, weight, out)
    finish(outgoing)


def total(partial, size):
    if size == 2:
        other = lax.ppermute(partial, "tp", [(0, 1), (1, 0)])
        return (partial.astype(jnp.float32) + other.astype(jnp.float32)).astype(jnp.bfloat16)
    return lax.psum(partial, "tp")


def near(x):
    return pltpu.with_memory_space_constraint(x, pltpu.VMEM)


def hbm(x):
    return pltpu.with_memory_space_constraint(x, pltpu.HBM)


def step_order(n):
    half = n // 2
    crossing = list(range(half, n))
    staying = list(range(1, half))
    for queue, at in ((crossing, half // 2), (staying, half // 4)):
        queue[at], queue[-1] = queue[-1], queue[at]
    order = []
    for kind in "cncncncncncncnc":
        queue = crossing if kind == "c" else staying
        if queue:
            order.append(queue.pop(0))
    while crossing or staying:
        order += crossing[:1] + staying[:1]
        del crossing[:1], staying[:1]
    return order


def shards(
    n,
    tp,
    query_one,
    key_one,
    value_one,
    key_pages,
    value_pages,
    page_table,
    lengths,
    dest_instance,
    dest_slot,
    query_two,
    key_two,
    value_two,
    out_weight,
):
    slots, pages = page_table.shape
    pool, kv_heads, size, width = key_pages.shape
    heads = query_one.shape[1]
    depth, columns = out_weight.shape
    span = pages * size
    assert kv_heads == 1 and slots == n and n >= 16 and span <= 256
    key_pages = key_pages.reshape(pool, size, width)
    value_pages = value_pages.reshape(pool, size, width)
    key_one = key_one.reshape(slots, width)
    value_one = value_one.reshape(slots, width)
    key_two = key_two.reshape(slots, width)
    value_two = value_two.reshape(slots, width)

    vmem = pl.BlockSpec(memory_space=pltpu.VMEM)
    far = pl.BlockSpec(memory_space=pltpu.HBM)
    params = pltpu.CompilerParams(vmem_limit_bytes=VMEM_BYTES)
    bf16, f32, i32 = jnp.bfloat16, jnp.float32, jnp.int32
    rows = 2 * span
    order = step_order(n)
    steps = [0] + order

    def block(height):
        return jax.ShapeDtypeStruct((height, width), bf16)

    shapes = [block(rows)] * n

    def pack(chosen):
        return pl.pallas_call(
            functools.partial(pack_kernel, n, chosen, pages),
            out_shape=[jax.ShapeDtypeStruct((rows, width), bf16)] * len(chosen),
            in_specs=[far] * 8,
            out_specs=[vmem] * len(chosen),
            scratch_shapes=[
                pltpu.SMEM((pages, slots), i32),
                pltpu.SMEM((slots,), i32),
                pltpu.SMEM((slots,), i32),
                pltpu.SMEM((slots,), i32),
                pltpu.VMEM((slots, width), bf16),
                pltpu.VMEM((slots, width), bf16),
                pltpu.VMEM((pool, size, width), bf16),
                pltpu.VMEM((pool, size, width), bf16),
                pltpu.SMEM((n,), i32),
                pltpu.SemaphoreType.DMA((8,)),
            ],
            compiler_params=params,
            cost_estimate=pl.CostEstimate(
                flops=0, bytes_accessed=4 * len(chosen) * rows * width, transcendentals=0
            ),
            name="pack",
        )(
            hbm(page_table.T),
            hbm(lengths),
            hbm(dest_instance),
            hbm(dest_slot),
            hbm(key_one),
            hbm(value_one),
            hbm(key_pages),
            hbm(value_pages),
        )

    steps = step_order(n) + [0]
    packed = pack(steps[:AHEAD]) + pack(steps[AHEAD:])

    flops = 4 * slots * heads * span * width + 2 * slots * depth * columns
    moved = 2 * depth * columns + 4 * slots * span * width
    def send(i, *after):
        block = lax.optimization_barrier((packed[i], *after))[0] if after else packed[i]
        return lax.ppermute(block, "inst", [(d, d ^ steps[i]) for d in range(n)])

    arrived = [send(i) for i in range(AHEAD)]
    partial_one, weight = pl.pallas_call(
        functools.partial(first_kernel, steps, span),
        out_shape=[
            jax.ShapeDtypeStruct((slots, columns), bf16),
            jax.ShapeDtypeStruct((depth, columns), bf16),
        ],
        in_specs=[far] * 4 + [vmem] * len(shapes),
        out_specs=[vmem, vmem],
        scratch_shapes=[
            pltpu.SMEM((slots,), i32),
            pltpu.SMEM((slots,), i32),
            pltpu.VMEM((slots, heads, width), bf16),
            pltpu.SMEM((n,), i32),
            pltpu.VMEM((slots, heads, width), f32),
            pltpu.SemaphoreType.DMA((4,)),
        ],
        compiler_params=params,
        cost_estimate=pl.CostEstimate(flops=flops, bytes_accessed=moved, transcendentals=slots * heads * span),
        name="first",
    )(hbm(lengths), hbm(dest_instance), hbm(query_one), hbm(out_weight), *packed)

    arrived += [send(i, partial_one) for i in range(AHEAD, n - 1)]
    early, late = [packed[-1]] + arrived[:-LATE], arrived[-LATE:]
    cache = jax.ShapeDtypeStruct((slots, span, width), bf16)
    mixed = jax.ShapeDtypeStruct((slots, heads, width), f32)
    some = len(early)
    results = pl.pallas_call(
        functools.partial(early_kernel, some, span),
        out_shape=[cache, cache, mixed]
        + [jax.ShapeDtypeStruct((slots, heads, width), bf16)]
        + [jax.ShapeDtypeStruct((slots, width), f32)] * 2,
        in_specs=[vmem] * some + [far] * 3,
        out_specs=[far, far] + [vmem] * 4,
        scratch_shapes=[
            pltpu.VMEM((slots, width), bf16),
            pltpu.VMEM((slots, width), bf16),
            pltpu.VMEM((2, some, span, width), bf16),
            pltpu.SemaphoreType.DMA((3,)),
            pltpu.SemaphoreType.DMA((2, some)),
        ],
        compiler_params=params,
        cost_estimate=pl.CostEstimate(
            flops=4 * some * heads * span * width,
            bytes_accessed=8 * some * span * width,
            transcendentals=some * heads * span,
        ),
        name="early",
    )(*early, hbm(query_two), hbm(key_two), hbm(value_two))
    key_cache, value_cache, *carried = results
    partial_one = lax.optimization_barrier((partial_one, carried[0]))[0]
    out_one = total(partial_one, tp)

    partial_two, key_cache, value_cache = pl.pallas_call(
        functools.partial(late_kernel, LATE, span),
        out_shape=[jax.ShapeDtypeStruct((slots, columns), bf16), cache, cache],
        in_specs=[vmem] * (len(late) + 5) + [far] * 2,
        out_specs=[vmem, far, far],
        input_output_aliases={len(late) + 5: 1, len(late) + 6: 2},
        scratch_shapes=[
            pltpu.VMEM((2, LATE, span, width), bf16),
            pltpu.VMEM((slots, heads, width), f32),
            pltpu.SemaphoreType.DMA((2, LATE)),
        ],
        compiler_params=params,
        cost_estimate=pl.CostEstimate(flops=flops, bytes_accessed=moved, transcendentals=LATE * heads * span),
        name="late",
    )(
        *late,
        *[near(x) for x in carried[1:]],
        near(weight),
        near(carried[0]),
        hbm(key_cache),
        hbm(value_cache),
    )
    out_two = total(partial_two, tp)
    shape = (slots * pages, kv_heads, size, width)
    return (out_one, out_two, key_cache.reshape(shape), value_cache.reshape(shape))


def solution(mesh):
    sizes = dict(mesh.shape)
    return jax.shard_map(
        functools.partial(shards, sizes["inst"], sizes["tp"]),
        mesh=mesh,
        in_specs=(
            P("inst", "tp", None),
            P("inst", "tp", None),
            P("inst", "tp", None),
            P("inst", "tp", None, None),
            P("inst", "tp", None, None),
            P("inst", None),
            P("inst"),
            P("inst"),
            P("inst"),
            P("inst", "tp", None),
            P("inst", "tp", None),
            P("inst", "tp", None),
            P("tp", None),
        ),
        out_specs=(
            P("inst", None),
            P("inst", None),
            P("inst", "tp", None, None),
            P("inst", "tp", None, None),
        ),
        check_vma=False,
    )
```

```python
import functools

import jax
import jax.numpy as jnp
from jax import lax
from jax.experimental import pallas as pl
from jax.experimental.pallas import tpu as pltpu
from jax.sharding import PartitionSpec as P

NEG = -1e30
TILE = 16
SPLIT = 64
CHUNKS = 8
AHEAD = 5
LATE = 5
VMEM_BYTES = 24 * 1024 * 1024


def row_of(block, at):
    rows = lax.broadcasted_iota(jnp.int32, block.shape, 0)
    return jnp.sum(jnp.where(rows == at, block, 0.0), axis=0, keepdims=True)


def row_at(block, position):
    base = pl.multiple_of(position // TILE * TILE, TILE)
    return row_of(block[pl.ds(base, TILE), :].astype(jnp.float32), position % TILE)


def put_row(block, row, position):
    base = pl.multiple_of(position // TILE * TILE, TILE)
    part = block[pl.ds(base, TILE), :]
    at = lax.broadcasted_iota(jnp.int32, part.shape, 0)
    mixed = jnp.where(at == position % TILE, row, part.astype(jnp.float32))
    block[pl.ds(base, TILE), :] = mixed.astype(jnp.bfloat16)


def put_last(block, row):
    end = block.shape[0]
    part = block[end - TILE : end, :]
    at = lax.broadcasted_iota(jnp.int32, part.shape, 0)
    mixed = jnp.where(at == TILE - 1, row, part.astype(jnp.float32))
    block[end - TILE : end, :] = mixed.astype(jnp.bfloat16)


def last_row(block):
    end = block.shape[0]
    return block[end - TILE : end, :].astype(jnp.float32)[TILE - 1 : TILE, :]


def invert(dest, source, n):
    def note(r, carry):
        source[dest[r]] = r
        return carry

    lax.fori_loop(0, n, note, 0)


def begin(pairs, sem):
    copies = [pltpu.make_async_copy(a, b, sem.at[i]) for i, (a, b) in enumerate(pairs)]
    for copy in copies:
        copy.start()
    return copies


def finish(copies):
    for copy in copies:
        copy.wait()


def parcels_of(refs, span):
    return [(ref.at[pl.ds(0, span)], ref.at[pl.ds(span, span)]) for ref in refs]


def sources(source, steps):
    me = lax.axis_index("inst")
    return [source[me ^ s] for s in steps]


def pack_kernel(n, steps, pages, *refs):
    count = len(steps)
    far, outs = refs[:8], refs[8 : 8 + count]
    table, lengths, dest, slot, key_one, value_one, key_pool, value_pool, source, sems = refs[8 + count :]
    copies = begin(list(zip(far, (table, lengths, dest, slot, key_one, value_one, key_pool, value_pool))), sems)
    size = key_pool.shape[1]
    parcels = parcels_of(outs, pages * size)
    finish(copies[:6])
    invert(dest, source, n)
    at = sources(source, steps)
    tokens = (key_one[...].astype(jnp.float32), value_one[...].astype(jnp.float32))
    lanes = lax.broadcasted_iota(jnp.int32, (1, key_one.shape[1]), 1)
    for which, pool in ((0, key_pool), (1, value_pool)):
        copies[6 + which].wait()
        for r, parcel in zip(at, parcels):
            for p in range(pages):
                parcel[which][p * size : (p + 1) * size, :] = pool[table[p, r]]
            put_row(parcel[which], row_of(tokens[which], r), lengths[r])
            if which == 0:
                put_row(parcel[0], last_row(parcel[0]), lengths[r] + 1)
                note = jnp.where(lanes < SPLIT, slot[r], lengths[r]).astype(jnp.float32)
                put_last(parcel[0], note)


def attend(queries, keys, values, counts):
    width = queries[0].shape[1]
    scores = []
    for q, k, count in zip(queries, keys, counts):
        s = lax.dot_general(q, k, (((1,), (1,)), ((), ())), preferred_element_type=jnp.float32)
        live = lax.broadcasted_iota(jnp.int32, s.shape, 1) < count
        scores.append(jnp.where(live, s * width ** (-0.5), NEG))
    group = scores[0].shape[0]
    score = jnp.concatenate(scores, axis=0)
    top = jnp.max(score, axis=-1, keepdims=True)
    expo = jnp.exp(score - top)
    weights = (expo / jnp.sum(expo, axis=-1, keepdims=True)).astype(jnp.bfloat16)
    return [
        jnp.dot(weights[i * group : (i + 1) * group], v, preferred_element_type=jnp.float32)
        for i, v in enumerate(values)
    ]


def project(mixed, weight, out):
    heads = mixed.shape[1]
    rows = jnp.concatenate([mixed[:, h, :] for h in range(heads)], axis=1).astype(jnp.bfloat16)
    width = weight.shape[1] // CHUNKS
    for c in range(CHUNKS):
        part = jnp.dot(
            rows, weight[:, c * width : (c + 1) * width], preferred_element_type=jnp.float32
        )
        out[:, c * width : (c + 1) * width] = part.astype(jnp.bfloat16)


def first_kernel(steps, span, *refs):
    n = len(steps)
    far, parcels, out, weight = refs[:4], refs[4 : 4 + n], refs[4 + n], refs[5 + n]
    lengths, dest, query, source, mixed, sems = refs[6 + n :]
    copies = begin(list(zip(far, (lengths, dest, query, weight))), sems)
    parcels = parcels_of(parcels, span)
    finish(copies[:3])
    invert(dest, source, n)
    at = sources(source, steps)
    results = attend(
        [query[r] for r in at],
        [parcel[0][...] for parcel in parcels],
        [parcel[1][...] for parcel in parcels],
        [lengths[r] + 1 for r in at],
    )
    for r, result in zip(at, results):
        mixed[r] = result
    copies[3].wait()
    project(mixed, weight, out)


def place(arrived, query, key_two, value_two, key_cache, value_cache, held, mixed, osems):
    count = len(arrived)
    slots = []
    lengths = []
    for parcel in arrived:
        note = last_row(parcel[0])
        lanes = lax.broadcasted_iota(jnp.int32, note.shape, 1)
        slots.append(jnp.max(jnp.where(lanes < SPLIT, note, 0.0)).astype(jnp.int32))
        lengths.append(jnp.max(jnp.where(lanes < SPLIT, 0.0, note)).astype(jnp.int32))
    for i, parcel in enumerate(arrived):
        held[0, i] = parcel[0][...]
        held[1, i] = parcel[1][...]
        put_last(held.at[0, i], row_at(parcel[0], lengths[i] + 1))
    outgoing = []
    for i in range(count):
        for which, (token, cache) in enumerate(((key_two, key_cache), (value_two, value_cache))):
            put_row(held.at[which, i], token[pl.ds(slots[i], 1), :], lengths[i] + 1)
            copy = pltpu.make_async_copy(held.at[which, i], cache.at[slots[i]], osems.at[which, i])
            copy.start()
            outgoing.append(copy)
    results = attend(
        [query[j] for j in slots],
        [held[0, i] for i in range(count)],
        [held[1, i] for i in range(count)],
        [length + 2 for length in lengths],
    )
    for j, result in zip(slots, results):
        mixed[j] = result
    return outgoing


def early_kernel(count, span, *refs):
    arrived, far = refs[:count], refs[count : count + 3]
    key_cache, value_cache, mixed, query, new_k, new_v = refs[count + 3 : count + 9]
    key_two, value_two, held, sems, osems = refs[-5:]
    copies = begin(list(zip(far, (query, key_two, value_two))), sems)
    finish(copies)
    new_k[...] = key_two[...].astype(jnp.float32)
    new_v[...] = value_two[...].astype(jnp.float32)
    parcels = parcels_of(arrived, span)
    finish(place(parcels, query, new_k, new_v, key_cache, value_cache, held, mixed, osems))


def late_kernel(count, span, *refs):
    arrived, (query, new_k, new_v, weight, before) = refs[:count], refs[count : count + 5]
    out, key_cache, value_cache, held, mixed, osems = refs[count + 7 :]
    mixed[...] = before[...]
    parcels = parcels_of(arrived, span)
    outgoing = place(parcels, query, new_k, new_v, key_cache, value_cache, held, mixed, osems)
    project(mixed, weight, out)
    finish(outgoing)


def total(partial, size):
    if size == 2:
        other = lax.ppermute(partial, "tp", [(0, 1), (1, 0)])
        return (partial.astype(jnp.float32) + other.astype(jnp.float32)).astype(jnp.bfloat16)
    return lax.psum(partial, "tp")


def near(x):
    return pltpu.with_memory_space_constraint(x, pltpu.VMEM)


def hbm(x):
    return pltpu.with_memory_space_constraint(x, pltpu.HBM)


def step_order(n):
    half = n // 2
    crossing = list(range(half, n))
    staying = list(range(1, half))
    for queue, at in ((crossing, half // 2), (staying, half // 4)):
        queue[at], queue[-1] = queue[-1], queue[at]
    for queue, at in ((crossing, half // 4), (staying, half // 4 - 1)):
        queue[at], queue[-2] = queue[-2], queue[at]
    order = []
    for kind in "cncncncncncncnc":
        queue = crossing if kind == "c" else staying
        if queue:
            order.append(queue.pop(0))
    while crossing or staying:
        order += crossing[:1] + staying[:1]
        del crossing[:1], staying[:1]
    return order


def shards(
    n,
    tp,
    query_one,
    key_one,
    value_one,
    key_pages,
    value_pages,
    page_table,
    lengths,
    dest_instance,
    dest_slot,
    query_two,
    key_two,
    value_two,
    out_weight,
):
    slots, pages = page_table.shape
    pool, kv_heads, size, width = key_pages.shape
    heads = query_one.shape[1]
    depth, columns = out_weight.shape
    span = pages * size
    assert kv_heads == 1 and slots == n and n >= 16 and span <= 256
    key_pages = key_pages.reshape(pool, size, width)
    value_pages = value_pages.reshape(pool, size, width)
    key_one = key_one.reshape(slots, width)
    value_one = value_one.reshape(slots, width)
    key_two = key_two.reshape(slots, width)
    value_two = value_two.reshape(slots, width)

    vmem = pl.BlockSpec(memory_space=pltpu.VMEM)
    far = pl.BlockSpec(memory_space=pltpu.HBM)
    params = pltpu.CompilerParams(vmem_limit_bytes=VMEM_BYTES)
    bf16, f32, i32 = jnp.bfloat16, jnp.float32, jnp.int32
    rows = 2 * span
    order = step_order(n)
    steps = [0] + order

    def block(height):
        return jax.ShapeDtypeStruct((height, width), bf16)

    shapes = [block(rows)] * n

    def pack(chosen):
        return pl.pallas_call(
            functools.partial(pack_kernel, n, chosen, pages),
            out_shape=[jax.ShapeDtypeStruct((rows, width), bf16)] * len(chosen),
            in_specs=[far] * 8,
            out_specs=[vmem] * len(chosen),
            scratch_shapes=[
                pltpu.SMEM((pages, slots), i32),
                pltpu.SMEM((slots,), i32),
                pltpu.SMEM((slots,), i32),
                pltpu.SMEM((slots,), i32),
                pltpu.VMEM((slots, width), bf16),
                pltpu.VMEM((slots, width), bf16),
                pltpu.VMEM((pool, size, width), bf16),
                pltpu.VMEM((pool, size, width), bf16),
                pltpu.SMEM((n,), i32),
                pltpu.SemaphoreType.DMA((8,)),
            ],
            compiler_params=params,
            cost_estimate=pl.CostEstimate(
                flops=0, bytes_accessed=4 * len(chosen) * rows * width, transcendentals=0
            ),
            name="pack",
        )(
            hbm(page_table.T),
            hbm(lengths),
            hbm(dest_instance),
            hbm(dest_slot),
            hbm(key_one),
            hbm(value_one),
            hbm(key_pages),
            hbm(value_pages),
        )

    steps = step_order(n) + [0]
    packed = pack(steps[:AHEAD]) + pack(steps[AHEAD:])

    flops = 4 * slots * heads * span * width + 2 * slots * depth * columns
    moved = 2 * depth * columns + 4 * slots * span * width
    def send(i, *after):
        block = lax.optimization_barrier((packed[i], *after))[0] if after else packed[i]
        return lax.ppermute(block, "inst", [(d, d ^ steps[i]) for d in range(n)])

    arrived = [send(i) for i in range(AHEAD)]
    partial_one, weight = pl.pallas_call(
        functools.partial(first_kernel, steps, span),
        out_shape=[
            jax.ShapeDtypeStruct((slots, columns), bf16),
            jax.ShapeDtypeStruct((depth, columns), bf16),
        ],
        in_specs=[far] * 4 + [vmem] * len(shapes),
        out_specs=[vmem, vmem],
        scratch_shapes=[
            pltpu.SMEM((slots,), i32),
            pltpu.SMEM((slots,), i32),
            pltpu.VMEM((slots, heads, width), bf16),
            pltpu.SMEM((n,), i32),
            pltpu.VMEM((slots, heads, width), f32),
            pltpu.SemaphoreType.DMA((4,)),
        ],
        compiler_params=params,
        cost_estimate=pl.CostEstimate(flops=flops, bytes_accessed=moved, transcendentals=slots * heads * span),
        name="first",
    )(hbm(lengths), hbm(dest_instance), hbm(query_one), hbm(out_weight), *packed)

    arrived += [send(i, partial_one) for i in range(AHEAD, n - 1)]
    early, late = [packed[-1]] + arrived[:-LATE], arrived[-LATE:]
    cache = jax.ShapeDtypeStruct((slots, span, width), bf16)
    mixed = jax.ShapeDtypeStruct((slots, heads, width), f32)
    some = len(early)
    results = pl.pallas_call(
        functools.partial(early_kernel, some, span),
        out_shape=[cache, cache, mixed]
        + [jax.ShapeDtypeStruct((slots, heads, width), bf16)]
        + [jax.ShapeDtypeStruct((slots, width), f32)] * 2,
        in_specs=[vmem] * some + [far] * 3,
        out_specs=[far, far] + [vmem] * 4,
        scratch_shapes=[
            pltpu.VMEM((slots, width), bf16),
            pltpu.VMEM((slots, width), bf16),
            pltpu.VMEM((2, some, span, width), bf16),
            pltpu.SemaphoreType.DMA((3,)),
            pltpu.SemaphoreType.DMA((2, some)),
        ],
        compiler_params=params,
        cost_estimate=pl.CostEstimate(
            flops=4 * some * heads * span * width,
            bytes_accessed=8 * some * span * width,
            transcendentals=some * heads * span,
        ),
        name="early",
    )(*early, hbm(query_two), hbm(key_two), hbm(value_two))
    key_cache, value_cache, *carried = results
    partial_one = lax.optimization_barrier((partial_one, carried[0]))[0]
    out_one = total(partial_one, tp)

    partial_two, key_cache, value_cache = pl.pallas_call(
        functools.partial(late_kernel, LATE, span),
        out_shape=[jax.ShapeDtypeStruct((slots, columns), bf16), cache, cache],
        in_specs=[vmem] * (len(late) + 5) + [far] * 2,
        out_specs=[vmem, far, far],
        input_output_aliases={len(late) + 5: 1, len(late) + 6: 2},
        scratch_shapes=[
            pltpu.VMEM((2, LATE, span, width), bf16),
            pltpu.VMEM((slots, heads, width), f32),
            pltpu.SemaphoreType.DMA((2, LATE)),
        ],
        compiler_params=params,
        cost_estimate=pl.CostEstimate(flops=flops, bytes_accessed=moved, transcendentals=LATE * heads * span),
        name="late",
    )(
        *late,
        *[near(x) for x in carried[1:]],
        near(weight),
        near(carried[0]),
        hbm(key_cache),
        hbm(value_cache),
    )
    out_two = total(partial_two, tp)
    shape = (slots * pages, kv_heads, size, width)
    return (out_one, out_two, key_cache.reshape(shape), value_cache.reshape(shape))


def solution(mesh):
    sizes = dict(mesh.shape)
    return jax.shard_map(
        functools.partial(shards, sizes["inst"], sizes["tp"]),
        mesh=mesh,
        in_specs=(
            P("inst", "tp", None),
            P("inst", "tp", None),
            P("inst", "tp", None),
            P("inst", "tp", None, None),
            P("inst", "tp", None, None),
            P("inst", None),
            P("inst"),
            P("inst"),
            P("inst"),
            P("inst", "tp", None),
            P("inst", "tp", None),
            P("inst", "tp", None),
            P("tp", None),
        ),
        out_specs=(
            P("inst", None),
            P("inst", None),
            P("inst", "tp", None, None),
            P("inst", "tp", None, None),
        ),
        check_vma=False,
    )
```

```python
import functools

import jax
import jax.numpy as jnp
from jax import lax
from jax.experimental import pallas as pl
from jax.experimental.pallas import tpu as pltpu
from jax.sharding import PartitionSpec as P

NEG = -1e30
TILE = 16
SPLIT = 64
CHUNKS = 8
AHEAD = 5
LATE = 5
VMEM_BYTES = 24 * 1024 * 1024


def row_of(block, at):
    rows = lax.broadcasted_iota(jnp.int32, block.shape, 0)
    return jnp.sum(jnp.where(rows == at, block, 0.0), axis=0, keepdims=True)


def row_at(block, position):
    base = pl.multiple_of(position // TILE * TILE, TILE)
    return row_of(block[pl.ds(base, TILE), :].astype(jnp.float32), position % TILE)


def put_row(block, row, position):
    base = pl.multiple_of(position // TILE * TILE, TILE)
    part = block[pl.ds(base, TILE), :]
    at = lax.broadcasted_iota(jnp.int32, part.shape, 0)
    mixed = jnp.where(at == position % TILE, row, part.astype(jnp.float32))
    block[pl.ds(base, TILE), :] = mixed.astype(jnp.bfloat16)


def put_last(block, row):
    end = block.shape[0]
    part = block[end - TILE : end, :]
    at = lax.broadcasted_iota(jnp.int32, part.shape, 0)
    mixed = jnp.where(at == TILE - 1, row, part.astype(jnp.float32))
    block[end - TILE : end, :] = mixed.astype(jnp.bfloat16)


def last_row(block):
    end = block.shape[0]
    return block[end - TILE : end, :].astype(jnp.float32)[TILE - 1 : TILE, :]


def invert(dest, source, n):
    def note(r, carry):
        source[dest[r]] = r
        return carry

    lax.fori_loop(0, n, note, 0)


def begin(pairs, sem):
    copies = [pltpu.make_async_copy(a, b, sem.at[i]) for i, (a, b) in enumerate(pairs)]
    for copy in copies:
        copy.start()
    return copies


def finish(copies):
    for copy in copies:
        copy.wait()


def parcels_of(refs, span):
    return [(ref.at[pl.ds(0, span)], ref.at[pl.ds(span, span)]) for ref in refs]


def sources(source, steps):
    me = lax.axis_index("inst")
    return [source[me ^ s] for s in steps]


def pack_kernel(n, steps, pages, *refs):
    count = len(steps)
    far, outs = refs[:8], refs[8 : 8 + count]
    table, lengths, dest, slot, key_one, value_one, key_pool, value_pool, source, sems = refs[8 + count :]
    copies = begin(list(zip(far, (table, lengths, dest, slot, key_one, value_one, key_pool, value_pool))), sems)
    size = key_pool.shape[1]
    parcels = parcels_of(outs, pages * size)
    finish(copies[:6])
    invert(dest, source, n)
    at = sources(source, steps)
    tokens = (key_one[...].astype(jnp.float32), value_one[...].astype(jnp.float32))
    lanes = lax.broadcasted_iota(jnp.int32, (1, key_one.shape[1]), 1)
    for which, pool in ((0, key_pool), (1, value_pool)):
        copies[6 + which].wait()
        for r, parcel in zip(at, parcels):
            for p in range(pages):
                parcel[which][p * size : (p + 1) * size, :] = pool[table[p, r]]
            put_row(parcel[which], row_of(tokens[which], r), lengths[r])
            if which == 0:
                put_row(parcel[0], last_row(parcel[0]), lengths[r] + 1)
                note = jnp.where(lanes < SPLIT, slot[r], lengths[r]).astype(jnp.float32)
                put_last(parcel[0], note)


def attend(queries, keys, values, counts):
    width = queries[0].shape[1]
    scores = []
    for q, k, count in zip(queries, keys, counts):
        s = lax.dot_general(q, k, (((1,), (1,)), ((), ())), preferred_element_type=jnp.float32)
        live = lax.broadcasted_iota(jnp.int32, s.shape, 1) < count
        scores.append(jnp.where(live, s * width ** (-0.5), NEG))
    group = scores[0].shape[0]
    score = jnp.concatenate(scores, axis=0)
    top = jnp.max(score, axis=-1, keepdims=True)
    expo = jnp.exp(score - top)
    weights = (expo / jnp.sum(expo, axis=-1, keepdims=True)).astype(jnp.bfloat16)
    return [
        jnp.dot(weights[i * group : (i + 1) * group], v, preferred_element_type=jnp.float32)
        for i, v in enumerate(values)
    ]


def project(mixed, weight, out):
    heads = mixed.shape[1]
    rows = jnp.concatenate([mixed[:, h, :] for h in range(heads)], axis=1).astype(jnp.bfloat16)
    width = weight.shape[1] // CHUNKS
    for c in range(CHUNKS):
        part = jnp.dot(
            rows, weight[:, c * width : (c + 1) * width], preferred_element_type=jnp.float32
        )
        out[:, c * width : (c + 1) * width] = part.astype(jnp.bfloat16)


def first_kernel(steps, span, *refs):
    n = len(steps)
    far, parcels, out, weight = refs[:4], refs[4 : 4 + n], refs[4 + n], refs[5 + n]
    lengths, dest, query, source, mixed, sems = refs[6 + n :]
    copies = begin(list(zip(far, (lengths, dest, query, weight))), sems)
    parcels = parcels_of(parcels, span)
    finish(copies[:3])
    invert(dest, source, n)
    at = sources(source, steps)
    results = attend(
        [query[r] for r in at],
        [parcel[0][...] for parcel in parcels],
        [parcel[1][...] for parcel in parcels],
        [lengths[r] + 1 for r in at],
    )
    for r, result in zip(at, results):
        mixed[r] = result
    copies[3].wait()
    project(mixed, weight, out)


def place(arrived, query, key_two, value_two, key_cache, value_cache, held, mixed, osems):
    count = len(arrived)
    slots = []
    lengths = []
    for parcel in arrived:
        note = last_row(parcel[0])
        lanes = lax.broadcasted_iota(jnp.int32, note.shape, 1)
        slots.append(jnp.max(jnp.where(lanes < SPLIT, note, 0.0)).astype(jnp.int32))
        lengths.append(jnp.max(jnp.where(lanes < SPLIT, 0.0, note)).astype(jnp.int32))
    for i, parcel in enumerate(arrived):
        held[0, i] = parcel[0][...]
        held[1, i] = parcel[1][...]
        put_last(held.at[0, i], row_at(parcel[0], lengths[i] + 1))
    outgoing = []
    for i in range(count):
        for which, (token, cache) in enumerate(((key_two, key_cache), (value_two, value_cache))):
            put_row(held.at[which, i], token[pl.ds(slots[i], 1), :], lengths[i] + 1)
            copy = pltpu.make_async_copy(held.at[which, i], cache.at[slots[i]], osems.at[which, i])
            copy.start()
            outgoing.append(copy)
    results = attend(
        [query[j] for j in slots],
        [held[0, i] for i in range(count)],
        [held[1, i] for i in range(count)],
        [length + 2 for length in lengths],
    )
    for j, result in zip(slots, results):
        mixed[j] = result
    return outgoing


def early_kernel(count, span, *refs):
    arrived, far = refs[:count], refs[count : count + 3]
    key_cache, value_cache, mixed, query, new_k, new_v = refs[count + 3 : count + 9]
    key_two, value_two, held, sems, osems = refs[-5:]
    copies = begin(list(zip(far, (query, key_two, value_two))), sems)
    finish(copies)
    new_k[...] = key_two[...].astype(jnp.float32)
    new_v[...] = value_two[...].astype(jnp.float32)
    parcels = parcels_of(arrived, span)
    finish(place(parcels, query, new_k, new_v, key_cache, value_cache, held, mixed, osems))


def late_kernel(count, span, *refs):
    arrived, (query, new_k, new_v, weight, before) = refs[:count], refs[count : count + 5]
    out, key_cache, value_cache, held, mixed, osems = refs[count + 7 :]
    mixed[...] = before[...]
    parcels = parcels_of(arrived, span)
    outgoing = place(parcels, query, new_k, new_v, key_cache, value_cache, held, mixed, osems)
    project(mixed, weight, out)
    finish(outgoing)


def total(partial, size):
    if size == 2:
        other = lax.ppermute(partial, "tp", [(0, 1), (1, 0)])
        return (partial.astype(jnp.float32) + other.astype(jnp.float32)).astype(jnp.bfloat16)
    return lax.psum(partial, "tp")


def near(x):
    return pltpu.with_memory_space_constraint(x, pltpu.VMEM)


def hbm(x):
    return pltpu.with_memory_space_constraint(x, pltpu.HBM)


def step_order(n):
    half = n // 2
    crossing = list(range(half, n))
    staying = list(range(1, half))
    for queue, at in ((crossing, half // 2), (staying, half // 4)):
        queue[at], queue[-1] = queue[-1], queue[at]
    for queue, at in ((crossing, half // 4), (staying, half // 4 - 1)):
        queue[at], queue[-2] = queue[-2], queue[at]
    crossing[1], crossing[-3] = crossing[-3], crossing[1]
    order = []
    for kind in "cncncncncncncnc":
        queue = crossing if kind == "c" else staying
        if queue:
            order.append(queue.pop(0))
    while crossing or staying:
        order += crossing[:1] + staying[:1]
        del crossing[:1], staying[:1]
    return order


def shards(
    n,
    tp,
    query_one,
    key_one,
    value_one,
    key_pages,
    value_pages,
    page_table,
    lengths,
    dest_instance,
    dest_slot,
    query_two,
    key_two,
    value_two,
    out_weight,
):
    slots, pages = page_table.shape
    pool, kv_heads, size, width = key_pages.shape
    heads = query_one.shape[1]
    depth, columns = out_weight.shape
    span = pages * size
    assert kv_heads == 1 and slots == n and n >= 16 and span <= 256
    key_pages = key_pages.reshape(pool, size, width)
    value_pages = value_pages.reshape(pool, size, width)
    key_one = key_one.reshape(slots, width)
    value_one = value_one.reshape(slots, width)
    key_two = key_two.reshape(slots, width)
    value_two = value_two.reshape(slots, width)

    vmem = pl.BlockSpec(memory_space=pltpu.VMEM)
    far = pl.BlockSpec(memory_space=pltpu.HBM)
    params = pltpu.CompilerParams(vmem_limit_bytes=VMEM_BYTES)
    bf16, f32, i32 = jnp.bfloat16, jnp.float32, jnp.int32
    rows = 2 * span
    order = step_order(n)
    steps = [0] + order

    def block(height):
        return jax.ShapeDtypeStruct((height, width), bf16)

    shapes = [block(rows)] * n

    def pack(chosen):
        return pl.pallas_call(
            functools.partial(pack_kernel, n, chosen, pages),
            out_shape=[jax.ShapeDtypeStruct((rows, width), bf16)] * len(chosen),
            in_specs=[far] * 8,
            out_specs=[vmem] * len(chosen),
            scratch_shapes=[
                pltpu.SMEM((pages, slots), i32),
                pltpu.SMEM((slots,), i32),
                pltpu.SMEM((slots,), i32),
                pltpu.SMEM((slots,), i32),
                pltpu.VMEM((slots, width), bf16),
                pltpu.VMEM((slots, width), bf16),
                pltpu.VMEM((pool, size, width), bf16),
                pltpu.VMEM((pool, size, width), bf16),
                pltpu.SMEM((n,), i32),
                pltpu.SemaphoreType.DMA((8,)),
            ],
            compiler_params=params,
            cost_estimate=pl.CostEstimate(
                flops=0, bytes_accessed=4 * len(chosen) * rows * width, transcendentals=0
            ),
            name="pack",
        )(
            hbm(page_table.T),
            hbm(lengths),
            hbm(dest_instance),
            hbm(dest_slot),
            hbm(key_one),
            hbm(value_one),
            hbm(key_pages),
            hbm(value_pages),
        )

    steps = step_order(n) + [0]
    packed = pack(steps[:AHEAD]) + pack(steps[AHEAD:])

    flops = 4 * slots * heads * span * width + 2 * slots * depth * columns
    moved = 2 * depth * columns + 4 * slots * span * width
    def send(i, *after):
        block = lax.optimization_barrier((packed[i], *after))[0] if after else packed[i]
        return lax.ppermute(block, "inst", [(d, d ^ steps[i]) for d in range(n)])

    arrived = [send(i) for i in range(AHEAD)]
    partial_one, weight = pl.pallas_call(
        functools.partial(first_kernel, steps, span),
        out_shape=[
            jax.ShapeDtypeStruct((slots, columns), bf16),
            jax.ShapeDtypeStruct((depth, columns), bf16),
        ],
        in_specs=[far] * 4 + [vmem] * len(shapes),
        out_specs=[vmem, vmem],
        scratch_shapes=[
            pltpu.SMEM((slots,), i32),
            pltpu.SMEM((slots,), i32),
            pltpu.VMEM((slots, heads, width), bf16),
            pltpu.SMEM((n,), i32),
            pltpu.VMEM((slots, heads, width), f32),
            pltpu.SemaphoreType.DMA((4,)),
        ],
        compiler_params=params,
        cost_estimate=pl.CostEstimate(flops=flops, bytes_accessed=moved, transcendentals=slots * heads * span),
        name="first",
    )(hbm(lengths), hbm(dest_instance), hbm(query_one), hbm(out_weight), *packed)

    arrived += [send(i, partial_one) for i in range(AHEAD, n - 1)]
    early, late = [packed[-1]] + arrived[:-LATE], arrived[-LATE:]
    cache = jax.ShapeDtypeStruct((slots, span, width), bf16)
    mixed = jax.ShapeDtypeStruct((slots, heads, width), f32)
    some = len(early)
    results = pl.pallas_call(
        functools.partial(early_kernel, some, span),
        out_shape=[cache, cache, mixed]
        + [jax.ShapeDtypeStruct((slots, heads, width), bf16)]
        + [jax.ShapeDtypeStruct((slots, width), f32)] * 2,
        in_specs=[vmem] * some + [far] * 3,
        out_specs=[far, far] + [vmem] * 4,
        scratch_shapes=[
            pltpu.VMEM((slots, width), bf16),
            pltpu.VMEM((slots, width), bf16),
            pltpu.VMEM((2, some, span, width), bf16),
            pltpu.SemaphoreType.DMA((3,)),
            pltpu.SemaphoreType.DMA((2, some)),
        ],
        compiler_params=params,
        cost_estimate=pl.CostEstimate(
            flops=4 * some * heads * span * width,
            bytes_accessed=8 * some * span * width,
            transcendentals=some * heads * span,
        ),
        name="early",
    )(*early, hbm(query_two), hbm(key_two), hbm(value_two))
    key_cache, value_cache, *carried = results
    partial_one = lax.optimization_barrier((partial_one, carried[0]))[0]
    out_one = total(partial_one, tp)

    partial_two, key_cache, value_cache = pl.pallas_call(
        functools.partial(late_kernel, LATE, span),
        out_shape=[jax.ShapeDtypeStruct((slots, columns), bf16), cache, cache],
        in_specs=[vmem] * (len(late) + 5) + [far] * 2,
        out_specs=[vmem, far, far],
        input_output_aliases={len(late) + 5: 1, len(late) + 6: 2},
        scratch_shapes=[
            pltpu.VMEM((2, LATE, span, width), bf16),
            pltpu.VMEM((slots, heads, width), f32),
            pltpu.SemaphoreType.DMA((2, LATE)),
        ],
        compiler_params=params,
        cost_estimate=pl.CostEstimate(flops=flops, bytes_accessed=moved, transcendentals=LATE * heads * span),
        name="late",
    )(
        *late,
        *[near(x) for x in carried[1:]],
        near(weight),
        near(carried[0]),
        hbm(key_cache),
        hbm(value_cache),
    )
    out_two = total(partial_two, tp)
    shape = (slots * pages, kv_heads, size, width)
    return (out_one, out_two, key_cache.reshape(shape), value_cache.reshape(shape))


def solution(mesh):
    sizes = dict(mesh.shape)
    return jax.shard_map(
        functools.partial(shards, sizes["inst"], sizes["tp"]),
        mesh=mesh,
        in_specs=(
            P("inst", "tp", None),
            P("inst", "tp", None),
            P("inst", "tp", None),
            P("inst", "tp", None, None),
            P("inst", "tp", None, None),
            P("inst", None),
            P("inst"),
            P("inst"),
            P("inst"),
            P("inst", "tp", None),
            P("inst", "tp", None),
            P("inst", "tp", None),
            P("tp", None),
        ),
        out_specs=(
            P("inst", None),
            P("inst", None),
            P("inst", "tp", None, None),
            P("inst", "tp", None, None),
        ),
        check_vma=False,
    )
```
